32 devices in a mesh: ex: 4 (over y, x), ey: 2 (over core), lb: 4 (over z).
Axes of the slice: x: 2, y: 2, z: 4, core: 2. Of those that a mesh axis runs over, the one named last changes fastest.
Arguments:
- atmosphere_state: float32 [15, 128, 32, 256], P(None, 'lb', 'ex', 'ey'), may hold values from -6 to 6
- diffusivity: float32 [15], replicated, may hold values from 0.004 to 0.012
- mixing: float32 [127], replicated, may hold values from 0.5 to 50
- relaxation: float32 [128], replicated, may hold values from 0.05 to 0.5
- forcing: float32 [15, 128], replicated, may hold values from -3 to 3
- span_map: int32 [4, 2, 1024], P('ex', 'ey'), may hold values from 0 to 1023, each once within a row
- cost_class: int32 [32, 256], P('ex', 'ey'), may hold values from 0 to 3, as said below
Outputs:
- new_state: float32 [15, 128, 32, 256], P(None, 'lb', 'ex', 'ey')
The draws below stay inside these ranges and needn't reach their ends.
Inputs may be any that keep to these rules, and one draw needn't show every extreme that they name: `span_map`: each tile's row lists every one of its 1024 columns exactly once. `cost_class`: sunlit columns, a periodic band of 128 consecutive indices along the second direction, the same for every index along the first, have classes 2 or more; all other columns have classes below 2.
All inputs are finite; a program needn't handle non-finite values.
Results may differ from the reference program's by a relative error of at most 0.00011.
Values sent between devices are 32-bit elements; how exact they have to be, the bound alone decides.
A program may use at most 128 MiB of HBM per device.

```python
import math
import jax
import jax.numpy as jnp
import numpy as np
from jax import lax

F = 15
L = 128
STEPS = 2
SUBSTEPS = 4
CX = 8
CY = 128
TILES = 8
NX = 32
NY = 256
N_EX = 4
N_EY = 2


def draw_cost_class(key, part):
    key_shift = jax.random.fold_in(key, 11)
    key_noise = jax.random.fold_in(key, 23)
    shift = jax.random.randint(key_shift, (), 0, NY).astype(jnp.int32)
    column = jnp.arange(NY).astype(jnp.int32)
    sunlit = (column - shift) % NY < NY // 2
    half = SUBSTEPS // 2
    noise = jax.random.randint(key_noise, (NX, NY), 0, half).astype(jnp.int32)
    classes = jnp.where(sunlit[None, :], half + noise, noise)
    classes = classes.at[0, shift].set(SUBSTEPS - 1)
    classes = classes.at[0, (shift + NY // 2) % NY].set(0)
    return classes.astype(jnp.int32)


def block_scale(stream_key, extent, split, smallest, top_value):
    def one(dim, blocks):
        steps = jax.random.uniform(jax.random.fold_in(jax.random.fold_in(stream_key, 6), dim), (blocks,), jnp.float32, smallest / len(split), top_value / len(split))
        return jnp.repeat(jnp.exp(steps), extent[dim] // blocks).reshape((-1,) + (1,) * (len(extent) - dim - 1))

    factor_of = one(*split[0])
    for cut in split[1:]:
        factor_of = factor_of * one(*cut)
    return factor_of


def bell_draw(own_key, dims, width, reach, pieces=(), kind=jnp.bfloat16):
    gain = block_scale(own_key, dims, pieces, -0.22, 0.18) if pieces else 1.0
    values = jax.random.normal(own_key, dims, jnp.float32) * width * gain
    return jnp.minimum(jnp.maximum(values, -reach), reach).astype(kind)


def setup_inputs(seed: int = 0) -> dict:
    key_list = jax.random.split(jax.random.key(seed), 8)
    return {
        "atmosphere_state": bell_draw(key_list[0], (F, L, NX, NY), 1.0, 6.0, ((1, 4), (2, 4), (3, 2)), jnp.float32),
        "diffusivity": jnp.clip(jnp.exp(jax.random.uniform(key_list[1], (F,), jnp.float32, math.log(0.004), math.log(0.012))), 0.004, 0.012),
        "mixing": jnp.clip(jnp.exp(jax.random.uniform(key_list[2], (L - 1,), jnp.float32, math.log(0.5), math.log(50.0))), 0.5, 50.0),
        "relaxation": jnp.clip(jnp.exp(jax.random.uniform(key_list[3], (L,), jnp.float32, math.log(0.05), math.log(0.5))), 0.05, 0.5),
        "forcing": bell_draw(key_list[4], (F, L), 0.5, 3.0, (), jnp.float32),
        "span_map": jax.vmap(lambda own: jax.random.permutation(own, CX * CY))(jax.random.split(key_list[5], N_EX * N_EY)).reshape((N_EX, N_EY, CX * CY)).astype(jnp.int32),
        "cost_class": draw_cost_class(jax.random.fold_in(key_list[7], 71), 0),
    }


def second_table():
    inner_root = 1.0 / math.sqrt(5.0)
    gll_nodes = np.array([-1.0, -inner_root, inner_root, 1.0])
    weights = np.array([np.prod([gll_nodes[target] - gll_nodes[source] for source in range(4) if source != target]) for target in range(4)])
    first_table = np.zeros((4, 4))
    for target in range(4):
        for source in range(4):
            if source != target:
                first_table[target, source] = weights[target] / (weights[source] * (gll_nodes[target] - gll_nodes[source]))
    for target in range(4):
        first_table[target, target] = -first_table[target].sum()
    return (first_table @ first_table).astype(np.float32)

def derive(field, second):
    levels, width_x, width_y = field.shape
    along_x = jnp.einsum('ij,lejy->leiy', second, field.reshape(levels, width_x // 4, 4, width_y), precision=lax.Precision.HIGHEST)
    along_y = jnp.einsum('ij,lxej->lxei', second, field.reshape(levels, width_x, width_y // 4, 4), precision=lax.Precision.HIGHEST)
    return along_x.reshape(field.shape) + along_y.reshape(field.shape)

def join_edges(values):
    place_x = (jnp.arange(values.shape[1]) % 4)[:, None]
    after = jnp.roll(values, -1, axis=1)
    before = jnp.roll(values, 1, axis=1)
    values = jnp.where(place_x == 3, 0.5 * (values + after), jnp.where(place_x == 0, 0.5 * (values + before), values))
    place_y = jnp.arange(values.shape[2]) % 4
    after = jnp.roll(values, -1, axis=2)
    before = jnp.roll(values, 1, axis=2)
    return jnp.where(place_y == 3, 0.5 * (values + after), jnp.where(place_y == 0, 0.5 * (values + before), values))

def build_matrix(mixing, relaxation):
    zero = jnp.zeros((1,), jnp.float32)
    diagonal = 1.0 + relaxation + jnp.concatenate([zero, mixing]) + jnp.concatenate([mixing, zero])
    return jnp.diag(diagonal) - jnp.diag(mixing, 1) - jnp.diag(mixing, -1)

def reference(atmosphere_state, diffusivity, mixing, relaxation, forcing, span_map, cost_class):
    second = jnp.asarray(second_table())

    def dynamics(item):
        field, rate = item
        for repeat in range(STEPS):
            field = field + rate * join_edges(derive(field, second))
        return field
    moved = lax.map(dynamics, (atmosphere_state, diffusivity))
    tiled = moved.reshape(F, L, N_EX, CX, N_EY, CY).transpose(0, 1, 2, 4, 3, 5).reshape(F, L, TILES, CX * CY)
    order = span_map.reshape(TILES, CX * CY)
    ordered = jnp.take_along_axis(tiled, order[None, None], axis=3)
    classes = cost_class.reshape(N_EX, CX, N_EY, CY).transpose(0, 2, 1, 3).reshape(TILES, CX * CY)
    classes = jnp.take_along_axis(classes, order, axis=1).reshape(-1)
    factor = jnp.linalg.cholesky(build_matrix(mixing, relaxation))

    def physics(item):
        column_set, push = item
        start = column_set.reshape(L, TILES * CX * CY)
        current = start
        for substep in range(SUBSTEPS):
            solved = jax.scipy.linalg.cho_solve((factor, True), current) + push[:, None]
            current = jnp.where(substep <= classes, solved, current)
        change = lax.optimization_barrier(jnp.mean(current - start, axis=0)).reshape(TILES, CX * CY)
        shared = lax.optimization_barrier(jnp.mean(change, axis=0))
        return current.reshape(L, TILES, CX * CY) - shared[None, None, :]
    fixed = lax.map(physics, (ordered, forcing))
    inverse = jnp.argsort(order, axis=1).astype(jnp.int32)
    restored = jnp.take_along_axis(fixed, inverse[None, None], axis=3)
    return restored.reshape(F, L, N_EX, N_EY, CX, CY).transpose(0, 1, 2, 4, 3, 5).reshape(F, L, NX, NY)
```

```python
import functools
import math

import jax
import jax.numpy as jnp
import numpy as np
from jax import lax
from jax.experimental import pallas as pl
from jax.experimental.pallas import tpu as pltpu
from jax.sharding import PartitionSpec as P

STEPS = 2
SUBSTEPS = 4
MESH = pl.DeviceIdType.MESH
SKEW = 4


def second_table():
    inner_root = 1.0 / math.sqrt(5.0)
    gll_nodes = np.array([-1.0, -inner_root, inner_root, 1.0])
    weights = np.array(
        [
            np.prod(
                [gll_nodes[target] - gll_nodes[source] for source in range(4) if source != target]
            )
            for target in range(4)
        ]
    )
    first_table = np.zeros((4, 4))
    for target in range(4):
        for source in range(4):
            if source != target:
                first_table[target, source] = weights[target] / (
                    weights[source] * (gll_nodes[target] - gll_nodes[source])
                )
    for target in range(4):
        first_table[target, target] = -first_table[target].sum()
    return (first_table @ first_table).astype(np.float32)


def operator_tables(width_x, width_y):
    second = second_table()
    along = np.kron(np.eye(width_y // 4), second.T).astype(np.float64)
    edge = np.zeros((width_y, width_y))
    for y in range(width_y):
        if y % 4 == 3:
            edge[y, y] = 0.5
            if y + 1 < width_y:
                edge[y + 1, y] = 0.5
        elif y % 4 == 0:
            edge[y, y] = 0.5
            if y > 0:
                edge[y - 1, y] = 0.5
        else:
            edge[y, y] = 1.0
    rim = np.zeros((width_y, width_y))
    rim[0, width_y - 1] = 0.5
    rim[width_y - 1, 0] = 0.5
    both = np.concatenate([edge, rim], axis=1)
    weight = np.concatenate([along @ both, both], axis=0).astype(np.float32)
    high = weight.astype(jnp.bfloat16)
    low = (weight - high.astype(np.float32)).astype(jnp.bfloat16)
    shifts = np.zeros((7, width_x, width_y), np.float32)
    for x in range(width_x):
        for d in range(-3, 4):
            if 0 <= x % 4 + d < 4:
                shifts[d + 3, x, :] = second[x % 4, x % 4 + d]
    return high, low, shifts


def series_mul(u, v):
    return [sum(u[i] * v[k - i] for i in range(k + 1)) for k in range(len(u))]


def series_inverse(u):
    first = 1.0 / u[0]
    out = [first]
    for k in range(1, len(u)):
        out.append(-first * sum(u[i] * out[k - i] for i in range(1, k + 1)))
    return out


def prep_kernel(slab, count, params, u_out, sum_out, v_out, coef_out):
    levels = params.shape[1]
    shape = (8, levels)
    lo = jnp.broadcast_to(params[0:1, :], shape)
    hi = jnp.broadcast_to(params[1:2, :], shape)
    rel = jnp.broadcast_to(params[2:3, :], shape)
    lane = lax.broadcasted_iota(jnp.int32, shape, 1)
    row = lax.broadcasted_iota(jnp.int32, shape, 0)
    diag = 1.0 + rel + lo + hi

    def back(x, s):
        return pltpu.roll(x, s, 1)

    def ahead(x, s):
        return pltpu.roll(x, levels - s, 1)

    def reduce_system(a, b, c, extent):
        stages = []
        s = 1
        while s < extent:
            alpha = -a / back(b, s)
            gamma = -c / ahead(b, s)
            b = b + alpha * back(c, s) + gamma * ahead(a, s)
            a = alpha * back(a, s)
            c = gamma * ahead(c, s)
            stages.append((s, alpha, gamma))
            s *= 2
        return stages, 1.0 / b

    def solve(system, d):
        stages, inverse = system
        for s, alpha, gamma in stages:
            d = d + alpha * back(d, s) + gamma * ahead(d, s)
        return d * inverse

    whole = reduce_system(-lo, diag, -hi, levels)
    cut = reduce_system(
        jnp.where(lane % slab == 0, 0.0, -lo),
        diag,
        jnp.where(lane % slab == slab - 1, 0.0, -hi),
        slab,
    )
    push = [params[8:16, :], jnp.where(row == 7, 0.0, params[16:24, :])]
    held = [params[8:16, :], params[16:24, :]]
    for k in range(SUBSTEPS + 1):
        for h in range(2):
            u_out[k * 16 + h * 8 : k * 16 + h * 8 + 8, :] = held[h]
            sum_out[k * 16 + h * 8 : k * 16 + h * 8 + 8, :] = jnp.broadcast_to(
                jnp.sum(held[h], axis=1, keepdims=True), shape
            )
        if k < SUBSTEPS:
            held = [solve(whole, held[h]) + push[h] for h in range(2)]

    spot = jnp.where(row < 4, row * slab + slab - 1, (row - 4) * slab)
    tips = jnp.where((lane == spot) & (row % 4 < count), 1.0, 0.0)
    other = pltpu.roll(tips, 4, 0)

    def total(x):
        return jnp.broadcast_to(jnp.sum(x, axis=1, keepdims=True), shape)

    mix = total(jnp.where(row < 4, lo, hi) * other)
    near, far = [], []
    v = tips
    for k in range(SUBSTEPS):
        v = solve(cut, v)
        v_out[k * 8 : k * 8 + 8, :] = v
        near.append(total(v * tips))
        far.append(total(v * other))
    facing = [pltpu.roll(x, 4, 0) for x in near]
    square = mix * mix
    far_far = series_mul(far, far)

    def beside(z):
        return [jnp.where(row < 4, pltpu.roll(x, 1, 0), pltpu.roll(x, 7, 0)) for x in z]

    def gain(u, v):
        product = series_mul(u, v)
        return series_inverse(
            [(1.0 if k == 0 else 0.0) - square * x for k, x in enumerate(product)]
        )

    z = near
    for _ in range(count - 1):
        zn = beside(z)
        change = series_mul(series_mul(far_far, zn), gain(zn, facing))
        z = [x + square * y for x, y in zip(near, change)]
    zn = beside(z)
    first = [mix * x for x in series_mul(far, gain(zn, facing))]
    next_ = [mix * x for x in series_mul(first, zn)]
    edge = gain(zn, [pltpu.roll(x, 4, 0) for x in z])
    edge_one = [mix * x for x in edge]
    edge_two = [mix * x for x in series_mul(edge_one, zn)]
    for g, part in enumerate((first, next_, edge_one, edge_two)):
        for k in range(SUBSTEPS):
            at = (g * SUBSTEPS + k) * 8
            coef_out[at : at + 8, :] = part[k]


def prep(params, slab, count):
    levels = params.shape[1]
    shapes = [(5 * 16, levels), (5 * 16, levels), (SUBSTEPS * 8, levels), (16 * 8, levels)]
    return pl.pallas_call(
        functools.partial(prep_kernel, slab, count),
        out_shape=[jax.ShapeDtypeStruct(s, jnp.float32) for s in shapes],
        in_specs=[pl.BlockSpec(memory_space=pltpu.VMEM)],
        out_specs=[pl.BlockSpec(memory_space=pltpu.VMEM)] * 4,
    )(params)


def main_kernel(
    dims,
    state, classes, span, w_high, w_low, shifts, rate, u_s, sum_s, v_s, coef_s,
    moved, ends, share,
    lap, hy_out, hy_in, x_out, x_in, weights, p_loc, q_loc, p_out, p_in, q_out, q_in,
    tend, hot, slots, got_one, part, got_two, full,
    ys, yr, xs, xr, ps, pr, qs, qr, os, o_r, ts, t_r, fs, f_r,
):
    n_ex, n_ey, n_lb, fields, slab = dims
    rows = slab * 8
    tiles = n_ex * n_ey
    ex, ey, lb = lax.axis_index("ex"), lax.axis_index("ey"), lax.axis_index("lb")
    tile = ex * n_ey + ey
    sides = 1 if n_ey == 2 else 2

    def tile_peer(o):
        t = lax.rem(tile + o, tiles)
        return (t // n_ey, lax.rem(t, n_ey), lb)

    def slab_peer(o):
        return (ex, ey, lax.rem(lb + o, n_lb))

    barrier = pltpu.get_barrier_semaphore()

    def greet_tiles(o, c):
        pl.semaphore_signal(barrier, inc=1, device_id=tile_peer(o), device_id_type=MESH)
        return c

    def greet_slabs(o, c):
        pl.semaphore_signal(barrier, inc=1, device_id=slab_peer(o), device_id_type=MESH)
        return c

    lax.fori_loop(1, tiles, greet_tiles, 0)
    lax.fori_loop(1, n_lb, greet_slabs, 0)

    row_x = lax.broadcasted_iota(jnp.int32, (8, 128), 0)
    lane = lax.broadcasted_iota(jnp.int32, (8, 128), 1)
    cls = classes[...]

    def derive(f, source, step):
        s = source[f]
        along = shifts[3][None] * s
        for d in (-3, -2, -1, 1, 2, 3):
            along = along + shifts[d + 3][None] * pltpu.roll(s, (8 - d) % 8, 1)
        both = jnp.concatenate([s.reshape(rows, 128), along.reshape(rows, 128)], axis=1)
        high = both.astype(jnp.bfloat16)
        low = (both - high.astype(jnp.float32)).astype(jnp.bfloat16)
        result = (
            jnp.dot(high, w_high[...], preferred_element_type=jnp.float32)
            + jnp.dot(low, w_high[...], preferred_element_type=jnp.float32)
            + jnp.dot(high, w_low[...], preferred_element_type=jnp.float32)
        )
        lap[f] = result[:, :128]
        hy_out[step, f] = result[:, 128:]

    def y_copy(step, f, side):
        peer = lax.rem(ey + (1 if side == 0 else n_ey - 1), n_ey)
        return pltpu.make_async_remote_copy(
            src_ref=hy_out.at[step, f],
            dst_ref=hy_in.at[step, side, f],
            send_sem=ys.at[step, side, f],
            recv_sem=yr.at[step, side, f],
            device_id=(ex, peer, lb),
            device_id_type=MESH,
        )

    def x_copy(step, f, side):
        peer = lax.rem(ex + (1 if side == 0 else n_ex - 1), n_ex)
        return pltpu.make_async_remote_copy(
            src_ref=x_out.at[step, side, f],
            dst_ref=x_in.at[step, side, f],
            send_sem=xs.at[step, side, f],
            recv_sem=xr.at[step, side, f],
            device_id=(peer, ey, lb),
            device_id_type=MESH,
        )

    def start_y(f, step):
        for side in range(sides):
            y_copy(step, f, side).start()

    def spread(step):
        def body(f, c):
            for side in range(sides):
                y_copy(step, f, side).wait_recv()
            value = lap[f].reshape(slab, 8, 128)
            if sides == 1:
                value = value + hy_in[step, 0, f].reshape(slab, 8, 128)
            else:
                value = value + jnp.where(
                    lane == 0, hy_in[step, 0, f].reshape(slab, 8, 128), 0.0
                )
                value = value + jnp.where(
                    lane == 127, hy_in[step, 1, f].reshape(slab, 8, 128), 0.0
                )
            lap[f] = value.reshape(rows, 128)
            x_out[step, 0, f] = lap[f, pl.ds(7, slab, stride=8), :]
            x_out[step, 1, f] = lap[f, pl.ds(0, slab, stride=8), :]
            x_copy(step, f, 0).start()
            x_copy(step, f, 1).start()
            return c

        lax.fori_loop(0, fields, body, 0)

    def advance(f, source, step):
        x_copy(step, f, 0).wait_recv()
        x_copy(step, f, 1).wait_recv()
        value = lap[f].reshape(slab, 8, 128)
        before = pltpu.roll(value, 1, 1)
        after = pltpu.roll(value, 7, 1)
        first = jnp.broadcast_to(x_in[step, 0, f][:, None, :], (slab, 8, 128))
        last = jnp.broadcast_to(x_in[step, 1, f][:, None, :], (slab, 8, 128))
        partner = jnp.where(
            row_x == 0,
            first,
            jnp.where(row_x == 7, last, jnp.where(row_x == 3, after, before)),
        )
        joins = (row_x == 0) | (row_x == 3) | (row_x == 4) | (row_x == 7)
        edged = jnp.where(joins, 0.5 * (value + partner), value)
        moved[f] = source[f] + rate[f] * edged

    derive(0, state, 0)
    pl.semaphore_wait(barrier, tiles - 1 + n_lb - 1)
    start_y(0, 0)

    def open_rest(f, c):
        derive(f, state, 0)
        start_y(f, 0)
        return c

    lax.fori_loop(1, fields, open_rest, 0)
    spread(0)

    def set_weight(l, c):
        at = lb * slab + l
        w = [u_s[k * 16 + 15, at] - 1.0 for k in range(1, 5)]
        weights[l] = jnp.where(
            cls == 0, w[0], jnp.where(cls == 1, w[1], jnp.where(cls == 2, w[2], w[3]))
        )
        return c

    lax.fori_loop(0, slab, set_weight, 0)
    for x in range(8):
        mine = lax.broadcasted_iota(jnp.int32, (128, 1024), 0) + x * 128
        hot[x * 128 : (x + 1) * 128, :] = (
            (mine == span[...]).astype(jnp.float32).astype(jnp.bfloat16)
        )

    def middle(f, c):
        advance(f, state, 0)
        derive(f, moved, 1)
        start_y(f, 1)
        return c

    lax.fori_loop(0, fields, middle, 0)
    spread(1)

    def pick(group, k, base):
        return coef_s[(group * SUBSTEPS + k) * 8 + base + lb, 0]

    def convolve(group, base, k, value):
        out = pick(group, 0, base) * value[k]
        for i in range(1, k + 1):
            out = out + pick(group, i, base) * value[k - i]
        return out

    def scan_copy(f, down):
        if down:
            return pltpu.make_async_remote_copy(
                src_ref=p_out.at[f], dst_ref=p_in.at[f],
                send_sem=ps.at[f], recv_sem=pr.at[f],
                device_id=(ex, ey, lax.rem(lb + 1, n_lb)), device_id_type=MESH,
            )
        return pltpu.make_async_remote_copy(
            src_ref=q_out.at[f], dst_ref=q_in.at[f],
            send_sem=qs.at[f], recv_sem=qr.at[f],
            device_id=(ex, ey, lax.rem(lb + n_lb - 1, n_lb)), device_id_type=MESH,
        )

    def scan_step(f, down):
        arrives = lb > 0 if down else lb < n_lb - 1
        leaves = lb < n_lb - 1 if down else lb > 0
        inward, outward = (p_in, p_out) if down else (q_in, q_out)
        same, opposite = (p_loc, q_loc) if down else (q_loc, p_loc)
        base = 0 if down else 4

        @pl.when((f >= 0) & (f < fields))
        def _():
            @pl.when(arrives)
            def _():
                scan_copy(f, down).wait_recv()
                own = [same[f, k] for k in range(SUBSTEPS)]
                facing = [opposite[f, k] for k in range(SUBSTEPS)]
                coming = [inward[f, k] for k in range(SUBSTEPS)]
                for k in range(SUBSTEPS):
                    outward[f, k] = (
                        own[k] + convolve(0, base, k, coming) + convolve(1, base, k, facing)
                    )

            @pl.when(jnp.logical_not(arrives))
            def _():
                for k in range(SUBSTEPS):
                    outward[f, k] = same[f, k]

            @pl.when(leaves)
            def _():
                scan_copy(f, down).start()

    def scan_steps(i):
        scan_step(i - lb * SKEW, True)
        scan_step(i - (n_lb - 1 - lb) * SKEW, False)

    def summarise(f):
        zero = jnp.zeros((8, 128), jnp.float32)

        def level(l, c):
            x = moved[f, l]
            at = lb * slab + l
            out = [c[k] + v_s[k * 8 + lb, at] * x for k in range(4)]
            out += [c[4 + k] + v_s[k * 8 + 4 + lb, at] * x for k in range(4)]
            out.append(c[8] + weights[l] * x)
            return tuple(out)

        sums = lax.fori_loop(0, slab, level, (zero,) * 9, unroll=8)
        for k in range(SUBSTEPS):
            p_loc[f, k] = sums[k]
            q_loc[f, k] = sums[4 + k]
        h = [sum_s[k * 16 + f, 0] * (1.0 / n_lb) for k in range(4)]
        extra = jnp.where(
            cls == 0, h[0], jnp.where(cls == 1, h[1], jnp.where(cls == 2, h[2], h[3]))
        )
        tend[pl.ds(pl.multiple_of(f * 8, 8), 8), :] = sums[8] + extra

    tend[fields * 8 : 128, :] = jnp.zeros((128 - fields * 8, 128), jnp.float32)

    def closing(i, c):
        advance(i, moved, 1)
        summarise(i)
        scan_steps(i)
        return c

    lax.fori_loop(0, fields, closing, 0)

    def three(value):
        a = value.astype(jnp.bfloat16)
        rest = value - a.astype(jnp.float32)
        b = rest.astype(jnp.bfloat16)
        return a, b, (rest - b.astype(jnp.float32)).astype(jnp.bfloat16)

    span_slots = 1024 // n_lb
    gathered = jnp.zeros((16, 1024), jnp.float32)
    for x in range(8):
        for piece in three(tend[pl.ds(x, 16, stride=8), :]):
            gathered = gathered + jnp.dot(
                piece, hot[x * 128 : (x + 1) * 128, :], preferred_element_type=jnp.float32
            )
    for g in range(n_lb):
        slots[g] = gathered[:, g * span_slots : (g + 1) * span_slots]

    def one_copy(o):
        return pltpu.make_async_remote_copy(
            src_ref=slots.at[lax.rem(lb + o, n_lb)], dst_ref=got_one.at[o - 1],
            send_sem=os.at[o - 1], recv_sem=o_r.at[o - 1],
            device_id=slab_peer(o), device_id_type=MESH,
        )

    def two_copy(o):
        return pltpu.make_async_remote_copy(
            src_ref=part, dst_ref=got_two.at[o - 1],
            send_sem=ts.at[o - 1], recv_sem=t_r.at[o - 1],
            device_id=tile_peer(o), device_id_type=MESH,
        )

    def three_copy(o):
        return pltpu.make_async_remote_copy(
            src_ref=full.at[lb], dst_ref=full.at[lb],
            send_sem=fs.at[o - 1], recv_sem=f_r.at[o - 1],
            device_id=slab_peer(o), device_id_type=MESH,
        )

    def three_arrival(o):
        other = lax.rem(lb + n_lb - o, n_lb)
        return pltpu.make_async_remote_copy(
            src_ref=full.at[other], dst_ref=full.at[other],
            send_sem=fs.at[o - 1], recv_sem=f_r.at[o - 1],
            device_id=slab_peer(o), device_id_type=MESH,
        )

    for o in range(1, n_lb):
        one_copy(o).start()

    tail = (n_lb - 1) * SKEW
    half = fields + tail // 2

    def trailing(i, c):
        scan_steps(i)
        return c

    lax.fori_loop(fields, half, trailing, 0)
    total = slots[lb]
    for o in range(1, n_lb):
        one_copy(o).wait_recv()
        total = total + got_one[o - 1]
    part[...] = total

    def start_two(o, c):
        two_copy(o).start()
        return c

    lax.fori_loop(1, tiles, start_two, 0)
    lax.fori_loop(half, fields + tail, trailing, 0)

    def add_two(o, c):
        two_copy(o).wait_recv()
        return c + got_two[o - 1]

    total = lax.fori_loop(1, tiles, add_two, part[...])
    full[lb] = total * (1.0 / (tiles * slab * n_lb))
    for o in range(1, n_lb):
        three_copy(o).start()

    @pl.when(lb == 0)
    def _():
        p_in[...] = jnp.zeros_like(p_in)

    @pl.when(lb == n_lb - 1)
    def _():
        q_in[...] = jnp.zeros_like(q_in)

    def finish(f, c):
        above = [p_in[f, k] for k in range(SUBSTEPS)]
        below = [q_in[f, k] for k in range(SUBSTEPS)]
        own_p = [p_out[f, k] for k in range(SUBSTEPS)]
        own_q = [q_out[f, k] for k in range(SUBSTEPS)]
        for k in range(SUBSTEPS):
            ends[f, k] = convolve(2, 0, k, above) + convolve(3, 0, k, own_q)
            ends[f, SUBSTEPS + k] = convolve(2, 4, k, below) + convolve(3, 4, k, own_p)
        return c

    lax.fori_loop(0, fields, finish, 0)
    for o in range(1, n_lb):
        three_arrival(o).wait_recv()
    for x in range(8):
        value = jnp.zeros((16, 128), jnp.float32)
        for g in range(n_lb):
            pick_hot = hot[x * 128 : (x + 1) * 128, g * span_slots : (g + 1) * span_slots]
            for piece in three(full[g]):
                value = value + lax.dot_general(
                    piece, pick_hot, (((1,), (1,)), ((), ())),
                    preferred_element_type=jnp.float32,
                )
        share[pl.ds(x, 16, stride=8), :] = value

    def drain(f, c):
        for step in range(STEPS):
            for side in range(sides):
                y_copy(step, f, side).wait_send()
            for side in range(2):
                x_copy(step, f, side).wait_send()

        @pl.when(lb < n_lb - 1)
        def _():
            scan_copy(f, True).wait_send()

        @pl.when(lb > 0)
        def _():
            scan_copy(f, False).wait_send()

        return c

    lax.fori_loop(0, fields, drain, 0)
    for o in range(1, n_lb):
        one_copy(o).wait_send()
        three_copy(o).wait_send()

    def drain_two(o, c):
        two_copy(o).wait_send()
        return c

    lax.fori_loop(1, tiles, drain_two, 0)


def dynamics(dims, state, classes, span, rate, u_t, sum_t, v_t, coef_t):
    n_ex, n_ey, n_lb, fields, slab = dims
    rows = slab * 8
    tiles = n_ex * n_ey
    sides = 1 if n_ey == 2 else 2
    high, low, shifts = operator_tables(8, 128)
    vmem = pl.BlockSpec(memory_space=pltpu.VMEM)
    smem = pl.BlockSpec(memory_space=pltpu.SMEM)
    f32 = jnp.float32
    dma = pltpu.SemaphoreType.DMA
    wide = 1024 // n_lb
    return pl.pallas_call(
        functools.partial(main_kernel, dims),
        out_shape=[
            jax.ShapeDtypeStruct((fields, slab, 8, 128), f32),
            jax.ShapeDtypeStruct((fields, 2 * SUBSTEPS, 8, 128), f32),
            jax.ShapeDtypeStruct((128, 128), f32),
        ],
        in_specs=[vmem] * 6 + [smem] * 5,
        out_specs=[vmem] * 3,
        scratch_shapes=[
            pltpu.VMEM((fields, rows, 128), f32),
            pltpu.VMEM((STEPS, fields, rows, 128), f32),
            pltpu.VMEM((STEPS, sides, fields, rows, 128), f32),
            pltpu.VMEM((STEPS, 2, fields, slab, 128), f32),
            pltpu.VMEM((STEPS, 2, fields, slab, 128), f32),
            pltpu.VMEM((slab, 8, 128), f32),
        ]
        + [pltpu.VMEM((fields, SUBSTEPS, 8, 128), f32)] * 6
        + [
            pltpu.VMEM((128, 128), f32),
            pltpu.VMEM((1024, 1024), jnp.bfloat16),
            pltpu.VMEM((n_lb, 16, wide), f32),
            pltpu.VMEM((n_lb - 1, 16, wide), f32),
            pltpu.VMEM((16, wide), f32),
            pltpu.VMEM((tiles - 1, 16, wide), f32),
            pltpu.VMEM((n_lb, 16, wide), f32),
            dma((STEPS, sides, fields)),
            dma((STEPS, sides, fields)),
            dma((STEPS, 2, fields)),
            dma((STEPS, 2, fields)),
            dma((fields,)),
            dma((fields,)),
            dma((fields,)),
            dma((fields,)),
            dma((n_lb - 1,)),
            dma((n_lb - 1,)),
            dma((tiles - 1,)),
            dma((tiles - 1,)),
            dma((n_lb - 1,)),
            dma((n_lb - 1,)),
        ],
        compiler_params=pltpu.CompilerParams(
            collective_id=0, has_side_effects=True, vmem_limit_bytes=48 * 1024 * 1024
        ),
    )(
        state, classes, span, jnp.asarray(high), jnp.asarray(low), jnp.asarray(shifts),
        rate, u_t, sum_t, v_t, coef_t,
    )


def finish_kernel(
    n_lb, moved, ends, share, classes, params, u_s, out, current, swept, carry, scale, link
):
    group, slab = moved.shape[0], moved.shape[1]
    lb = lax.axis_index("lb")
    step = pl.program_id(0)

    @pl.when(step == 0)
    def _():
        def factor(l, previous):
            at = lb * slab + l
            low = jnp.where(l == 0, 0.0, params[0, at])
            high = jnp.where(l == slab - 1, 0.0, params[1, at])
            ratio = low * previous
            diag = 1.0 + params[2, at] + params[0, at] + params[1, at]
            inverse = 1.0 / (diag - low * ratio)
            carry[l] = ratio
            scale[l] = inverse
            link[l] = high * inverse
            return inverse

        lax.fori_loop(0, slab, factor, jnp.zeros((8, 128), jnp.float32))

    cls = classes[...]
    for k in range(SUBSTEPS):
        source = moved if k == 0 else current

        def down(l, z, source=source):
            z = source[:, l] + carry[l][None] * z
            swept[:, l] = z
            return z

        z = source[:, 0] + ends[:, k]
        swept[:, 0] = z
        z = lax.fori_loop(1, slab, down, z, unroll=4)
        y = (z + ends[:, SUBSTEPS + k]) * scale[slab - 1][None]
        active = cls >= k
        current[:, slab - 1] = jnp.where(active, y, source[:, slab - 1])

        def up(i, y, source=source, active=active):
            l = slab - 1 - i
            y = swept[:, l] * scale[l][None] + link[l][None] * y
            current[:, l] = jnp.where(active, y, source[:, l])
            return y

        lax.fori_loop(1, slab, up, y, unroll=4)

    def close(l, c):
        at = lb * slab + l
        for f in range(group):
            h = [u_s[k * 16 + step * group + f, at] for k in range(4)]
            push = jnp.where(
                cls == 0, h[0], jnp.where(cls == 1, h[1], jnp.where(cls == 2, h[2], h[3]))
            )
            out[f, l] = current[f, l] + (push - share[f])
        return c

    lax.fori_loop(0, slab, close, 0, unroll=2)


def finish(moved, ends, share, classes, params, u_t, n_lb):
    fields, slab = moved.shape[:2]
    group = 5 if fields % 5 == 0 else 1
    f32 = jnp.float32
    return pl.pallas_call(
        functools.partial(finish_kernel, n_lb),
        out_shape=jax.ShapeDtypeStruct(moved.shape, f32),
        grid=(fields // group,),
        in_specs=[
            pl.BlockSpec((group, slab, 8, 128), lambda i: (i, 0, 0, 0)),
            pl.BlockSpec((group, 2 * SUBSTEPS, 8, 128), lambda i: (i, 0, 0, 0)),
            pl.BlockSpec((group, 8, 128), lambda i: (i, 0, 0)),
            pl.BlockSpec((8, 128), lambda i: (0, 0)),
            pl.BlockSpec(memory_space=pltpu.SMEM),
            pl.BlockSpec(memory_space=pltpu.SMEM),
        ],
        out_specs=pl.BlockSpec((group, slab, 8, 128), lambda i: (i, 0, 0, 0)),
        scratch_shapes=[
            pltpu.VMEM((group, slab, 8, 128), f32),
            pltpu.VMEM((group, slab, 8, 128), f32),
            pltpu.VMEM((slab, 8, 128), f32),
            pltpu.VMEM((slab, 8, 128), f32),
            pltpu.VMEM((slab, 8, 128), f32),
        ],
        compiler_params=pltpu.CompilerParams(vmem_limit_bytes=32 * 1024 * 1024),
    )(moved, ends, share, classes, params, u_t)


def local(atmosphere_state, diffusivity, mixing, relaxation, forcing, span_map, cost_class):
    fields, slab, width_x, width_y = atmosphere_state.shape
    n_ex, n_ey, n_lb = (lax.axis_size(a) for a in ("ex", "ey", "lb"))
    levels = slab * n_lb
    zero = jnp.zeros((1,), jnp.float32)
    params = jnp.concatenate(
        [
            jnp.concatenate([zero, mixing])[None],
            jnp.concatenate([mixing, zero])[None],
            relaxation[None],
            jnp.zeros((5, levels), jnp.float32),
            forcing,
            jnp.ones((1, levels), jnp.float32),
        ]
    )
    u_t, sum_t, v_t, coef_t = prep(params, slab, n_lb)
    dims = (n_ex, n_ey, n_lb, fields, slab)
    moved, ends, share = dynamics(
        dims, atmosphere_state, cost_class, span_map.reshape(1, width_x * width_y),
        diffusivity, u_t, sum_t, v_t, coef_t,
    )
    share = share.reshape(16, 8, 128)
    return finish(moved, ends, share, cost_class, params, u_t, n_lb)


def solution(mesh):
    return jax.shard_map(
        local,
        mesh=mesh,
        in_specs=(
            P(None, "lb", "ex", "ey"),
            P(),
            P(),
            P(),
            P(),
            P("ex", "ey", None),
            P("ex", "ey"),
        ),
        out_specs=P(None, "lb", "ex", "ey"),
        check_vma=False,
    )
```

```python
import functools
import math

import jax
import jax.numpy as jnp
import numpy as np
from jax import lax
from jax.experimental import pallas as pl
from jax.experimental.pallas import tpu as pltpu
from jax.sharding import PartitionSpec as P

STEPS = 2
SUBSTEPS = 4
MESH = pl.DeviceIdType.MESH
SKEW = 4
VMEM_MIB = 63


def second_table():
    inner_root = 1.0 / math.sqrt(5.0)
    gll_nodes = np.array([-1.0, -inner_root, inner_root, 1.0])
    weights = np.array(
        [
            np.prod(
                [gll_nodes[target] - gll_nodes[source] for source in range(4) if source != target]
            )
            for target in range(4)
        ]
    )
    first_table = np.zeros((4, 4))
    for target in range(4):
        for source in range(4):
            if source != target:
                first_table[target, source] = weights[target] / (
                    weights[source] * (gll_nodes[target] - gll_nodes[source])
                )
    for target in range(4):
        first_table[target, target] = -first_table[target].sum()
    return (first_table @ first_table).astype(np.float32)


def operator_tables(width_x, width_y):
    second = second_table()
    along = np.kron(np.eye(width_y // 4), second.T).astype(np.float64)
    edge = np.zeros((width_y, width_y))
    for y in range(width_y):
        if y % 4 == 3:
            edge[y, y] = 0.5
            if y + 1 < width_y:
                edge[y + 1, y] = 0.5
        elif y % 4 == 0:
            edge[y, y] = 0.5
            if y > 0:
                edge[y - 1, y] = 0.5
        else:
            edge[y, y] = 1.0
    rim = np.zeros((width_y, width_y))
    rim[0, width_y - 1] = 0.5
    rim[width_y - 1, 0] = 0.5
    both = np.concatenate([edge, rim], axis=1)
    weight = np.concatenate([along @ both, both], axis=0).astype(np.float32)
    shifts = np.zeros((7, width_x, width_y), np.float32)
    for x in range(width_x):
        for d in range(-3, 4):
            if 0 <= x % 4 + d < 4:
                shifts[d + 3, x, :] = second[x % 4, x % 4 + d]
    return weight, shifts


def series_mul(u, v):
    return [sum(u[i] * v[k - i] for i in range(k + 1)) for k in range(len(u))]


def series_inverse(u):
    first = 1.0 / u[0]
    out = [first]
    for k in range(1, len(u)):
        out.append(-first * sum(u[i] * out[k - i] for i in range(1, k + 1)))
    return out


def prepare(slab, count, params, mix_in, relax_in, push_in, u_out, sum_out, v_out, coef_out):
    levels = relax_in.shape[1]
    fields = push_in.shape[0]
    shape = (8, levels)
    params[...] = jnp.zeros_like(params)
    params[0:1, 0 : levels - 1] = mix_in[...]
    params[8 : 8 + fields, :] = push_in[...]
    params[23:24, :] = jnp.ones((1, levels), jnp.float32)
    hi = jnp.broadcast_to(params[0:1, :], shape)
    lo = pltpu.roll(hi, 1, 1)
    rel = jnp.broadcast_to(relax_in[...], shape)
    params[1:2, :] = relax_in[...]
    params[2:3, :] = lo[0:1, :]
    lane = lax.broadcasted_iota(jnp.int32, shape, 1)
    row = lax.broadcasted_iota(jnp.int32, shape, 0)
    diag = 1.0 + rel + lo + hi

    def back(x, s):
        return pltpu.roll(x, s, 1)

    def ahead(x, s):
        return pltpu.roll(x, levels - s, 1)

    def reduce_system(a, b, c, extent):
        stages = []
        s = 1
        while s < extent:
            alpha = -a / back(b, s)
            gamma = -c / ahead(b, s)
            b = b + alpha * back(c, s) + gamma * ahead(a, s)
            a = alpha * back(a, s)
            c = gamma * ahead(c, s)
            stages.append((s, alpha, gamma))
            s *= 2
        return stages, 1.0 / b

    def solve(system, d):
        stages, inverse = system
        for s, alpha, gamma in stages:
            d = d + alpha * back(d, s) + gamma * ahead(d, s)
        return d * inverse

    whole = reduce_system(-lo, diag, -hi, levels)
    cut = reduce_system(
        jnp.where(lane % slab == 0, 0.0, -lo),
        diag,
        jnp.where(lane % slab == slab - 1, 0.0, -hi),
        slab,
    )
    push = [params[8:16, :], jnp.where(row == 7, 0.0, params[16:24, :])]
    held = [params[8:16, :], params[16:24, :]]
    sums = [jnp.zeros(shape, jnp.float32)] * 2
    for k in range(SUBSTEPS + 1):
        for h in range(2):
            u_out[k * 16 + h * 8 : k * 16 + h * 8 + 8, :] = held[h]
            sums[h] = jnp.where(lane == k, jnp.sum(held[h], axis=1, keepdims=True), sums[h])
        if k < SUBSTEPS:
            held = [solve(whole, held[h]) + push[h] for h in range(2)]

    sum_out[0:8, :] = sums[0]
    sum_out[8:16, :] = sums[1]
    spot = jnp.where(row < 4, row * slab + slab - 1, (row - 4) * slab)
    tips = jnp.where((lane == spot) & (row % 4 < count), 1.0, 0.0)
    other = pltpu.roll(tips, 4, 0)

    def total(x):
        return jnp.broadcast_to(jnp.sum(x, axis=1, keepdims=True), shape)

    mix = total(jnp.where(row < 4, lo, hi) * other)
    near, far = [], []
    v = tips
    for k in range(SUBSTEPS):
        v = solve(cut, v)
        v_out[k * 8 : k * 8 + 8, :] = v
        near.append(total(v * tips))
        far.append(total(v * other))
    facing = [pltpu.roll(x, 4, 0) for x in near]
    square = mix * mix
    far_far = series_mul(far, far)

    def beside(z):
        return [jnp.where(row < 4, pltpu.roll(x, 1, 0), pltpu.roll(x, 7, 0)) for x in z]

    def gain(u, v):
        product = series_mul(u, v)
        return series_inverse(
            [(1.0 if k == 0 else 0.0) - square * x for k, x in enumerate(product)]
        )

    z = near
    for _ in range(count - 1):
        zn = beside(z)
        change = series_mul(series_mul(far_far, zn), gain(zn, facing))
        z = [x + square * y for x, y in zip(near, change)]
    zn = beside(z)
    first = [mix * x for x in series_mul(far, gain(zn, facing))]
    next_ = [mix * x for x in series_mul(first, zn)]
    edge = gain(zn, [pltpu.roll(x, 4, 0) for x in z])
    edge_one = [mix * x for x in edge]
    edge_two = [mix * x for x in series_mul(edge_one, zn)]
    packed = jnp.zeros(shape, jnp.float32)
    for g, part in enumerate((first, next_, edge_one, edge_two)):
        for k in range(SUBSTEPS):
            packed = jnp.where(lane == g * SUBSTEPS + k, part[k], packed)
    coef_out[...] = packed


def main_kernel(
    dims,
    state_h, classes_h, span_h, w_h, shifts_h, rate_h, mix_h, relax_h, push_h,
    out,
    state, classes, span, table, weight, shifts, rate, mix_v, relax_v, push_v,
    params, u_v, sum_v, v_v, coef_v, u_s, sum_s, v_s, coef_s, own_s,
    moved, swept, carry, scale, link, share,
    lap, hy_out, hy_in, x_out, x_in, weights, p_loc, q_loc, p_out, p_in, q_out, q_in,
    tend, hot, slots, got_one, part, got_two, full,
    state_sem, in_sem, table_sem,
    ys, yr, xs, xr, ps, pr, qs, qr, os, o_r, ts, t_r, fs, f_r,
):
    n_ex, n_ey, n_lb, fields, slab = dims
    rows = slab * 8
    tiles = n_ex * n_ey
    ex, ey, lb = lax.axis_index("ex"), lax.axis_index("ey"), lax.axis_index("lb")
    tile = ex * n_ey + ey
    sides = 1 if n_ey == 2 else 2

    def tile_peer(o):
        t = lax.rem(tile + o, tiles)
        return (t // n_ey, lax.rem(t, n_ey), lb)

    def slab_peer(o):
        return (ex, ey, lax.rem(lb + o, n_lb))

    barrier = pltpu.get_barrier_semaphore()

    def greet_tiles(o, c):
        pl.semaphore_signal(barrier, inc=1, device_id=tile_peer(o), device_id_type=MESH)
        return c

    def greet_slabs(o, c):
        pl.semaphore_signal(barrier, inc=1, device_id=slab_peer(o), device_id_type=MESH)
        return c

    loads = [
        pltpu.make_async_copy(a, b, in_sem.at[i])
        for i, (a, b) in enumerate(
            (
                (shifts_h, shifts), (w_h, table), (classes_h, classes), (span_h, span),
                (rate_h, rate), (mix_h, mix_v), (relax_h, relax_v), (push_h, push_v),
            )
        )
    ]

    def load_state(f):
        return pltpu.make_async_copy(state_h.at[f], state.at[f], state_sem.at[f])

    def fetch(f, c):
        load_state(f).start()
        return c

    for copy in loads[:2]:
        copy.start()
    lax.fori_loop(0, fields, fetch, 0)
    for copy in loads[2:]:
        copy.start()
    lax.fori_loop(1, tiles, greet_tiles, 0)
    lax.fori_loop(1, n_lb, greet_slabs, 0)

    row_x = lax.broadcasted_iota(jnp.int32, (8, 128), 0)
    lane = lax.broadcasted_iota(jnp.int32, (8, 128), 1)
    def derive(f, source, step):
        s = source[f]
        along = shifts[3][None] * s
        for d in (-3, -2, -1, 1, 2, 3):
            along = along + shifts[d + 3][None] * pltpu.roll(s, (8 - d) % 8, 1)
        both = jnp.concatenate([s.reshape(rows, 128), along.reshape(rows, 128)], axis=1)
        high = both.astype(jnp.bfloat16)
        low = (both - high.astype(jnp.float32)).astype(jnp.bfloat16)
        result = (
            jnp.dot(high, weight[0], preferred_element_type=jnp.float32)
            + jnp.dot(low, weight[0], preferred_element_type=jnp.float32)
            + jnp.dot(high, weight[1], preferred_element_type=jnp.float32)
        )
        lap[f] = result[:, :128]
        hy_out[step, f] = result[:, 128:]

    def y_copy(step, f, side):
        peer = lax.rem(ey + (1 if side == 0 else n_ey - 1), n_ey)
        return pltpu.make_async_remote_copy(
            src_ref=hy_out.at[step, f],
            dst_ref=hy_in.at[step, side, f],
            send_sem=ys.at[step, side, f],
            recv_sem=yr.at[step, side, f],
            device_id=(ex, peer, lb),
            device_id_type=MESH,
        )

    def x_copy(step, f, side):
        peer = lax.rem(ex + (1 if side == 0 else n_ex - 1), n_ex)
        return pltpu.make_async_remote_copy(
            src_ref=x_out.at[step, side, f],
            dst_ref=x_in.at[step, side, f],
            send_sem=xs.at[step, side, f],
            recv_sem=xr.at[step, side, f],
            device_id=(peer, ey, lb),
            device_id_type=MESH,
        )

    def start_y(f, step):
        for side in range(sides):
            y_copy(step, f, side).start()

    def spread(f, step):
        for side in range(sides):
            y_copy(step, f, side).wait_recv()
        value = lap[f].reshape(slab, 8, 128)
        if sides == 1:
            value = value + hy_in[step, 0, f].reshape(slab, 8, 128)
        else:
            value = value + jnp.where(lane == 0, hy_in[step, 0, f].reshape(slab, 8, 128), 0.0)
            value = value + jnp.where(lane == 127, hy_in[step, 1, f].reshape(slab, 8, 128), 0.0)
        lap[f] = value.reshape(rows, 128)
        x_out[step, 0, f] = lap[f, pl.ds(7, slab, stride=8), :]
        x_out[step, 1, f] = lap[f, pl.ds(0, slab, stride=8), :]
        x_copy(step, f, 0).start()
        x_copy(step, f, 1).start()

    def advance(f, source, step):
        x_copy(step, f, 0).wait_recv()
        x_copy(step, f, 1).wait_recv()
        value = lap[f].reshape(slab, 8, 128)
        before = pltpu.roll(value, 1, 1)
        after = pltpu.roll(value, 7, 1)
        first = jnp.broadcast_to(x_in[step, 0, f][:, None, :], (slab, 8, 128))
        last = jnp.broadcast_to(x_in[step, 1, f][:, None, :], (slab, 8, 128))
        partner = jnp.where(
            row_x == 0,
            first,
            jnp.where(row_x == 7, last, jnp.where(row_x == 3, after, before)),
        )
        joins = (row_x == 0) | (row_x == 3) | (row_x == 4) | (row_x == 7)
        edged = jnp.where(joins, 0.5 * (value + partner), value)
        moved[f] = source[f] + rate[f] * edged

    for copy in loads[:2]:
        copy.wait()
    high = table[...].astype(jnp.bfloat16)
    weight[0] = high
    weight[1] = (table[...] - high.astype(jnp.float32)).astype(jnp.bfloat16)
    load_state(0).wait()
    derive(0, state, 0)
    pl.semaphore_wait(barrier, tiles - 1 + n_lb - 1)
    start_y(0, 0)

    def open_rest(f, c):
        load_state(f).wait()
        derive(f, state, 0)
        start_y(f, 0)
        spread(f - 1, 0)
        return c

    lax.fori_loop(1, fields, open_rest, 0)
    spread(fields - 1, 0)
    for copy in loads[2:]:
        copy.wait()
    cls = classes[...]
    prepare(slab, n_lb, params, mix_v, relax_v, push_v, u_v, sum_v, v_v, coef_v)
    own_v = ((u_v, u_s), (sum_v, sum_s), (v_v, v_s), (coef_v, coef_s))
    tables = [pltpu.make_async_copy(a, b, table_sem.at[i]) for i, (a, b) in enumerate(own_v)]
    tables.append(pltpu.make_async_copy(params, own_s, table_sem.at[4]))
    for copy in tables:
        copy.start()
    for x in range(8):
        mine = lax.broadcasted_iota(jnp.int32, (128, 1024), 0) + x * 128
        hot[x * 128 : (x + 1) * 128, :] = (
            (mine == span[...]).astype(jnp.float32).astype(jnp.bfloat16)
        )
    for copy in tables:
        copy.wait()

    def factor(l, previous):
        at = lb * slab + l
        high = own_s[0, at]
        low = own_s[2, at]
        inner_low = jnp.where(l == 0, 0.0, low)
        inner_high = jnp.where(l == slab - 1, 0.0, high)
        ratio = inner_low * previous
        inverse = 1.0 / (1.0 + own_s[1, at] + low + high - inner_low * ratio)
        carry[l] = ratio
        scale[l] = inverse
        link[l] = inner_high * inverse
        return inverse

    lax.fori_loop(0, slab, factor, jnp.zeros((8, 128), jnp.float32))

    def set_weight(l, c):
        at = lb * slab + l
        w = [u_s[k * 16 + 15, at] - 1.0 for k in range(1, 5)]
        weights[l] = jnp.where(
            cls == 0, w[0], jnp.where(cls == 1, w[1], jnp.where(cls == 2, w[2], w[3]))
        )
        return c

    lax.fori_loop(0, slab, set_weight, 0)
    def middle(f, c):
        advance(f, state, 0)
        derive(f, moved, 1)
        start_y(f, 1)

        @pl.when(f > 0)
        def _():
            spread(f - 1, 1)

        return c

    lax.fori_loop(0, fields, middle, 0)
    spread(fields - 1, 1)

    def pick(group, k, base):
        return coef_s[base + lb, group * SUBSTEPS + k]

    def convolve(group, base, k, value):
        out = pick(group, 0, base) * value[k]
        for i in range(1, k + 1):
            out = out + pick(group, i, base) * value[k - i]
        return out

    def scan_copy(f, down):
        if down:
            return pltpu.make_async_remote_copy(
                src_ref=p_out.at[f], dst_ref=p_in.at[f],
                send_sem=ps.at[f], recv_sem=pr.at[f],
                device_id=(ex, ey, lax.rem(lb + 1, n_lb)), device_id_type=MESH,
            )
        return pltpu.make_async_remote_copy(
            src_ref=q_out.at[f], dst_ref=q_in.at[f],
            send_sem=qs.at[f], recv_sem=qr.at[f],
            device_id=(ex, ey, lax.rem(lb + n_lb - 1, n_lb)), device_id_type=MESH,
        )

    def scan_step(f, down):
        arrives = lb > 0 if down else lb < n_lb - 1
        leaves = lb < n_lb - 1 if down else lb > 0
        inward, outward = (p_in, p_out) if down else (q_in, q_out)
        same, opposite = (p_loc, q_loc) if down else (q_loc, p_loc)
        base = 0 if down else 4

        @pl.when((f >= 0) & (f < fields))
        def _():
            @pl.when(arrives)
            def _():
                scan_copy(f, down).wait_recv()
                own = [same[f, k] for k in range(SUBSTEPS)]
                facing = [opposite[f, k] for k in range(SUBSTEPS)]
                coming = [inward[f, k] for k in range(SUBSTEPS)]
                for k in range(SUBSTEPS):
                    outward[f, k] = (
                        own[k] + convolve(0, base, k, coming) + convolve(1, base, k, facing)
                    )

            @pl.when(jnp.logical_not(arrives))
            def _():
                for k in range(SUBSTEPS):
                    outward[f, k] = same[f, k]

            @pl.when(leaves)
            def _():
                scan_copy(f, down).start()

    def scan_steps(i):
        scan_step(i - lb * SKEW, True)
        scan_step(i - (n_lb - 1 - lb) * SKEW, False)

    def summarise(f):
        zero = jnp.zeros((8, 128), jnp.float32)

        def level(l, c):
            x = moved[f, l]
            at = lb * slab + l
            out = [c[k] + v_s[k * 8 + lb, at] * x for k in range(4)]
            out += [c[4 + k] + v_s[k * 8 + 4 + lb, at] * x for k in range(4)]
            out.append(c[8] + weights[l] * x)
            return tuple(out)

        sums = lax.fori_loop(0, slab, level, (zero,) * 9, unroll=8)
        for k in range(SUBSTEPS):
            p_loc[f, k] = sums[k]
            q_loc[f, k] = sums[4 + k]
        h = [sum_s[f, k] * (1.0 / n_lb) for k in range(4)]
        extra = jnp.where(
            cls == 0, h[0], jnp.where(cls == 1, h[1], jnp.where(cls == 2, h[2], h[3]))
        )
        tend[pl.ds(pl.multiple_of(f * 8, 8), 8), :] = sums[8] + extra

    tend[fields * 8 : 128, :] = jnp.zeros((128 - fields * 8, 128), jnp.float32)

    def closing(i, c):
        advance(i, moved, 1)
        summarise(i)
        scan_steps(i)
        return c

    lax.fori_loop(0, fields, closing, 0)

    def three(value):
        a = value.astype(jnp.bfloat16)
        rest = value - a.astype(jnp.float32)
        b = rest.astype(jnp.bfloat16)
        return a, b, (rest - b.astype(jnp.float32)).astype(jnp.bfloat16)

    span_slots = 1024 // n_lb
    gathered = jnp.zeros((16, 1024), jnp.float32)
    for x in range(8):
        for piece in three(tend[pl.ds(x, 16, stride=8), :]):
            gathered = gathered + jnp.dot(
                piece, hot[x * 128 : (x + 1) * 128, :], preferred_element_type=jnp.float32
            )
    for g in range(n_lb):
        slots[g] = gathered[:, g * span_slots : (g + 1) * span_slots]

    def one_copy(o):
        return pltpu.make_async_remote_copy(
            src_ref=slots.at[lax.rem(lb + o, n_lb)], dst_ref=got_one.at[o - 1],
            send_sem=os.at[o - 1], recv_sem=o_r.at[o - 1],
            device_id=slab_peer(o), device_id_type=MESH,
        )

    def two_copy(o):
        return pltpu.make_async_remote_copy(
            src_ref=part, dst_ref=got_two.at[o - 1],
            send_sem=ts.at[o - 1], recv_sem=t_r.at[o - 1],
            device_id=tile_peer(o), device_id_type=MESH,
        )

    def three_copy(o):
        return pltpu.make_async_remote_copy(
            src_ref=full.at[lb], dst_ref=full.at[lb],
            send_sem=fs.at[o - 1], recv_sem=f_r.at[o - 1],
            device_id=slab_peer(o), device_id_type=MESH,
        )

    def three_arrival(o):
        other = lax.rem(lb + n_lb - o, n_lb)
        return pltpu.make_async_remote_copy(
            src_ref=full.at[other], dst_ref=full.at[other],
            send_sem=fs.at[o - 1], recv_sem=f_r.at[o - 1],
            device_id=slab_peer(o), device_id_type=MESH,
        )

    for o in range(1, n_lb):
        one_copy(o).start()

    tail = (n_lb - 1) * SKEW
    half = fields + tail // 2

    def trailing(i, c):
        scan_steps(i)
        return c

    lax.fori_loop(fields, half, trailing, 0)
    total = slots[lb]
    for o in range(1, n_lb):
        one_copy(o).wait_recv()
        total = total + got_one[o - 1]
    part[...] = total

    def start_two(o, c):
        two_copy(o).start()
        return c

    lax.fori_loop(1, tiles, start_two, 0)
    lax.fori_loop(half, fields + tail, trailing, 0)

    def add_two(o, c):
        two_copy(o).wait_recv()
        return c + got_two[o - 1]

    total = lax.fori_loop(1, tiles, add_two, part[...])
    full[lb] = total * (1.0 / (tiles * slab * n_lb))
    for o in range(1, n_lb):
        three_copy(o).start()

    @pl.when(lb == 0)
    def _():
        p_in[...] = jnp.zeros_like(p_in)

    @pl.when(lb == n_lb - 1)
    def _():
        q_in[...] = jnp.zeros_like(q_in)

    group = 5 if fields % 5 == 0 else 1

    def sweep(g, c):
        at = pl.ds(g * group, group)
        above = [p_in[at, k] for k in range(SUBSTEPS)]
        below = [q_in[at, k] for k in range(SUBSTEPS)]
        own_p = [p_out[at, k] for k in range(SUBSTEPS)]
        own_q = [q_out[at, k] for k in range(SUBSTEPS)]
        for k in range(SUBSTEPS):
            p_loc[at, k] = convolve(2, 0, k, above) + convolve(3, 0, k, own_q)
            q_loc[at, k] = convolve(2, 4, k, below) + convolve(3, 4, k, own_p)
        for k in range(SUBSTEPS):

            def down(l, z):
                z = moved[at, l] + carry[l][None] * z
                swept[at, l] = z
                return z

            z = moved[at, 0] + p_loc[at, k]
            swept[at, 0] = z
            z = lax.fori_loop(1, slab, down, z, unroll=4)
            y = (z + q_loc[at, k]) * scale[slab - 1][None]
            active = cls >= k
            moved[at, slab - 1] = jnp.where(active, y, moved[at, slab - 1])

            def up(i, y, active=active):
                l = slab - 1 - i
                y = swept[at, l] * scale[l][None] + link[l][None] * y
                moved[at, l] = jnp.where(active, y, moved[at, l])
                return y

            lax.fori_loop(1, slab, up, y, unroll=4)

        def close(l, c):
            for f in range(group):
                h = [u_s[k * 16 + g * group + f, lb * slab + l] for k in range(4)]
                push = jnp.where(
                    cls == 0, h[0], jnp.where(cls == 1, h[1], jnp.where(cls == 2, h[2], h[3]))
                )
                moved[g * group + f, l] = moved[g * group + f, l] + push
            return c

        return lax.fori_loop(0, slab, close, c, unroll=2)

    lax.fori_loop(0, fields // group, sweep, 0)
    for o in range(1, n_lb):
        three_arrival(o).wait_recv()
    for x in range(8):
        value = jnp.zeros((16, 128), jnp.float32)
        for g in range(n_lb):
            pick_hot = hot[x * 128 : (x + 1) * 128, g * span_slots : (g + 1) * span_slots]
            for piece in three(full[g]):
                value = value + lax.dot_general(
                    piece, pick_hot, (((1,), (1,)), ((), ())),
                    preferred_element_type=jnp.float32,
                )
        share[pl.ds(x, 16, stride=8), :] = value

    def store(f):
        return pltpu.make_async_copy(moved.at[f], out.at[f], state_sem.at[f])

    def settle(f, c):
        moved[f] = moved[f] - share[pl.ds(pl.multiple_of(f * 8, 8), 8), :][None]
        store(f).start()
        return c

    lax.fori_loop(0, fields, settle, 0)

    def drain(f, c):
        store(f).wait()
        for step in range(STEPS):
            for side in range(sides):
                y_copy(step, f, side).wait_send()
            for side in range(2):
                x_copy(step, f, side).wait_send()

        @pl.when(lb < n_lb - 1)
        def _():
            scan_copy(f, True).wait_send()

        @pl.when(lb > 0)
        def _():
            scan_copy(f, False).wait_send()

        return c

    lax.fori_loop(0, fields, drain, 0)
    for o in range(1, n_lb):
        one_copy(o).wait_send()
        three_copy(o).wait_send()

    def drain_two(o, c):
        two_copy(o).wait_send()
        return c

    lax.fori_loop(1, tiles, drain_two, 0)


def local(atmosphere_state, diffusivity, mixing, relaxation, forcing, span_map, cost_class):
    fields, slab, width_x, width_y = atmosphere_state.shape
    n_ex, n_ey, n_lb = (lax.axis_size(a) for a in ("ex", "ey", "lb"))
    levels = slab * n_lb
    dims = (n_ex, n_ey, n_lb, fields, slab)
    rows = slab * 8
    tiles = n_ex * n_ey
    sides = 1 if n_ey == 2 else 2
    weight, shifts = operator_tables(width_x, width_y)
    hbm = pl.BlockSpec(memory_space=pltpu.HBM)
    f32 = jnp.float32
    dma = pltpu.SemaphoreType.DMA
    wide = 1024 // n_lb
    volume = (fields, slab, 8, 128)
    return pl.pallas_call(
        functools.partial(main_kernel, dims),
        out_shape=jax.ShapeDtypeStruct(volume, f32),
        in_specs=[hbm] * 9,
        out_specs=hbm,
        scratch_shapes=[
            pltpu.VMEM(volume, f32),
            pltpu.VMEM((8, 128), jnp.int32),
            pltpu.VMEM((1, 1024), jnp.int32),
            pltpu.VMEM((256, 256), f32),
            pltpu.VMEM((2, 256, 256), jnp.bfloat16),
            pltpu.VMEM((7, 8, 128), f32),
            pltpu.SMEM((fields,), f32),
            pltpu.VMEM((1, levels - 1), f32),
            pltpu.VMEM((1, levels), f32),
            pltpu.VMEM((fields, levels), f32),
            pltpu.VMEM((24, levels), f32),
            pltpu.VMEM((80, levels), f32),
            pltpu.VMEM((16, levels), f32),
            pltpu.VMEM((SUBSTEPS * 8, levels), f32),
            pltpu.VMEM((8, levels), f32),
            pltpu.SMEM((80, levels), f32),
            pltpu.SMEM((16, levels), f32),
            pltpu.SMEM((SUBSTEPS * 8, levels), f32),
            pltpu.SMEM((8, levels), f32),
            pltpu.SMEM((24, levels), f32),
            pltpu.VMEM(volume, f32),
            pltpu.VMEM(volume, f32),
            pltpu.VMEM((slab, 8, 128), f32),
            pltpu.VMEM((slab, 8, 128), f32),
            pltpu.VMEM((slab, 8, 128), f32),
            pltpu.VMEM((128, 128), f32),
            pltpu.VMEM((fields, rows, 128), f32),
            pltpu.VMEM((STEPS, fields, rows, 128), f32),
            pltpu.VMEM((STEPS, sides, fields, rows, 128), f32),
            pltpu.VMEM((STEPS, 2, fields, slab, 128), f32),
            pltpu.VMEM((STEPS, 2, fields, slab, 128), f32),
            pltpu.VMEM((slab, 8, 128), f32),
        ]
        + [pltpu.VMEM((fields, SUBSTEPS, 8, 128), f32)] * 6
        + [
            pltpu.VMEM((128, 128), f32),
            pltpu.VMEM((1024, 1024), jnp.bfloat16),
            pltpu.VMEM((n_lb, 16, wide), f32),
            pltpu.VMEM((n_lb - 1, 16, wide), f32),
            pltpu.VMEM((16, wide), f32),
            pltpu.VMEM((tiles - 1, 16, wide), f32),
            pltpu.VMEM((n_lb, 16, wide), f32),
            dma((fields,)),
            dma((8,)),
            dma((5,)),
            dma((STEPS, sides, fields)),
            dma((STEPS, sides, fields)),
            dma((STEPS, 2, fields)),
            dma((STEPS, 2, fields)),
            dma((fields,)),
            dma((fields,)),
            dma((fields,)),
            dma((fields,)),
            dma((n_lb - 1,)),
            dma((n_lb - 1,)),
            dma((tiles - 1,)),
            dma((tiles - 1,)),
            dma((n_lb - 1,)),
            dma((n_lb - 1,)),
        ],
        compiler_params=pltpu.CompilerParams(
            collective_id=0, has_side_effects=True, vmem_limit_bytes=VMEM_MIB * 1024 * 1024
        ),
    )(
        atmosphere_state, cost_class, span_map.reshape(1, width_x * width_y),
        jnp.asarray(weight), jnp.asarray(shifts), diffusivity,
        mixing.reshape(1, levels - 1), relaxation.reshape(1, levels), forcing,
    )


def solution(mesh):
    return jax.shard_map(
        local,
        mesh=mesh,
        in_specs=(
            P(None, "lb", "ex", "ey"),
            P(),
            P(),
            P(),
            P(),
            P("ex", "ey", None),
            P("ex", "ey"),
        ),
        out_specs=P(None, "lb", "ex", "ey"),
        check_vma=False,
    )
```

```python
import functools
import math

import jax
import jax.numpy as jnp
import numpy as np
from jax import lax
from jax.experimental import pallas as pl
from jax.experimental.pallas import tpu as pltpu
from jax.sharding import PartitionSpec as P

STEPS = 2
SUBSTEPS = 4
MESH = pl.DeviceIdType.MESH
SKEW = 2
VMEM_MIB = 63


def second_table():
    inner_root = 1.0 / math.sqrt(5.0)
    gll_nodes = np.array([-1.0, -inner_root, inner_root, 1.0])
    weights = np.array(
        [
            np.prod(
                [gll_nodes[target] - gll_nodes[source] for source in range(4) if source != target]
            )
            for target in range(4)
        ]
    )
    first_table = np.zeros((4, 4))
    for target in range(4):
        for source in range(4):
            if source != target:
                first_table[target, source] = weights[target] / (
                    weights[source] * (gll_nodes[target] - gll_nodes[source])
                )
    for target in range(4):
        first_table[target, target] = -first_table[target].sum()
    return (first_table @ first_table).astype(np.float32)


def operator_tables(width_x, width_y):
    second = second_table()
    along = np.kron(np.eye(width_y // 4), second.T).astype(np.float64)
    edge = np.zeros((width_y, width_y))
    for y in range(width_y):
        if y % 4 == 3:
            edge[y, y] = 0.5
            if y + 1 < width_y:
                edge[y + 1, y] = 0.5
        elif y % 4 == 0:
            edge[y, y] = 0.5
            if y > 0:
                edge[y - 1, y] = 0.5
        else:
            edge[y, y] = 1.0
    rim = np.zeros((width_y, width_y))
    rim[0, width_y - 1] = 0.5
    rim[width_y - 1, 0] = 0.5
    both = np.concatenate([edge, rim], axis=1)
    weight = np.concatenate([along @ both, both], axis=0).astype(np.float32)
    shifts = np.zeros((7, width_x, width_y), np.float32)
    for x in range(width_x):
        for d in range(-3, 4):
            if 0 <= x % 4 + d < 4:
                shifts[d + 3, x, :] = second[x % 4, x % 4 + d]
    return weight, shifts


def series_mul(u, v):
    return [sum(u[i] * v[k - i] for i in range(k + 1)) for k in range(len(u))]


def series_inverse(u):
    first = 1.0 / u[0]
    out = [first]
    for k in range(1, len(u)):
        out.append(-first * sum(u[i] * out[k - i] for i in range(1, k + 1)))
    return out


def prepare(slab, count, params, mix_in, relax_in, push_in, u_out, sum_out, v_out, coef_out):
    levels = relax_in.shape[1]
    fields = push_in.shape[0]
    shape = (8, levels)
    params[...] = jnp.zeros_like(params)
    params[0:1, 0 : levels - 1] = mix_in[...]
    params[8 : 8 + fields, :] = push_in[...]
    params[23:24, :] = jnp.ones((1, levels), jnp.float32)
    hi = jnp.broadcast_to(params[0:1, :], shape)
    lo = pltpu.roll(hi, 1, 1)
    rel = jnp.broadcast_to(relax_in[...], shape)
    params[1:2, :] = relax_in[...]
    params[2:3, :] = lo[0:1, :]
    lane = lax.broadcasted_iota(jnp.int32, shape, 1)
    row = lax.broadcasted_iota(jnp.int32, shape, 0)
    diag = 1.0 + rel + lo + hi

    def back(x, s):
        return pltpu.roll(x, s, 1)

    def ahead(x, s):
        return pltpu.roll(x, levels - s, 1)

    def reduce_system(a, b, c, extent):
        stages = []
        s = 1
        while s < extent:
            alpha = -a / back(b, s)
            gamma = -c / ahead(b, s)
            b = b + alpha * back(c, s) + gamma * ahead(a, s)
            a = alpha * back(a, s)
            c = gamma * ahead(c, s)
            stages.append((s, alpha, gamma))
            s *= 2
        return stages, 1.0 / b

    def solve(system, d):
        stages, inverse = system
        for s, alpha, gamma in stages:
            d = d + alpha * back(d, s) + gamma * ahead(d, s)
        return d * inverse

    whole = reduce_system(-lo, diag, -hi, levels)
    cut = reduce_system(
        jnp.where(lane % slab == 0, 0.0, -lo),
        diag,
        jnp.where(lane % slab == slab - 1, 0.0, -hi),
        slab,
    )
    push = [params[8:16, :], jnp.where(row == 7, 0.0, params[16:24, :])]
    held = [params[8:16, :], params[16:24, :]]
    sums = [jnp.zeros(shape, jnp.float32)] * 2
    for k in range(SUBSTEPS + 1):
        for h in range(2):
            u_out[k * 16 + h * 8 : k * 16 + h * 8 + 8, :] = held[h]
            sums[h] = jnp.where(lane == k, jnp.sum(held[h], axis=1, keepdims=True), sums[h])
        if k < SUBSTEPS:
            held = [solve(whole, held[h]) + push[h] for h in range(2)]

    sum_out[0:8, :] = sums[0]
    sum_out[8:16, :] = sums[1]
    spot = jnp.where(row < 4, row * slab + slab - 1, (row - 4) * slab)
    tips = jnp.where((lane == spot) & (row % 4 < count), 1.0, 0.0)
    other = pltpu.roll(tips, 4, 0)

    def total(x):
        return jnp.broadcast_to(jnp.sum(x, axis=1, keepdims=True), shape)

    mix = total(jnp.where(row < 4, lo, hi) * other)
    near, far = [], []
    v = tips
    for k in range(SUBSTEPS):
        v = solve(cut, v)
        v_out[k * 8 : k * 8 + 8, :] = v
        near.append(total(v * tips))
        far.append(total(v * other))
    facing = [pltpu.roll(x, 4, 0) for x in near]
    square = mix * mix
    far_far = series_mul(far, far)

    def beside(z):
        return [jnp.where(row < 4, pltpu.roll(x, 1, 0), pltpu.roll(x, 7, 0)) for x in z]

    def gain(u, v):
        product = series_mul(u, v)
        return series_inverse(
            [(1.0 if k == 0 else 0.0) - square * x for k, x in enumerate(product)]
        )

    z = near
    for _ in range(count - 1):
        zn = beside(z)
        change = series_mul(series_mul(far_far, zn), gain(zn, facing))
        z = [x + square * y for x, y in zip(near, change)]
    zn = beside(z)
    first = [mix * x for x in series_mul(far, gain(zn, facing))]
    next_ = [mix * x for x in series_mul(first, zn)]
    edge = gain(zn, [pltpu.roll(x, 4, 0) for x in z])
    edge_one = [mix * x for x in edge]
    edge_two = [mix * x for x in series_mul(edge_one, zn)]
    packed = jnp.zeros(shape, jnp.float32)
    for g, part in enumerate((first, next_, edge_one, edge_two)):
        for k in range(SUBSTEPS):
            packed = jnp.where(lane == g * SUBSTEPS + k, part[k], packed)
    coef_out[...] = packed


def main_kernel(
    dims,
    state_h, classes_h, span_h, w_h, shifts_h, rate_h, mix_h, relax_h, push_h,
    out,
    state, classes, span, table, weight, shifts, rate, mix_v, relax_v, push_v,
    params, u_v, sum_v, v_v, coef_v, u_s, sum_s, v_s, coef_s, own_s,
    moved, swept, carry, scale, link, share,
    lap, hy_out, hy_in, x_out, x_in, weights, p_loc, q_loc, p_out, p_in, q_out, q_in,
    tend, hot, slots, got_one, part, got_two, full,
    state_sem, in_sem, table_sem,
    ys, yr, xs, xr, ps, pr, qs, qr, os, o_r, ts, t_r, fs, f_r,
):
    n_ex, n_ey, n_lb, fields, slab = dims
    rows = slab * 8
    tiles = n_ex * n_ey
    ex, ey, lb = lax.axis_index("ex"), lax.axis_index("ey"), lax.axis_index("lb")
    tile = ex * n_ey + ey
    sides = 1 if n_ey == 2 else 2
    size = 3 if fields % 3 == 0 else 1
    chunks = fields // size

    def tile_peer(o):
        t = lax.rem(tile + o, tiles)
        return (t // n_ey, lax.rem(t, n_ey), lb)

    def slab_peer(o):
        return (ex, ey, lax.rem(lb + o, n_lb))

    barrier = pltpu.get_barrier_semaphore()

    def greet_tiles(o, c):
        pl.semaphore_signal(barrier, inc=1, device_id=tile_peer(o), device_id_type=MESH)
        return c

    def greet_slabs(o, c):
        pl.semaphore_signal(barrier, inc=1, device_id=slab_peer(o), device_id_type=MESH)
        return c

    loads = [
        pltpu.make_async_copy(a, b, in_sem.at[i])
        for i, (a, b) in enumerate(
            (
                (shifts_h, shifts), (w_h, table), (classes_h, classes), (span_h, span),
                (rate_h, rate), (mix_h, mix_v), (relax_h, relax_v), (push_h, push_v),
            )
        )
    ]

    def chunk(f):
        return pl.ds(f * size, size)

    def load_state(f):
        return pltpu.make_async_copy(state_h.at[chunk(f)], state.at[chunk(f)], state_sem.at[f])

    def fetch(f, c):
        load_state(f).start()
        return c

    for copy in loads:
        copy.start()
    lax.fori_loop(0, chunks, fetch, 0)
    lax.fori_loop(1, tiles, greet_tiles, 0)
    lax.fori_loop(1, n_lb, greet_slabs, 0)

    row_x = lax.broadcasted_iota(jnp.int32, (8, 128), 0)
    lane = lax.broadcasted_iota(jnp.int32, (8, 128), 1)
    def derive(f, source, step):
        s = source[chunk(f)].reshape(size * slab, 8, 128)
        along = shifts[3][None] * s
        for d in (-3, -2, -1, 1, 2, 3):
            along = along + shifts[d + 3][None] * pltpu.roll(s, (8 - d) % 8, 1)
        both = jnp.concatenate(
            [s.reshape(size * rows, 128), along.reshape(size * rows, 128)], axis=1
        )
        high = both.astype(jnp.bfloat16)
        low = (both - high.astype(jnp.float32)).astype(jnp.bfloat16)
        result = (
            jnp.dot(high, weight[0], preferred_element_type=jnp.float32)
            + jnp.dot(low, weight[0], preferred_element_type=jnp.float32)
            + jnp.dot(high, weight[1], preferred_element_type=jnp.float32)
        )
        lap[chunk(f)] = result[:, :128].reshape(size, rows, 128)
        hy_out[step, chunk(f)] = result[:, 128:].reshape(size, rows, 128)

    def y_copy(step, f, side):
        peer = lax.rem(ey + (1 if side == 0 else n_ey - 1), n_ey)
        return pltpu.make_async_remote_copy(
            src_ref=hy_out.at[step, chunk(f)],
            dst_ref=hy_in.at[step, side, chunk(f)],
            send_sem=ys.at[step, side, f],
            recv_sem=yr.at[step, side, f],
            device_id=(ex, peer, lb),
            device_id_type=MESH,
        )

    def x_copy(step, f, side):
        peer = lax.rem(ex + (1 if side == 0 else n_ex - 1), n_ex)
        return pltpu.make_async_remote_copy(
            src_ref=x_out.at[step, side, chunk(f)],
            dst_ref=x_in.at[step, side, chunk(f)],
            send_sem=xs.at[step, side, f],
            recv_sem=xr.at[step, side, f],
            device_id=(peer, ey, lb),
            device_id_type=MESH,
        )

    def start_y(f, step):
        for side in range(sides):
            y_copy(step, f, side).start()

    def spread(f, step):
        for side in range(sides):
            y_copy(step, f, side).wait_recv()
        shape = (size * slab, 8, 128)
        value = lap[chunk(f)].reshape(shape)
        if sides == 1:
            value = value + hy_in[step, 0, chunk(f)].reshape(shape)
        else:
            value = value + jnp.where(lane == 0, hy_in[step, 0, chunk(f)].reshape(shape), 0.0)
            value = value + jnp.where(lane == 127, hy_in[step, 1, chunk(f)].reshape(shape), 0.0)
        lap[chunk(f)] = value.reshape(size, rows, 128)
        for i in range(size):
            x_out[step, 0, f * size + i] = lap[f * size + i, pl.ds(7, slab, stride=8), :]
            x_out[step, 1, f * size + i] = lap[f * size + i, pl.ds(0, slab, stride=8), :]
        x_copy(step, f, 0).start()
        x_copy(step, f, 1).start()

    def advance(f, source, step):
        x_copy(step, f, 0).wait_recv()
        x_copy(step, f, 1).wait_recv()
        joins = (row_x == 0) | (row_x == 3) | (row_x == 4) | (row_x == 7)
        for i in range(size):
            g = f * size + i
            value = lap[g].reshape(slab, 8, 128)
            before = pltpu.roll(value, 1, 1)
            after = pltpu.roll(value, 7, 1)
            first = jnp.broadcast_to(x_in[step, 0, g][:, None, :], (slab, 8, 128))
            last = jnp.broadcast_to(x_in[step, 1, g][:, None, :], (slab, 8, 128))
            partner = jnp.where(
                row_x == 0,
                first,
                jnp.where(row_x == 7, last, jnp.where(row_x == 3, after, before)),
            )
            edged = jnp.where(joins, 0.5 * (value + partner), value)
            moved[g] = source[g] + rate[g] * edged

    for copy in loads:
        copy.wait()
    prepare(slab, n_lb, params, mix_v, relax_v, push_v, u_v, sum_v, v_v, coef_v)
    own_v = ((u_v, u_s), (sum_v, sum_s), (v_v, v_s), (coef_v, coef_s), (params, own_s))
    tables = [pltpu.make_async_copy(a, b, table_sem.at[i]) for i, (a, b) in enumerate(own_v)]
    for copy in tables:
        copy.start()
    split = table[...].astype(jnp.bfloat16)
    weight[0] = split
    weight[1] = (table[...] - split.astype(jnp.float32)).astype(jnp.bfloat16)
    load_state(0).wait()
    derive(0, state, 0)
    pl.semaphore_wait(barrier, tiles - 1 + n_lb - 1)
    start_y(0, 0)

    def open_rest(f, c):
        load_state(f).wait()
        derive(f, state, 0)
        start_y(f, 0)
        spread(f - 1, 0)
        return c

    lax.fori_loop(1, chunks, open_rest, 0)
    spread(chunks - 1, 0)
    cls = classes[...]
    for x in range(8):
        mine = lax.broadcasted_iota(jnp.int32, (128, 1024), 0) + x * 128
        hot[x * 128 : (x + 1) * 128, :] = (
            (mine == span[...]).astype(jnp.float32).astype(jnp.bfloat16)
        )
    for copy in tables:
        copy.wait()

    def factor(l, previous):
        at = lb * slab + l
        high = own_s[0, at]
        low = own_s[2, at]
        inner_low = jnp.where(l == 0, 0.0, low)
        inner_high = jnp.where(l == slab - 1, 0.0, high)
        ratio = inner_low * previous
        inverse = 1.0 / (1.0 + own_s[1, at] + low + high - inner_low * ratio)
        carry[l] = ratio
        scale[l] = inverse
        link[l] = inner_high * inverse
        return inverse

    lax.fori_loop(0, slab, factor, jnp.zeros((8, 128), jnp.float32))

    def set_weight(l, c):
        at = lb * slab + l
        w = [u_s[k * 16 + 15, at] - 1.0 for k in range(1, 5)]
        weights[l] = jnp.where(
            cls == 0, w[0], jnp.where(cls == 1, w[1], jnp.where(cls == 2, w[2], w[3]))
        )
        return c

    lax.fori_loop(0, slab, set_weight, 0)
    def middle(f, c):
        advance(f, state, 0)
        derive(f, moved, 1)
        start_y(f, 1)

        @pl.when(f > 0)
        def _():
            spread(f - 1, 1)

        return c

    lax.fori_loop(0, chunks, middle, 0)
    spread(chunks - 1, 1)

    def pick(group, k, base):
        return coef_s[base + lb, group * SUBSTEPS + k]

    def convolve(group, base, k, value):
        out = pick(group, 0, base) * value[k]
        for i in range(1, k + 1):
            out = out + pick(group, i, base) * value[k - i]
        return out

    def scan_copy(f, down):
        if down:
            return pltpu.make_async_remote_copy(
                src_ref=p_out.at[chunk(f)], dst_ref=p_in.at[chunk(f)],
                send_sem=ps.at[f], recv_sem=pr.at[f],
                device_id=(ex, ey, lax.rem(lb + 1, n_lb)), device_id_type=MESH,
            )
        return pltpu.make_async_remote_copy(
            src_ref=q_out.at[chunk(f)], dst_ref=q_in.at[chunk(f)],
            send_sem=qs.at[f], recv_sem=qr.at[f],
            device_id=(ex, ey, lax.rem(lb + n_lb - 1, n_lb)), device_id_type=MESH,
        )

    def scan_step(f, down):
        arrives = lb > 0 if down else lb < n_lb - 1
        leaves = lb < n_lb - 1 if down else lb > 0
        inward, outward = (p_in, p_out) if down else (q_in, q_out)
        same, opposite = (p_loc, q_loc) if down else (q_loc, p_loc)
        base = 0 if down else 4

        @pl.when((f >= 0) & (f < chunks))
        def _():
            @pl.when(arrives)
            def _():
                scan_copy(f, down).wait_recv()
                own = [same[chunk(f), k] for k in range(SUBSTEPS)]
                facing = [opposite[chunk(f), k] for k in range(SUBSTEPS)]
                coming = [inward[chunk(f), k] for k in range(SUBSTEPS)]
                for k in range(SUBSTEPS):
                    outward[chunk(f), k] = (
                        own[k] + convolve(0, base, k, coming) + convolve(1, base, k, facing)
                    )

            @pl.when(jnp.logical_not(arrives))
            def _():
                for k in range(SUBSTEPS):
                    outward[chunk(f), k] = same[chunk(f), k]

            @pl.when(leaves)
            def _():
                scan_copy(f, down).start()

    def scan_steps(i):
        scan_step(i - lb * SKEW, True)
        scan_step(i - (n_lb - 1 - lb) * SKEW, False)

    def summarise(f):
        zero = jnp.zeros((size, 8, 128), jnp.float32)

        def level(l, c):
            x = moved[chunk(f), l]
            at = lb * slab + l
            out = [c[k] + v_s[k * 8 + lb, at] * x for k in range(4)]
            out += [c[4 + k] + v_s[k * 8 + 4 + lb, at] * x for k in range(4)]
            out.append(c[8] + weights[l][None] * x)
            return tuple(out)

        sums = lax.fori_loop(0, slab, level, (zero,) * 9, unroll=4)
        for k in range(SUBSTEPS):
            p_loc[chunk(f), k] = sums[k]
            q_loc[chunk(f), k] = sums[4 + k]
        for i in range(size):
            g = f * size + i
            h = [sum_s[g, k] * (1.0 / n_lb) for k in range(4)]
            extra = jnp.where(
                cls == 0, h[0], jnp.where(cls == 1, h[1], jnp.where(cls == 2, h[2], h[3]))
            )
            tend[pl.ds(pl.multiple_of(g * 8, 8), 8), :] = sums[8][i] + extra

    tend[fields * 8 : 128, :] = jnp.zeros((128 - fields * 8, 128), jnp.float32)

    def closing(i, c):
        advance(i, moved, 1)
        summarise(i)
        scan_steps(i)
        return c

    lax.fori_loop(0, chunks, closing, 0)

    def three(value):
        a = value.astype(jnp.bfloat16)
        rest = value - a.astype(jnp.float32)
        b = rest.astype(jnp.bfloat16)
        last = (rest - b.astype(jnp.float32)).astype(jnp.bfloat16)
        return jnp.concatenate([a, b, last], axis=0)

    def together(value):
        return value[:16] + value[16:32] + value[32:]

    span_slots = 1024 // n_lb
    gathered = jnp.zeros((48, 1024), jnp.float32)
    for x in range(0, 8, 2):
        pair = [three(tend[pl.ds(x + i, 16, stride=8), :]) for i in range(2)]
        gathered = gathered + jnp.dot(
            jnp.concatenate(pair, axis=1),
            hot[x * 128 : (x + 2) * 128, :],
            preferred_element_type=jnp.float32,
        )
    gathered = together(gathered)
    for g in range(n_lb):
        slots[g] = gathered[:, g * span_slots : (g + 1) * span_slots]

    def one_copy(o):
        return pltpu.make_async_remote_copy(
            src_ref=slots.at[lax.rem(lb + o, n_lb)], dst_ref=got_one.at[o - 1],
            send_sem=os.at[o - 1], recv_sem=o_r.at[o - 1],
            device_id=slab_peer(o), device_id_type=MESH,
        )

    def two_copy(o):
        return pltpu.make_async_remote_copy(
            src_ref=part, dst_ref=got_two.at[o - 1],
            send_sem=ts.at[o - 1], recv_sem=t_r.at[o - 1],
            device_id=tile_peer(o), device_id_type=MESH,
        )

    def three_copy(o):
        return pltpu.make_async_remote_copy(
            src_ref=full.at[lb], dst_ref=full.at[lb],
            send_sem=fs.at[o - 1], recv_sem=f_r.at[o - 1],
            device_id=slab_peer(o), device_id_type=MESH,
        )

    def three_arrival(o):
        other = lax.rem(lb + n_lb - o, n_lb)
        return pltpu.make_async_remote_copy(
            src_ref=full.at[other], dst_ref=full.at[other],
            send_sem=fs.at[o - 1], recv_sem=f_r.at[o - 1],
            device_id=slab_peer(o), device_id_type=MESH,
        )

    for o in range(1, n_lb):
        one_copy(o).start()

    @pl.when(lb == 0)
    def _():
        p_in[...] = jnp.zeros_like(p_in)

    @pl.when(lb == n_lb - 1)
    def _():
        q_in[...] = jnp.zeros_like(q_in)

    def sweep(start, group):
        at = slice(start, start + group)
        above = [p_in[at, k] for k in range(SUBSTEPS)]
        below = [q_in[at, k] for k in range(SUBSTEPS)]
        own_p = [p_out[at, k] for k in range(SUBSTEPS)]
        own_q = [q_out[at, k] for k in range(SUBSTEPS)]
        for k in range(SUBSTEPS):
            p_loc[at, k] = convolve(2, 0, k, above) + convolve(3, 0, k, own_q)
            q_loc[at, k] = convolve(2, 4, k, below) + convolve(3, 4, k, own_p)

        def push(f, l):
            h = [u_s[k * 16 + f, lb * slab + l] for k in range(4)]
            return jnp.where(
                cls == 0, h[0], jnp.where(cls == 1, h[1], jnp.where(cls == 2, h[2], h[3]))
            )

        def keep(k, l, y):
            if k > 0:
                y = jnp.where(cls >= k, y, moved[at, l])
            if k < SUBSTEPS - 1:
                moved[at, l] = y
            else:
                for f in range(group):
                    moved[start + f, l] = y[f] + push(start + f, l)

        for k in range(SUBSTEPS):

            def down(l, z):
                z = moved[at, l] + carry[l][None] * z
                swept[at, l] = z
                return z

            z = moved[at, 0] + p_loc[at, k]
            swept[at, 0] = z
            z = lax.fori_loop(1, slab, down, z, unroll=4)
            y = (z + q_loc[at, k]) * scale[slab - 1][None]
            keep(k, slab - 1, y)

            def up(i, y, k=k):
                l = slab - 1 - i
                y = swept[at, l] * scale[l][None] + link[l][None] * y
                keep(k, l, y)
                return y

            lax.fori_loop(1, slab, up, y, unroll=4 if k < SUBSTEPS - 1 else 2)

    def trailing(i, c):
        scan_steps(i)
        return c

    lax.fori_loop(chunks, chunks + 2, trailing, 0)
    total = slots[lb]
    for o in range(1, n_lb):
        one_copy(o).wait_recv()
        total = total + got_one[o - 1]
    part[...] = total

    def start_two(o, c):
        two_copy(o).start()
        return c

    lax.fori_loop(1, tiles, start_two, 0)
    last_step = chunks + (n_lb - 1) * SKEW
    if fields == 15 and n_lb == 4:
        lax.fori_loop(chunks + 2, chunks + 3, trailing, 0)
        sweep(0, 6)
        lax.fori_loop(chunks + 3, chunks + 4, trailing, 0)
        sweep(6, 3)
        lax.fori_loop(chunks + 4, last_step, trailing, 0)
        rest = (9, 6)
    else:
        lax.fori_loop(chunks + 2, last_step, trailing, 0)
        rest = (0, fields)
    def add_two(o, c):
        two_copy(o).wait_recv()
        return c + got_two[o - 1]

    total = lax.fori_loop(1, tiles, add_two, part[...])
    full[lb] = total * (1.0 / (tiles * slab * n_lb))
    for o in range(1, n_lb):
        three_copy(o).start()

    sweep(*rest)
    for o in range(1, n_lb):
        three_arrival(o).wait_recv()
    spread_share = jnp.zeros((48, 1024), jnp.float32)
    for g in range(n_lb):
        spread_share = spread_share + lax.dot_general(
            three(full[g]),
            hot[:, g * span_slots : (g + 1) * span_slots],
            (((1,), (1,)), ((), ())),
            preferred_element_type=jnp.float32,
        )
    spread_share = together(spread_share)
    for x in range(8):
        share[pl.ds(x, 16, stride=8), :] = spread_share[:, x * 128 : (x + 1) * 128]

    def store(f):
        return pltpu.make_async_copy(moved.at[f], out.at[f], state_sem.at[f])

    def settle(f, c):
        moved[f] = moved[f] - share[pl.ds(pl.multiple_of(f * 8, 8), 8), :][None]
        store(f).start()
        return c

    lax.fori_loop(0, fields, settle, 0)

    def drain_store(f, c):
        store(f).wait()
        return c

    lax.fori_loop(0, fields, drain_store, 0)

    def drain(f, c):
        for step in range(STEPS):
            for side in range(sides):
                y_copy(step, f, side).wait_send()
            for side in range(2):
                x_copy(step, f, side).wait_send()

        @pl.when(lb < n_lb - 1)
        def _():
            scan_copy(f, True).wait_send()

        @pl.when(lb > 0)
        def _():
            scan_copy(f, False).wait_send()

        return c

    lax.fori_loop(0, chunks, drain, 0)
    for o in range(1, n_lb):
        one_copy(o).wait_send()
        three_copy(o).wait_send()

    def drain_two(o, c):
        two_copy(o).wait_send()
        return c

    lax.fori_loop(1, tiles, drain_two, 0)


def local(atmosphere_state, diffusivity, mixing, relaxation, forcing, span_map, cost_class):
    fields, slab, width_x, width_y = atmosphere_state.shape
    n_ex, n_ey, n_lb = (lax.axis_size(a) for a in ("ex", "ey", "lb"))
    levels = slab * n_lb
    dims = (n_ex, n_ey, n_lb, fields, slab)
    rows = slab * 8
    tiles = n_ex * n_ey
    sides = 1 if n_ey == 2 else 2
    weight, shifts = operator_tables(width_x, width_y)
    hbm = pl.BlockSpec(memory_space=pltpu.HBM)
    f32 = jnp.float32
    dma = pltpu.SemaphoreType.DMA
    wide = 1024 // n_lb
    volume = (fields, slab, 8, 128)
    return pl.pallas_call(
        functools.partial(main_kernel, dims),
        out_shape=jax.ShapeDtypeStruct(volume, f32),
        in_specs=[hbm] * 9,
        out_specs=hbm,
        scratch_shapes=[
            pltpu.VMEM(volume, f32),
            pltpu.VMEM((8, 128), jnp.int32),
            pltpu.VMEM((1, 1024), jnp.int32),
            pltpu.VMEM((256, 256), f32),
            pltpu.VMEM((2, 256, 256), jnp.bfloat16),
            pltpu.VMEM((7, 8, 128), f32),
            pltpu.SMEM((fields,), f32),
            pltpu.VMEM((1, levels - 1), f32),
            pltpu.VMEM((1, levels), f32),
            pltpu.VMEM((fields, levels), f32),
            pltpu.VMEM((24, levels), f32),
            pltpu.VMEM((80, levels), f32),
            pltpu.VMEM((16, levels), f32),
            pltpu.VMEM((SUBSTEPS * 8, levels), f32),
            pltpu.VMEM((8, levels), f32),
            pltpu.SMEM((80, levels), f32),
            pltpu.SMEM((16, levels), f32),
            pltpu.SMEM((SUBSTEPS * 8, levels), f32),
            pltpu.SMEM((8, levels), f32),
            pltpu.SMEM((24, levels), f32),
            pltpu.VMEM(volume, f32),
            pltpu.VMEM(volume, f32),
            pltpu.VMEM((slab, 8, 128), f32),
            pltpu.VMEM((slab, 8, 128), f32),
            pltpu.VMEM((slab, 8, 128), f32),
            pltpu.VMEM((128, 128), f32),
            pltpu.VMEM((fields, rows, 128), f32),
            pltpu.VMEM((STEPS, fields, rows, 128), f32),
            pltpu.VMEM((STEPS, sides, fields, rows, 128), f32),
            pltpu.VMEM((STEPS, 2, fields, slab, 128), f32),
            pltpu.VMEM((STEPS, 2, fields, slab, 128), f32),
            pltpu.VMEM((slab, 8, 128), f32),
        ]
        + [pltpu.VMEM((fields, SUBSTEPS, 8, 128), f32)] * 6
        + [
            pltpu.VMEM((128, 128), f32),
            pltpu.VMEM((1024, 1024), jnp.bfloat16),
            pltpu.VMEM((n_lb, 16, wide), f32),
            pltpu.VMEM((n_lb - 1, 16, wide), f32),
            pltpu.VMEM((16, wide), f32),
            pltpu.VMEM((tiles - 1, 16, wide), f32),
            pltpu.VMEM((n_lb, 16, wide), f32),
            dma((fields,)),
            dma((8,)),
            dma((5,)),
            dma((STEPS, sides, fields)),
            dma((STEPS, sides, fields)),
            dma((STEPS, 2, fields)),
            dma((STEPS, 2, fields)),
            dma((fields,)),
            dma((fields,)),
            dma((fields,)),
            dma((fields,)),
            dma((n_lb - 1,)),
            dma((n_lb - 1,)),
            dma((tiles - 1,)),
            dma((tiles - 1,)),
            dma((n_lb - 1,)),
            dma((n_lb - 1,)),
        ],
        compiler_params=pltpu.CompilerParams(
            collective_id=0, has_side_effects=True, vmem_limit_bytes=VMEM_MIB * 1024 * 1024
        ),
    )(
        atmosphere_state, cost_class, span_map.reshape(1, width_x * width_y),
        jnp.asarray(weight), jnp.asarray(shifts), diffusivity,
        mixing.reshape(1, levels - 1), relaxation.reshape(1, levels), forcing,
    )


def solution(mesh):
    return jax.shard_map(
        local,
        mesh=mesh,
        in_specs=(
            P(None, "lb", "ex", "ey"),
            P(),
            P(),
            P(),
            P(),
            P("ex", "ey", None),
            P("ex", "ey"),
        ),
        out_specs=P(None, "lb", "ex", "ey"),
        check_vma=False,
    )
```

```python
import functools
import math

import jax
import jax.numpy as jnp
import numpy as np
from jax import lax
from jax.experimental import pallas as pl
from jax.experimental.pallas import tpu as pltpu
from jax.sharding import PartitionSpec as P

STEPS = 2
SUBSTEPS = 4
MESH = pl.DeviceIdType.MESH
SKEW = 1
VMEM_MIB = 63


def second_table():
    inner_root = 1.0 / math.sqrt(5.0)
    gll_nodes = np.array([-1.0, -inner_root, inner_root, 1.0])
    weights = np.array(
        [
            np.prod(
                [gll_nodes[target] - gll_nodes[source] for source in range(4) if source != target]
            )
            for target in range(4)
        ]
    )
    first_table = np.zeros((4, 4))
    for target in range(4):
        for source in range(4):
            if source != target:
                first_table[target, source] = weights[target] / (
                    weights[source] * (gll_nodes[target] - gll_nodes[source])
                )
    for target in range(4):
        first_table[target, target] = -first_table[target].sum()
    return (first_table @ first_table).astype(np.float32)


def operator_tables(width_x, width_y):
    second = second_table()
    along = np.kron(np.eye(width_y // 4), second.T).astype(np.float64)
    edge = np.zeros((width_y, width_y))
    for y in range(width_y):
        if y % 4 == 3:
            edge[y, y] = 0.5
            if y + 1 < width_y:
                edge[y + 1, y] = 0.5
        elif y % 4 == 0:
            edge[y, y] = 0.5
            if y > 0:
                edge[y - 1, y] = 0.5
        else:
            edge[y, y] = 1.0
    rim = np.zeros((width_y, width_y))
    rim[0, width_y - 1] = 0.5
    rim[width_y - 1, 0] = 0.5
    both = np.concatenate([edge, rim], axis=1)
    weight = np.concatenate([along @ both, both], axis=0).astype(np.float32)
    shifts = np.zeros((7, width_x, width_y), np.float32)
    for x in range(width_x):
        for d in range(-3, 4):
            if 0 <= x % 4 + d < 4:
                shifts[d + 3, x, :] = second[x % 4, x % 4 + d]
    return weight, shifts


def series_mul(u, v):
    return [sum(u[i] * v[k - i] for i in range(k + 1)) for k in range(len(u))]


def series_inverse(u):
    first = 1.0 / u[0]
    out = [first]
    for k in range(1, len(u)):
        out.append(-first * sum(u[i] * out[k - i] for i in range(1, k + 1)))
    return out


def prepare(slab, count, params, mix_in, relax_in, push_in, u_out, sum_out, v_out, coef_out):
    levels = relax_in.shape[1]
    fields = push_in.shape[0]
    shape = (8, levels)
    params[...] = jnp.zeros_like(params)
    params[0:1, 0 : levels - 1] = mix_in[...]
    params[8 : 8 + fields, :] = push_in[...]
    params[23:24, :] = jnp.ones((1, levels), jnp.float32)
    hi = jnp.broadcast_to(params[0:1, :], shape)
    lo = pltpu.roll(hi, 1, 1)
    rel = jnp.broadcast_to(relax_in[...], shape)
    params[1:2, :] = relax_in[...]
    params[2:3, :] = lo[0:1, :]
    lane = lax.broadcasted_iota(jnp.int32, shape, 1)
    row = lax.broadcasted_iota(jnp.int32, shape, 0)
    diag = 1.0 + rel + lo + hi

    def back(x, s):
        return pltpu.roll(x, s, 1)

    def ahead(x, s):
        return pltpu.roll(x, levels - s, 1)

    def reduce_system(a, b, c, extent):
        stages = []
        s = 1
        while s < extent:
            alpha = -a / back(b, s)
            gamma = -c / ahead(b, s)
            b = b + alpha * back(c, s) + gamma * ahead(a, s)
            a = alpha * back(a, s)
            c = gamma * ahead(c, s)
            stages.append((s, alpha, gamma))
            s *= 2
        return stages, 1.0 / b

    def solve(system, d):
        stages, inverse = system
        for s, alpha, gamma in stages:
            d = d + alpha * back(d, s) + gamma * ahead(d, s)
        return d * inverse

    whole = reduce_system(-lo, diag, -hi, levels)
    cut = reduce_system(
        jnp.where(lane % slab == 0, 0.0, -lo),
        diag,
        jnp.where(lane % slab == slab - 1, 0.0, -hi),
        slab,
    )
    push = [params[8:16, :], jnp.where(row == 7, 0.0, params[16:24, :])]
    held = [params[8:16, :], params[16:24, :]]
    sums = [jnp.zeros(shape, jnp.float32)] * 2
    for k in range(SUBSTEPS + 1):
        for h in range(2):
            u_out[k * 16 + h * 8 : k * 16 + h * 8 + 8, :] = held[h]
            sums[h] = jnp.where(lane == k, jnp.sum(held[h], axis=1, keepdims=True), sums[h])
        if k < SUBSTEPS:
            held = [solve(whole, held[h]) + push[h] for h in range(2)]

    sum_out[0:8, :] = sums[0]
    sum_out[8:16, :] = sums[1]
    spot = jnp.where(row < 4, row * slab + slab - 1, (row - 4) * slab)
    tips = jnp.where((lane == spot) & (row % 4 < count), 1.0, 0.0)
    other = pltpu.roll(tips, 4, 0)

    def total(x):
        return jnp.broadcast_to(jnp.sum(x, axis=1, keepdims=True), shape)

    mix = total(jnp.where(row < 4, lo, hi) * other)
    near, far = [], []
    v = tips
    for k in range(SUBSTEPS):
        v = solve(cut, v)
        v_out[k * 8 : k * 8 + 8, :] = v
        near.append(total(v * tips))
        far.append(total(v * other))
    facing = [pltpu.roll(x, 4, 0) for x in near]
    square = mix * mix
    far_far = series_mul(far, far)

    def beside(z):
        return [jnp.where(row < 4, pltpu.roll(x, 1, 0), pltpu.roll(x, 7, 0)) for x in z]

    def gain(u, v):
        product = series_mul(u, v)
        return series_inverse(
            [(1.0 if k == 0 else 0.0) - square * x for k, x in enumerate(product)]
        )

    z = near
    for _ in range(count - 1):
        zn = beside(z)
        change = series_mul(series_mul(far_far, zn), gain(zn, facing))
        z = [x + square * y for x, y in zip(near, change)]
    zn = beside(z)
    first = [mix * x for x in series_mul(far, gain(zn, facing))]
    next_ = [mix * x for x in series_mul(first, zn)]
    edge = gain(zn, [pltpu.roll(x, 4, 0) for x in z])
    edge_one = [mix * x for x in edge]
    edge_two = [mix * x for x in series_mul(edge_one, zn)]
    packed = jnp.zeros(shape, jnp.float32)
    for g, part in enumerate((first, next_, edge_one, edge_two)):
        for k in range(SUBSTEPS):
            packed = jnp.where(lane == g * SUBSTEPS + k, part[k], packed)
    coef_out[...] = packed


def main_kernel(
    dims,
    state_h, classes_h, span_h, w_h, shifts_h, rate_h, mix_h, relax_h, push_h,
    out, share,
    state, classes, span, table, weight, shifts, rate, mix_v, relax_v, push_v,
    params, u_v, sum_v, v_v, coef_v, u_s, sum_s, v_s, coef_s, own_s,
    moved, swept, carry, scale, link,
    lap, hy_out, hy_in, x_out, x_in, weights, p_loc, q_loc, p_out, p_in, q_out, q_in,
    tend, hot, slots, got_one, part, got_two, full,
    state_sem, in_sem, table_sem,
    ys, yr, xs, xr, ps, pr, qs, qr, os, o_r, ts, t_r, fs, f_r,
):
    n_ex, n_ey, n_lb, fields, slab = dims
    rows = slab * 8
    tiles = n_ex * n_ey
    ex, ey, lb = lax.axis_index("ex"), lax.axis_index("ey"), lax.axis_index("lb")
    tile = ex * n_ey + ey
    sides = 1 if n_ey == 2 else 2
    size = 3 if fields % 3 == 0 else 1
    chunks = fields // size

    def tile_peer(o):
        t = lax.rem(tile + o, tiles)
        return (t // n_ey, lax.rem(t, n_ey), lb)

    def slab_peer(o):
        return (ex, ey, lax.rem(lb + o, n_lb))

    barrier = pltpu.get_barrier_semaphore()

    def greet_tiles(o, c):
        pl.semaphore_signal(barrier, inc=1, device_id=tile_peer(o), device_id_type=MESH)
        return c

    def greet_slabs(o, c):
        pl.semaphore_signal(barrier, inc=1, device_id=slab_peer(o), device_id_type=MESH)
        return c

    loads = [
        pltpu.make_async_copy(a, b, in_sem.at[i])
        for i, (a, b) in enumerate(
            (
                (shifts_h, shifts), (w_h, table), (classes_h, classes), (span_h, span),
                (rate_h, rate), (mix_h, mix_v), (relax_h, relax_v), (push_h, push_v),
            )
        )
    ]

    def chunk(f):
        return pl.ds(f * size, size)

    def load_state(f):
        return pltpu.make_async_copy(state_h.at[chunk(f)], state.at[chunk(f)], state_sem.at[f])

    def fetch(f, c):
        load_state(f).start()
        return c

    for copy in loads:
        copy.start()
    lax.fori_loop(0, chunks, fetch, 0)
    lax.fori_loop(1, tiles, greet_tiles, 0)
    lax.fori_loop(1, n_lb, greet_slabs, 0)

    row_x = lax.broadcasted_iota(jnp.int32, (8, 128), 0)
    lane = lax.broadcasted_iota(jnp.int32, (8, 128), 1)
    def derive(f, source, step):
        s = source[chunk(f)].reshape(size * slab, 8, 128)
        along = shifts[3][None] * s
        for d in (-3, -2, -1, 1, 2, 3):
            along = along + shifts[d + 3][None] * pltpu.roll(s, (8 - d) % 8, 1)
        both = jnp.concatenate(
            [s.reshape(size * rows, 128), along.reshape(size * rows, 128)], axis=1
        )
        high = both.astype(jnp.bfloat16)
        low = (both - high.astype(jnp.float32)).astype(jnp.bfloat16)
        result = (
            jnp.dot(high, weight[0], preferred_element_type=jnp.float32)
            + jnp.dot(low, weight[0], preferred_element_type=jnp.float32)
            + jnp.dot(high, weight[1], preferred_element_type=jnp.float32)
        )
        lap[chunk(f)] = result[:, :128].reshape(size, rows, 128)
        hy_out[step, chunk(f)] = result[:, 128:].reshape(size, rows, 128)

    def y_copy(step, f, side):
        peer = lax.rem(ey + (1 if side == 0 else n_ey - 1), n_ey)
        return pltpu.make_async_remote_copy(
            src_ref=hy_out.at[step, chunk(f)],
            dst_ref=hy_in.at[step, side, chunk(f)],
            send_sem=ys.at[step, side, f],
            recv_sem=yr.at[step, side, f],
            device_id=(ex, peer, lb),
            device_id_type=MESH,
        )

    def x_copy(step, f, side):
        peer = lax.rem(ex + (1 if side == 0 else n_ex - 1), n_ex)
        return pltpu.make_async_remote_copy(
            src_ref=x_out.at[step, side, chunk(f)],
            dst_ref=x_in.at[step, side, chunk(f)],
            send_sem=xs.at[step, side, f],
            recv_sem=xr.at[step, side, f],
            device_id=(peer, ey, lb),
            device_id_type=MESH,
        )

    def start_y(f, step):
        for side in range(sides):
            y_copy(step, f, side).start()

    def spread(f, step):
        for side in range(sides):
            y_copy(step, f, side).wait_recv()
        shape = (size * slab, 8, 128)
        value = lap[chunk(f)].reshape(shape)
        if sides == 1:
            value = value + hy_in[step, 0, chunk(f)].reshape(shape)
        else:
            value = value + jnp.where(lane == 0, hy_in[step, 0, chunk(f)].reshape(shape), 0.0)
            value = value + jnp.where(lane == 127, hy_in[step, 1, chunk(f)].reshape(shape), 0.0)
        lap[chunk(f)] = value.reshape(size, rows, 128)
        for i in range(size):
            x_out[step, 0, f * size + i] = lap[f * size + i, pl.ds(7, slab, stride=8), :]
            x_out[step, 1, f * size + i] = lap[f * size + i, pl.ds(0, slab, stride=8), :]
        x_copy(step, f, 0).start()
        x_copy(step, f, 1).start()

    def advance(f, source, step):
        x_copy(step, f, 0).wait_recv()
        x_copy(step, f, 1).wait_recv()
        joins = (row_x == 0) | (row_x == 3) | (row_x == 4) | (row_x == 7)
        for i in range(size):
            g = f * size + i
            value = lap[g].reshape(slab, 8, 128)
            before = pltpu.roll(value, 1, 1)
            after = pltpu.roll(value, 7, 1)
            first = jnp.broadcast_to(x_in[step, 0, g][:, None, :], (slab, 8, 128))
            last = jnp.broadcast_to(x_in[step, 1, g][:, None, :], (slab, 8, 128))
            partner = jnp.where(
                row_x == 0,
                first,
                jnp.where(row_x == 7, last, jnp.where(row_x == 3, after, before)),
            )
            edged = jnp.where(joins, 0.5 * (value + partner), value)
            moved[g] = source[g] + rate[g] * edged

    for copy in loads[:2]:
        copy.wait()
    split = table[...].astype(jnp.bfloat16)
    weight[0] = split
    weight[1] = (table[...] - split.astype(jnp.float32)).astype(jnp.bfloat16)
    load_state(0).wait()
    derive(0, state, 0)
    pl.semaphore_wait(barrier, tiles - 1 + n_lb - 1)
    start_y(0, 0)

    def open_rest(f, c):
        load_state(f).wait()
        derive(f, state, 0)
        start_y(f, 0)
        spread(f - 1, 0)
        return c

    lax.fori_loop(1, chunks, open_rest, 0)
    spread(chunks - 1, 0)
    for copy in loads[2:]:
        copy.wait()
    prepare(slab, n_lb, params, mix_v, relax_v, push_v, u_v, sum_v, v_v, coef_v)
    own_v = ((u_v, u_s), (sum_v, sum_s), (v_v, v_s), (coef_v, coef_s), (params, own_s))
    tables = [pltpu.make_async_copy(a, b, table_sem.at[i]) for i, (a, b) in enumerate(own_v)]
    for copy in tables:
        copy.start()
    cls = classes[...]
    for x in range(8):
        mine = lax.broadcasted_iota(jnp.int32, (128, 1024), 0) + x * 128
        hot[x * 128 : (x + 1) * 128, :] = (
            (mine == span[...]).astype(jnp.float32).astype(jnp.bfloat16)
        )
    for copy in tables:
        copy.wait()

    def factor(l, previous):
        at = lb * slab + l
        high = own_s[0, at]
        low = own_s[2, at]
        inner_low = jnp.where(l == 0, 0.0, low)
        inner_high = jnp.where(l == slab - 1, 0.0, high)
        ratio = inner_low * previous
        inverse = 1.0 / (1.0 + own_s[1, at] + low + high - inner_low * ratio)
        carry[l] = ratio
        scale[l] = inverse
        link[l] = inner_high * inverse
        return inverse

    lax.fori_loop(0, slab, factor, jnp.zeros((8, 128), jnp.float32))

    def set_weight(l, c):
        at = lb * slab + l
        w = [u_s[k * 16 + 15, at] - 1.0 for k in range(1, 5)]
        weights[l] = jnp.where(
            cls == 0, w[0], jnp.where(cls == 1, w[1], jnp.where(cls == 2, w[2], w[3]))
        )
        return c

    lax.fori_loop(0, slab, set_weight, 0)
    def middle(f, c):
        advance(f, state, 0)
        derive(f, moved, 1)
        start_y(f, 1)

        @pl.when(f > 0)
        def _():
            spread(f - 1, 1)

        return c

    lax.fori_loop(0, chunks, middle, 0)
    spread(chunks - 1, 1)

    def pick(group, k, base):
        return coef_s[base + lb, group * SUBSTEPS + k]

    def convolve(group, base, k, value):
        out = pick(group, 0, base) * value[k]
        for i in range(1, k + 1):
            out = out + pick(group, i, base) * value[k - i]
        return out

    def scan_copy(f, down):
        if down:
            return pltpu.make_async_remote_copy(
                src_ref=p_out.at[chunk(f)], dst_ref=p_in.at[chunk(f)],
                send_sem=ps.at[f], recv_sem=pr.at[f],
                device_id=(ex, ey, lax.rem(lb + 1, n_lb)), device_id_type=MESH,
            )
        return pltpu.make_async_remote_copy(
            src_ref=q_out.at[chunk(f)], dst_ref=q_in.at[chunk(f)],
            send_sem=qs.at[f], recv_sem=qr.at[f],
            device_id=(ex, ey, lax.rem(lb + n_lb - 1, n_lb)), device_id_type=MESH,
        )

    def scan_step(f, down):
        arrives = lb > 0 if down else lb < n_lb - 1
        leaves = lb < n_lb - 1 if down else lb > 0
        inward, outward = (p_in, p_out) if down else (q_in, q_out)
        same, opposite = (p_loc, q_loc) if down else (q_loc, p_loc)
        base = 0 if down else 4

        @pl.when((f >= 0) & (f < chunks))
        def _():
            @pl.when(arrives)
            def _():
                scan_copy(f, down).wait_recv()
                own = [same[chunk(f), k] for k in range(SUBSTEPS)]
                facing = [opposite[chunk(f), k] for k in range(SUBSTEPS)]
                coming = [inward[chunk(f), k] for k in range(SUBSTEPS)]
                for k in range(SUBSTEPS):
                    outward[chunk(f), k] = (
                        own[k] + convolve(0, base, k, coming) + convolve(1, base, k, facing)
                    )

            @pl.when(jnp.logical_not(arrives))
            def _():
                for k in range(SUBSTEPS):
                    outward[chunk(f), k] = same[chunk(f), k]

            @pl.when(leaves)
            def _():
                scan_copy(f, down).start()

    def scan_steps(i):
        scan_step(i - lb * SKEW, True)
        scan_step(i - (n_lb - 1 - lb) * SKEW, False)

    def summarise(f):
        zero = jnp.zeros((size, 8, 128), jnp.float32)

        def level(l, c):
            x = moved[chunk(f), l]
            at = lb * slab + l
            out = [c[k] + v_s[k * 8 + lb, at] * x for k in range(4)]
            out += [c[4 + k] + v_s[k * 8 + 4 + lb, at] * x for k in range(4)]
            out.append(c[8] + weights[l][None] * x)
            return tuple(out)

        sums = lax.fori_loop(0, slab, level, (zero,) * 9, unroll=4)
        for k in range(SUBSTEPS):
            p_loc[chunk(f), k] = sums[k]
            q_loc[chunk(f), k] = sums[4 + k]
        for i in range(size):
            g = f * size + i
            h = [sum_s[g, k] * (1.0 / n_lb) for k in range(4)]
            extra = jnp.where(
                cls == 0, h[0], jnp.where(cls == 1, h[1], jnp.where(cls == 2, h[2], h[3]))
            )
            tend[pl.ds(pl.multiple_of(g * 8, 8), 8), :] = sums[8][i] + extra

    tend[fields * 8 : 128, :] = jnp.zeros((128 - fields * 8, 128), jnp.float32)

    @pl.when(lb == 0)
    def _():
        p_in[...] = jnp.zeros_like(p_in)

    @pl.when(lb == n_lb - 1)
    def _():
        q_in[...] = jnp.zeros_like(q_in)

    def store(f):
        return pltpu.make_async_copy(
            moved.at[chunk(f)], out.at[chunk(f)], state_sem.at[f]
        )

    def sweep(g):
        group = size
        start = g * size
        at = chunk(g)
        above = [p_in[at, k] for k in range(SUBSTEPS)]
        below = [q_in[at, k] for k in range(SUBSTEPS)]
        own_p = [p_out[at, k] for k in range(SUBSTEPS)]
        own_q = [q_out[at, k] for k in range(SUBSTEPS)]
        for k in range(SUBSTEPS):
            p_loc[at, k] = convolve(2, 0, k, above) + convolve(3, 0, k, own_q)
            q_loc[at, k] = convolve(2, 4, k, below) + convolve(3, 4, k, own_p)

        def push(f, l):
            h = [u_s[k * 16 + f, lb * slab + l] for k in range(4)]
            return jnp.where(
                cls == 0, h[0], jnp.where(cls == 1, h[1], jnp.where(cls == 2, h[2], h[3]))
            )

        def keep(k, l, y):
            if k > 0:
                y = jnp.where(cls >= k, y, moved[at, l])
            if k < SUBSTEPS - 1:
                moved[at, l] = y
            else:
                for f in range(group):
                    moved[start + f, l] = y[f] + push(start + f, l)

        for k in range(SUBSTEPS):

            def down(l, z):
                z = moved[at, l] + carry[l][None] * z
                swept[at, l] = z
                return z

            z = moved[at, 0] + p_loc[at, k]
            swept[at, 0] = z
            z = lax.fori_loop(1, slab, down, z, unroll=4)
            y = (z + q_loc[at, k]) * scale[slab - 1][None]
            keep(k, slab - 1, y)

            def up(i, y, k=k):
                l = slab - 1 - i
                y = swept[at, l] * scale[l][None] + link[l][None] * y
                keep(k, l, y)
                return y

            lax.fori_loop(1, slab, up, y, unroll=4 if k < SUBSTEPS - 1 else 2)
        store(g).start()

    def closing(i, c):
        advance(i, moved, 1)
        summarise(i)
        scan_steps(i)
        return c

    hops = (n_lb - 1) * SKEW

    def closing_sweep(i, c):
        closing(i, c)
        sweep(i - hops)
        return c

    lax.fori_loop(0, hops, closing, 0)
    lax.fori_loop(hops, chunks, closing_sweep, 0)

    def three(value):
        a = value.astype(jnp.bfloat16)
        rest = value - a.astype(jnp.float32)
        b = rest.astype(jnp.bfloat16)
        last = (rest - b.astype(jnp.float32)).astype(jnp.bfloat16)
        return jnp.concatenate([a, b, last], axis=0)

    def together(value):
        return value[:16] + value[16:32] + value[32:]

    span_slots = 1024 // n_lb
    gathered = jnp.zeros((48, 1024), jnp.float32)
    for x in range(0, 8, 2):
        pair = [three(tend[pl.ds(x + i, 16, stride=8), :]) for i in range(2)]
        gathered = gathered + jnp.dot(
            jnp.concatenate(pair, axis=1),
            hot[x * 128 : (x + 2) * 128, :],
            preferred_element_type=jnp.float32,
        )
    gathered = together(gathered)
    for g in range(n_lb):
        slots[g] = gathered[:, g * span_slots : (g + 1) * span_slots]

    def one_copy(o):
        return pltpu.make_async_remote_copy(
            src_ref=slots.at[lax.rem(lb + o, n_lb)], dst_ref=got_one.at[o - 1],
            send_sem=os.at[o - 1], recv_sem=o_r.at[o - 1],
            device_id=slab_peer(o), device_id_type=MESH,
        )

    def two_copy(o):
        return pltpu.make_async_remote_copy(
            src_ref=part, dst_ref=got_two.at[o - 1],
            send_sem=ts.at[o - 1], recv_sem=t_r.at[o - 1],
            device_id=tile_peer(o), device_id_type=MESH,
        )

    def three_copy(o):
        return pltpu.make_async_remote_copy(
            src_ref=full.at[lb], dst_ref=full.at[lb],
            send_sem=fs.at[o - 1], recv_sem=f_r.at[o - 1],
            device_id=slab_peer(o), device_id_type=MESH,
        )

    def three_arrival(o):
        other = lax.rem(lb + n_lb - o, n_lb)
        return pltpu.make_async_remote_copy(
            src_ref=full.at[other], dst_ref=full.at[other],
            send_sem=fs.at[o - 1], recv_sem=f_r.at[o - 1],
            device_id=slab_peer(o), device_id_type=MESH,
        )

    for o in range(1, n_lb):
        one_copy(o).start()

    def trailing(i, c):
        scan_steps(i)
        sweep(i - hops)
        return c

    lax.fori_loop(chunks, chunks + 1, trailing, 0)
    total = slots[lb]
    for o in range(1, n_lb):
        one_copy(o).wait_recv()
        total = total + got_one[o - 1]
    part[...] = total

    def start_two(o, c):
        two_copy(o).start()
        return c

    lax.fori_loop(1, tiles, start_two, 0)
    lax.fori_loop(chunks + 1, chunks + 2, trailing, 0)

    def add_two(o, c):
        two_copy(o).wait_recv()
        return c + got_two[o - 1]

    total = lax.fori_loop(1, tiles, add_two, part[...])
    full[lb] = total * (1.0 / (tiles * slab * n_lb))
    for o in range(1, n_lb):
        three_copy(o).start()

    lax.fori_loop(chunks + 2, chunks + hops, trailing, 0)
    for o in range(1, n_lb):
        three_arrival(o).wait_recv()
    spread_share = jnp.zeros((48, 1024), jnp.float32)
    for g in range(n_lb):
        spread_share = spread_share + lax.dot_general(
            three(full[g]),
            hot[:, g * span_slots : (g + 1) * span_slots],
            (((1,), (1,)), ((), ())),
            preferred_element_type=jnp.float32,
        )
    spread_share = together(spread_share)
    for x in range(8):
        share[pl.ds(x, fields, stride=8), :] = spread_share[:fields, x * 128 : (x + 1) * 128]

    def drain_store(f, c):
        store(f).wait()
        return c

    lax.fori_loop(0, chunks, drain_store, 0)

    def drain(f, c):
        for step in range(STEPS):
            for side in range(sides):
                y_copy(step, f, side).wait_send()
            for side in range(2):
                x_copy(step, f, side).wait_send()

        @pl.when(lb < n_lb - 1)
        def _():
            scan_copy(f, True).wait_send()

        @pl.when(lb > 0)
        def _():
            scan_copy(f, False).wait_send()

        return c

    lax.fori_loop(0, chunks, drain, 0)
    for o in range(1, n_lb):
        one_copy(o).wait_send()
        three_copy(o).wait_send()

    def drain_two(o, c):
        two_copy(o).wait_send()
        return c

    lax.fori_loop(1, tiles, drain_two, 0)


def local(atmosphere_state, diffusivity, mixing, relaxation, forcing, span_map, cost_class):
    fields, slab, width_x, width_y = atmosphere_state.shape
    n_ex, n_ey, n_lb = (lax.axis_size(a) for a in ("ex", "ey", "lb"))
    levels = slab * n_lb
    dims = (n_ex, n_ey, n_lb, fields, slab)
    rows = slab * 8
    tiles = n_ex * n_ey
    sides = 1 if n_ey == 2 else 2
    weight, shifts = operator_tables(width_x, width_y)
    hbm = pl.BlockSpec(memory_space=pltpu.HBM)
    f32 = jnp.float32
    dma = pltpu.SemaphoreType.DMA
    wide = 1024 // n_lb
    volume = (fields, slab, 8, 128)
    physics, share = pl.pallas_call(
        functools.partial(main_kernel, dims),
        out_shape=[
            jax.ShapeDtypeStruct(volume, f32),
            jax.ShapeDtypeStruct((fields * 8, 128), f32),
        ],
        in_specs=[hbm] * 9,
        out_specs=[hbm, pl.BlockSpec(memory_space=pltpu.VMEM)],
        scratch_shapes=[
            pltpu.VMEM(volume, f32),
            pltpu.VMEM((8, 128), jnp.int32),
            pltpu.VMEM((1, 1024), jnp.int32),
            pltpu.VMEM((256, 256), f32),
            pltpu.VMEM((2, 256, 256), jnp.bfloat16),
            pltpu.VMEM((7, 8, 128), f32),
            pltpu.SMEM((fields,), f32),
            pltpu.VMEM((1, levels - 1), f32),
            pltpu.VMEM((1, levels), f32),
            pltpu.VMEM((fields, levels), f32),
            pltpu.VMEM((24, levels), f32),
            pltpu.VMEM((80, levels), f32),
            pltpu.VMEM((16, levels), f32),
            pltpu.VMEM((SUBSTEPS * 8, levels), f32),
            pltpu.VMEM((8, levels), f32),
            pltpu.SMEM((80, levels), f32),
            pltpu.SMEM((16, levels), f32),
            pltpu.SMEM((SUBSTEPS * 8, levels), f32),
            pltpu.SMEM((8, levels), f32),
            pltpu.SMEM((24, levels), f32),
            pltpu.VMEM(volume, f32),
            pltpu.VMEM(volume, f32),
            pltpu.VMEM((slab, 8, 128), f32),
            pltpu.VMEM((slab, 8, 128), f32),
            pltpu.VMEM((slab, 8, 128), f32),
            pltpu.VMEM((fields, rows, 128), f32),
            pltpu.VMEM((STEPS, fields, rows, 128), f32),
            pltpu.VMEM((STEPS, sides, fields, rows, 128), f32),
            pltpu.VMEM((STEPS, 2, fields, slab, 128), f32),
            pltpu.VMEM((STEPS, 2, fields, slab, 128), f32),
            pltpu.VMEM((slab, 8, 128), f32),
        ]
        + [pltpu.VMEM((fields, SUBSTEPS, 8, 128), f32)] * 6
        + [
            pltpu.VMEM((128, 128), f32),
            pltpu.VMEM((1024, 1024), jnp.bfloat16),
            pltpu.VMEM((n_lb, 16, wide), f32),
            pltpu.VMEM((n_lb - 1, 16, wide), f32),
            pltpu.VMEM((16, wide), f32),
            pltpu.VMEM((tiles - 1, 16, wide), f32),
            pltpu.VMEM((n_lb, 16, wide), f32),
            dma((fields,)),
            dma((8,)),
            dma((5,)),
            dma((STEPS, sides, fields)),
            dma((STEPS, sides, fields)),
            dma((STEPS, 2, fields)),
            dma((STEPS, 2, fields)),
            dma((fields,)),
            dma((fields,)),
            dma((fields,)),
            dma((fields,)),
            dma((n_lb - 1,)),
            dma((n_lb - 1,)),
            dma((tiles - 1,)),
            dma((tiles - 1,)),
            dma((n_lb - 1,)),
            dma((n_lb - 1,)),
        ],
        compiler_params=pltpu.CompilerParams(
            collective_id=0, has_side_effects=True, vmem_limit_bytes=VMEM_MIB * 1024 * 1024
        ),
    )(
        atmosphere_state, cost_class, span_map.reshape(1, width_x * width_y),
        jnp.asarray(weight), jnp.asarray(shifts), diffusivity,
        mixing.reshape(1, levels - 1), relaxation.reshape(1, levels), forcing,
    )
    return physics - share.reshape(fields, 1, 8, 128)


def solution(mesh):
    return jax.shard_map(
        local,
        mesh=mesh,
        in_specs=(
            P(None, "lb", "ex", "ey"),
            P(),
            P(),
            P(),
            P(),
            P("ex", "ey", None),
            P("ex", "ey"),
        ),
        out_specs=P(None, "lb", "ex", "ey"),
        check_vma=False,
    )
```

```python
import functools
import math

import jax
import jax.numpy as jnp
import numpy as np
from jax import lax
from jax.experimental import pallas as pl
from jax.experimental.pallas import tpu as pltpu
from jax.sharding import PartitionSpec as P

STEPS = 2
SUBSTEPS = 4
MESH = pl.DeviceIdType.MESH
SKEW = 1
VMEM_MIB = 63


def second_table():
    inner_root = 1.0 / math.sqrt(5.0)
    gll_nodes = np.array([-1.0, -inner_root, inner_root, 1.0])
    weights = np.array(
        [
            np.prod(
                [gll_nodes[target] - gll_nodes[source] for source in range(4) if source != target]
            )
            for target in range(4)
        ]
    )
    first_table = np.zeros((4, 4))
    for target in range(4):
        for source in range(4):
            if source != target:
                first_table[target, source] = weights[target] / (
                    weights[source] * (gll_nodes[target] - gll_nodes[source])
                )
    for target in range(4):
        first_table[target, target] = -first_table[target].sum()
    return (first_table @ first_table).astype(np.float32)


def operator_tables(width_x, width_y):
    second = second_table()
    along = np.kron(np.eye(width_y // 4), second.T).astype(np.float64)
    edge = np.zeros((width_y, width_y))
    for y in range(width_y):
        if y % 4 == 3:
            edge[y, y] = 0.5
            if y + 1 < width_y:
                edge[y + 1, y] = 0.5
        elif y % 4 == 0:
            edge[y, y] = 0.5
            if y > 0:
                edge[y - 1, y] = 0.5
        else:
            edge[y, y] = 1.0
    rim = np.zeros((width_y, width_y))
    rim[0, width_y - 1] = 0.5
    rim[width_y - 1, 0] = 0.5
    both = np.concatenate([edge, rim], axis=1)
    weight = np.concatenate([along @ both, both], axis=0).astype(np.float32)
    shifts = np.zeros((7, width_x, width_y), np.float32)
    for x in range(width_x):
        for d in range(-3, 4):
            if 0 <= x % 4 + d < 4:
                shifts[d + 3, x, :] = second[x % 4, x % 4 + d]
    return weight, shifts


def series_mul(u, v):
    return [sum(u[i] * v[k - i] for i in range(k + 1)) for k in range(len(u))]


def series_inverse(u):
    first = 1.0 / u[0]
    out = [first]
    for k in range(1, len(u)):
        out.append(-first * sum(u[i] * out[k - i] for i in range(1, k + 1)))
    return out


def prepare(slab, count, params, mix_in, relax_in, push_in, u_out, sum_out, v_out, coef_out):
    levels = relax_in.shape[1]
    fields = push_in.shape[0]
    shape = (8, levels)
    params[...] = jnp.zeros_like(params)
    params[0:1, 0 : levels - 1] = mix_in[...]
    params[8 : 8 + fields, :] = push_in[...]
    params[23:24, :] = jnp.ones((1, levels), jnp.float32)
    hi = jnp.broadcast_to(params[0:1, :], shape)
    lo = pltpu.roll(hi, 1, 1)
    rel = jnp.broadcast_to(relax_in[...], shape)
    params[1:2, :] = relax_in[...]
    params[2:3, :] = lo[0:1, :]
    lane = lax.broadcasted_iota(jnp.int32, shape, 1)
    row = lax.broadcasted_iota(jnp.int32, shape, 0)
    diag = 1.0 + rel + lo + hi

    def back(x, s):
        return pltpu.roll(x, s, 1)

    def ahead(x, s):
        return pltpu.roll(x, levels - s, 1)

    def reduce_system(a, b, c, extent):
        stages = []
        s = 1
        while s < extent:
            alpha = -a / back(b, s)
            gamma = -c / ahead(b, s)
            b = b + alpha * back(c, s) + gamma * ahead(a, s)
            a = alpha * back(a, s)
            c = gamma * ahead(c, s)
            stages.append((s, alpha, gamma))
            s *= 2
        return stages, 1.0 / b

    def solve(system, d):
        stages, inverse = system
        for s, alpha, gamma in stages:
            d = d + alpha * back(d, s) + gamma * ahead(d, s)
        return d * inverse

    whole = reduce_system(-lo, diag, -hi, levels)
    cut = reduce_system(
        jnp.where(lane % slab == 0, 0.0, -lo),
        diag,
        jnp.where(lane % slab == slab - 1, 0.0, -hi),
        slab,
    )
    push = [params[8:16, :], jnp.where(row == 7, 0.0, params[16:24, :])]
    held = [params[8:16, :], params[16:24, :]]
    sums = [jnp.zeros(shape, jnp.float32)] * 2
    for k in range(SUBSTEPS + 1):
        for h in range(2):
            u_out[k * 16 + h * 8 : k * 16 + h * 8 + 8, :] = held[h]
            sums[h] = jnp.where(lane == k, jnp.sum(held[h], axis=1, keepdims=True), sums[h])
        if k < SUBSTEPS:
            held = [solve(whole, held[h]) + push[h] for h in range(2)]

    sum_out[0:8, :] = sums[0]
    sum_out[8:16, :] = sums[1]
    spot = jnp.where(row < 4, row * slab + slab - 1, (row - 4) * slab)
    tips = jnp.where((lane == spot) & (row % 4 < count), 1.0, 0.0)
    other = pltpu.roll(tips, 4, 0)

    def total(x):
        return jnp.broadcast_to(jnp.sum(x, axis=1, keepdims=True), shape)

    mix = total(jnp.where(row < 4, lo, hi) * other)
    near, far = [], []
    v = tips
    for k in range(SUBSTEPS):
        v = solve(cut, v)
        v_out[k * 8 : k * 8 + 8, :] = v
        near.append(total(v * tips))
        far.append(total(v * other))
    facing = [pltpu.roll(x, 4, 0) for x in near]
    square = mix * mix
    far_far = series_mul(far, far)

    def beside(z):
        return [jnp.where(row < 4, pltpu.roll(x, 1, 0), pltpu.roll(x, 7, 0)) for x in z]

    def gain(u, v):
        product = series_mul(u, v)
        return series_inverse(
            [(1.0 if k == 0 else 0.0) - square * x for k, x in enumerate(product)]
        )

    z = near
    for _ in range(count - 1):
        zn = beside(z)
        change = series_mul(series_mul(far_far, zn), gain(zn, facing))
        z = [x + square * y for x, y in zip(near, change)]
    zn = beside(z)
    first = [mix * x for x in series_mul(far, gain(zn, facing))]
    next_ = [mix * x for x in series_mul(first, zn)]
    edge = gain(zn, [pltpu.roll(x, 4, 0) for x in z])
    edge_one = [mix * x for x in edge]
    edge_two = [mix * x for x in series_mul(edge_one, zn)]
    packed = jnp.zeros(shape, jnp.float32)
    for g, part in enumerate((first, next_, edge_one, edge_two)):
        for k in range(SUBSTEPS):
            packed = jnp.where(lane == g * SUBSTEPS + k, part[k], packed)
    coef_out[...] = packed


def main_kernel(
    dims,
    state_h, classes_h, span_h, w_h, shifts_h, rate_h, mix_h, relax_h, push_h,
    out, share,
    state, classes, span, table, weight, shifts, rate, mix_v, relax_v, push_v,
    params, u_v, sum_v, v_v, coef_v, u_s, sum_s, v_s, coef_s, own_s,
    moved, swept, carry, scale, link, middle_scale,
    lap, hy_out, hy_in, x_out, x_in, weights, p_loc, q_loc, p_out, p_in, q_out, q_in,
    tend, hot, slots, got_one, part, got_two, full,
    state_sem, in_sem, table_sem,
    ys, yr, xs, xr, ps, pr, qs, qr, os, o_r, ts, t_r, fs, f_r,
):
    n_ex, n_ey, n_lb, fields, slab = dims
    rows = slab * 8
    tiles = n_ex * n_ey
    ex, ey, lb = lax.axis_index("ex"), lax.axis_index("ey"), lax.axis_index("lb")
    tile = ex * n_ey + ey
    sides = 1 if n_ey == 2 else 2
    size = 3 if fields % 3 == 0 else 1
    chunks = fields // size

    def tile_peer(o):
        t = lax.rem(tile + o, tiles)
        return (t // n_ey, lax.rem(t, n_ey), lb)

    def slab_peer(o):
        return (ex, ey, lax.rem(lb + o, n_lb))

    barrier = pltpu.get_barrier_semaphore()

    def greet_tiles(o, c):
        pl.semaphore_signal(barrier, inc=1, device_id=tile_peer(o), device_id_type=MESH)
        return c

    def greet_slabs(o, c):
        pl.semaphore_signal(barrier, inc=1, device_id=slab_peer(o), device_id_type=MESH)
        return c

    loads = [
        pltpu.make_async_copy(a, b, in_sem.at[i])
        for i, (a, b) in enumerate(
            (
                (shifts_h, shifts), (w_h, table), (classes_h, classes), (span_h, span),
                (rate_h, rate), (mix_h, mix_v), (relax_h, relax_v), (push_h, push_v),
            )
        )
    ]

    def chunk(f):
        return pl.ds(f * size, size)

    def load_state(f):
        return pltpu.make_async_copy(state_h.at[chunk(f)], state.at[chunk(f)], state_sem.at[f])

    def fetch(f, c):
        load_state(f).start()
        return c

    for copy in loads:
        copy.start()
    lax.fori_loop(0, chunks, fetch, 0)
    lax.fori_loop(1, tiles, greet_tiles, 0)
    lax.fori_loop(1, n_lb, greet_slabs, 0)

    row_x = lax.broadcasted_iota(jnp.int32, (8, 128), 0)
    lane = lax.broadcasted_iota(jnp.int32, (8, 128), 1)
    def derive(f, source, step):
        s = source[chunk(f)].reshape(size * slab, 8, 128)
        along = shifts[3][None] * s
        for d in (-3, -2, -1, 1, 2, 3):
            along = along + shifts[d + 3][None] * pltpu.roll(s, (8 - d) % 8, 1)
        both = jnp.concatenate(
            [s.reshape(size * rows, 128), along.reshape(size * rows, 128)], axis=1
        )
        high = both.astype(jnp.bfloat16)
        low = (both - high.astype(jnp.float32)).astype(jnp.bfloat16)
        result = (
            jnp.dot(high, weight[0], preferred_element_type=jnp.float32)
            + jnp.dot(low, weight[0], preferred_element_type=jnp.float32)
            + jnp.dot(high, weight[1], preferred_element_type=jnp.float32)
        )
        lap[chunk(f)] = result[:, :128].reshape(size, rows, 128)
        hy_out[step, chunk(f)] = result[:, 128:].reshape(size, rows, 128)

    def y_copy(step, f, side):
        peer = lax.rem(ey + (1 if side == 0 else n_ey - 1), n_ey)
        return pltpu.make_async_remote_copy(
            src_ref=hy_out.at[step, chunk(f)],
            dst_ref=hy_in.at[step, side, chunk(f)],
            send_sem=ys.at[step, side, f],
            recv_sem=yr.at[step, side, f],
            device_id=(ex, peer, lb),
            device_id_type=MESH,
        )

    def x_copy(step, f, side):
        peer = lax.rem(ex + (1 if side == 0 else n_ex - 1), n_ex)
        return pltpu.make_async_remote_copy(
            src_ref=x_out.at[step, side, chunk(f)],
            dst_ref=x_in.at[step, side, chunk(f)],
            send_sem=xs.at[step, side, f],
            recv_sem=xr.at[step, side, f],
            device_id=(peer, ey, lb),
            device_id_type=MESH,
        )

    def start_y(f, step):
        for side in range(sides):
            y_copy(step, f, side).start()

    def spread(f, step):
        for side in range(sides):
            y_copy(step, f, side).wait_recv()
        shape = (size * slab, 8, 128)
        value = lap[chunk(f)].reshape(shape)
        if sides == 1:
            value = value + hy_in[step, 0, chunk(f)].reshape(shape)
        else:
            value = value + jnp.where(lane == 0, hy_in[step, 0, chunk(f)].reshape(shape), 0.0)
            value = value + jnp.where(lane == 127, hy_in[step, 1, chunk(f)].reshape(shape), 0.0)
        lap[chunk(f)] = value.reshape(size, rows, 128)
        for i in range(size):
            x_out[step, 0, f * size + i] = lap[f * size + i, pl.ds(7, slab, stride=8), :]
            x_out[step, 1, f * size + i] = lap[f * size + i, pl.ds(0, slab, stride=8), :]
        x_copy(step, f, 0).start()
        x_copy(step, f, 1).start()

    def advance(f, source, step):
        x_copy(step, f, 0).wait_recv()
        x_copy(step, f, 1).wait_recv()
        joins = (row_x == 0) | (row_x == 3) | (row_x == 4) | (row_x == 7)
        for i in range(size):
            g = f * size + i
            value = lap[g].reshape(slab, 8, 128)
            before = pltpu.roll(value, 1, 1)
            after = pltpu.roll(value, 7, 1)
            first = jnp.broadcast_to(x_in[step, 0, g][:, None, :], (slab, 8, 128))
            last = jnp.broadcast_to(x_in[step, 1, g][:, None, :], (slab, 8, 128))
            partner = jnp.where(
                row_x == 0,
                first,
                jnp.where(row_x == 7, last, jnp.where(row_x == 3, after, before)),
            )
            edged = jnp.where(joins, 0.5 * (value + partner), value)
            moved[g] = source[g] + rate[g] * edged

    for copy in loads[:2]:
        copy.wait()
    split = table[...].astype(jnp.bfloat16)
    weight[0] = split
    weight[1] = (table[...] - split.astype(jnp.float32)).astype(jnp.bfloat16)
    load_state(0).wait()
    derive(0, state, 0)
    pl.semaphore_wait(barrier, tiles - 1 + n_lb - 1)
    start_y(0, 0)

    def open_rest(f, c):
        load_state(f).wait()
        derive(f, state, 0)
        start_y(f, 0)
        spread(f - 1, 0)
        return c

    lax.fori_loop(1, chunks, open_rest, 0)
    spread(chunks - 1, 0)
    for copy in loads[2:]:
        copy.wait()
    prepare(slab, n_lb, params, mix_v, relax_v, push_v, u_v, sum_v, v_v, coef_v)
    own_v = ((u_v, u_s), (sum_v, sum_s), (v_v, v_s), (coef_v, coef_s), (params, own_s))
    tables = [pltpu.make_async_copy(a, b, table_sem.at[i]) for i, (a, b) in enumerate(own_v)]
    for copy in tables:
        copy.start()
    cls = classes[...]
    for x in range(8):
        mine = lax.broadcasted_iota(jnp.int32, (128, 1024), 0) + x * 128
        hot[x * 128 : (x + 1) * 128, :] = (
            (mine == span[...]).astype(jnp.float32).astype(jnp.bfloat16)
        )
    for copy in tables:
        copy.wait()

    half = slab // 2

    def factor(i, previous):
        found = []
        for side, before in enumerate(previous):
            l = i if side == 0 else slab - 1 - i
            at = lb * slab + l
            low, high = own_s[2, at], own_s[0, at]
            outer, inner = (low, high) if side == 0 else (high, low)
            ratio = jnp.where(i == 0, 0.0, outer) * before
            inverse = 1.0 / (1.0 + own_s[1, at] + low + high - jnp.where(i == 0, 0.0, outer) * ratio)
            carry[l] = ratio
            scale[l] = inverse
            link[l] = inner * inverse
            found.append(inverse)
        return tuple(found)

    lax.fori_loop(0, half, factor, (jnp.zeros((8, 128), jnp.float32),) * 2)
    middle_scale[...] = 1.0 / (1.0 - link[half - 1] * link[half])

    def set_weight(l, c):
        at = lb * slab + l
        w = [u_s[k * 16 + 15, at] - 1.0 for k in range(1, 5)]
        weights[l] = jnp.where(
            cls == 0, w[0], jnp.where(cls == 1, w[1], jnp.where(cls == 2, w[2], w[3]))
        )
        return c

    lax.fori_loop(0, slab, set_weight, 0)
    def middle(f, c):
        advance(f, state, 0)
        derive(f, moved, 1)
        start_y(f, 1)

        @pl.when(f > 0)
        def _():
            spread(f - 1, 1)

        return c

    lax.fori_loop(0, chunks, middle, 0)
    spread(chunks - 1, 1)

    def pick(group, k, base):
        return coef_s[base + lb, group * SUBSTEPS + k]

    def convolve(group, base, k, value):
        out = pick(group, 0, base) * value[k]
        for i in range(1, k + 1):
            out = out + pick(group, i, base) * value[k - i]
        return out

    def scan_copy(f, down):
        if down:
            return pltpu.make_async_remote_copy(
                src_ref=p_out.at[chunk(f)], dst_ref=p_in.at[chunk(f)],
                send_sem=ps.at[f], recv_sem=pr.at[f],
                device_id=(ex, ey, lax.rem(lb + 1, n_lb)), device_id_type=MESH,
            )
        return pltpu.make_async_remote_copy(
            src_ref=q_out.at[chunk(f)], dst_ref=q_in.at[chunk(f)],
            send_sem=qs.at[f], recv_sem=qr.at[f],
            device_id=(ex, ey, lax.rem(lb + n_lb - 1, n_lb)), device_id_type=MESH,
        )

    def scan_step(f, down):
        arrives = lb > 0 if down else lb < n_lb - 1
        leaves = lb < n_lb - 1 if down else lb > 0
        inward, outward = (p_in, p_out) if down else (q_in, q_out)
        same, opposite = (p_loc, q_loc) if down else (q_loc, p_loc)
        base = 0 if down else 4

        @pl.when((f >= 0) & (f < chunks))
        def _():
            @pl.when(arrives)
            def _():
                scan_copy(f, down).wait_recv()
                own = [same[chunk(f), k] for k in range(SUBSTEPS)]
                facing = [opposite[chunk(f), k] for k in range(SUBSTEPS)]
                coming = [inward[chunk(f), k] for k in range(SUBSTEPS)]
                for k in range(SUBSTEPS):
                    outward[chunk(f), k] = (
                        own[k] + convolve(0, base, k, coming) + convolve(1, base, k, facing)
                    )

            @pl.when(jnp.logical_not(arrives))
            def _():
                for k in range(SUBSTEPS):
                    outward[chunk(f), k] = same[chunk(f), k]

            @pl.when(leaves)
            def _():
                scan_copy(f, down).start()

    def scan_steps(i):
        scan_step(i - lb * SKEW, True)
        scan_step(i - (n_lb - 1 - lb) * SKEW, False)

    def summarise(f):
        zero = jnp.zeros((size, 8, 128), jnp.float32)

        def level(l, c):
            x = moved[chunk(f), l]
            at = lb * slab + l
            out = [c[k] + v_s[k * 8 + lb, at] * x for k in range(4)]
            out += [c[4 + k] + v_s[k * 8 + 4 + lb, at] * x for k in range(4)]
            out.append(c[8] + weights[l][None] * x)
            return tuple(out)

        sums = lax.fori_loop(0, slab, level, (zero,) * 9, unroll=4)
        for k in range(SUBSTEPS):
            p_loc[chunk(f), k] = sums[k]
            q_loc[chunk(f), k] = sums[4 + k]
        for i in range(size):
            g = f * size + i
            h = [sum_s[g, k] * (1.0 / n_lb) for k in range(4)]
            extra = jnp.where(
                cls == 0, h[0], jnp.where(cls == 1, h[1], jnp.where(cls == 2, h[2], h[3]))
            )
            tend[pl.ds(pl.multiple_of(g * 8, 8), 8), :] = sums[8][i] + extra

    tend[fields * 8 : 128, :] = jnp.zeros((128 - fields * 8, 128), jnp.float32)

    @pl.when(lb == 0)
    def _():
        p_in[...] = jnp.zeros_like(p_in)

    @pl.when(lb == n_lb - 1)
    def _():
        q_in[...] = jnp.zeros_like(q_in)

    def store(f):
        return pltpu.make_async_copy(
            moved.at[chunk(f)], out.at[chunk(f)], state_sem.at[f]
        )

    def sweep(g):
        group = size
        start = g * size
        at = chunk(g)
        above = [p_in[at, k] for k in range(SUBSTEPS)]
        below = [q_in[at, k] for k in range(SUBSTEPS)]
        own_p = [p_out[at, k] for k in range(SUBSTEPS)]
        own_q = [q_out[at, k] for k in range(SUBSTEPS)]
        for k in range(SUBSTEPS):
            p_loc[at, k] = convolve(2, 0, k, above) + convolve(3, 0, k, own_q)
            q_loc[at, k] = convolve(2, 4, k, below) + convolve(3, 4, k, own_p)

        def push(f, l):
            h = [u_s[k * 16 + f, lb * slab + l] for k in range(4)]
            return jnp.where(
                cls == 0, h[0], jnp.where(cls == 1, h[1], jnp.where(cls == 2, h[2], h[3]))
            )

        def keep(k, l, y):
            if k > 0:
                y = jnp.where(cls >= k, y, moved[at, l])
            if k < SUBSTEPS - 1:
                moved[at, l] = y
            else:
                for f in range(group):
                    moved[start + f, l] = y[f] + push(start + f, l)

        for k in range(SUBSTEPS):

            def inward(i, z):
                top, low = i, slab - 1 - i
                above = moved[at, top] + carry[top][None] * z[0]
                below = moved[at, low] + carry[low][None] * z[1]
                swept[at, top] = above
                swept[at, low] = below
                return above, below

            first = moved[at, 0] + p_loc[at, k]
            last = moved[at, slab - 1] + q_loc[at, k]
            swept[at, 0] = first
            swept[at, slab - 1] = last
            first, last = lax.fori_loop(1, half, inward, (first, last), unroll=5)
            first = first * scale[half - 1][None]
            last = last * scale[half][None]
            above = (first + link[half - 1][None] * last) * middle_scale[...][None]
            below = last + link[half][None] * above
            keep(k, half - 1, above)
            keep(k, half, below)

            def outward(i, y, k=k):
                top, low = half - 1 - i, half + i
                above = swept[at, top] * scale[top][None] + link[top][None] * y[0]
                below = swept[at, low] * scale[low][None] + link[low][None] * y[1]
                keep(k, top, above)
                keep(k, low, below)
                return above, below

            lax.fori_loop(1, half, outward, (above, below), unroll=5 if k < SUBSTEPS - 1 else 3)
        store(g).start()

    def closing(i, c):
        advance(i, moved, 1)
        summarise(i)
        scan_steps(i)
        return c

    hops = (n_lb - 1) * SKEW

    def closing_sweep(i, c):
        closing(i, c)
        sweep(i - hops)
        return c

    lax.fori_loop(0, hops, closing, 0)
    lax.fori_loop(hops, chunks, closing_sweep, 0)

    def three(value):
        a = value.astype(jnp.bfloat16)
        rest = value - a.astype(jnp.float32)
        b = rest.astype(jnp.bfloat16)
        last = (rest - b.astype(jnp.float32)).astype(jnp.bfloat16)
        return jnp.concatenate([a, b, last], axis=0)

    def together(value):
        return value[:16] + value[16:32] + value[32:]

    span_slots = 1024 // n_lb
    gathered = jnp.zeros((48, 1024), jnp.float32)
    for x in range(0, 8, 2):
        pair = [three(tend[pl.ds(x + i, 16, stride=8), :]) for i in range(2)]
        gathered = gathered + jnp.dot(
            jnp.concatenate(pair, axis=1),
            hot[x * 128 : (x + 2) * 128, :],
            preferred_element_type=jnp.float32,
        )
    gathered = together(gathered)
    for g in range(n_lb):
        slots[g] = gathered[:, g * span_slots : (g + 1) * span_slots]

    def one_copy(o):
        return pltpu.make_async_remote_copy(
            src_ref=slots.at[lax.rem(lb + o, n_lb)], dst_ref=got_one.at[o - 1],
            send_sem=os.at[o - 1], recv_sem=o_r.at[o - 1],
            device_id=slab_peer(o), device_id_type=MESH,
        )

    def two_copy(o):
        return pltpu.make_async_remote_copy(
            src_ref=part, dst_ref=got_two.at[o - 1],
            send_sem=ts.at[o - 1], recv_sem=t_r.at[o - 1],
            device_id=tile_peer(o), device_id_type=MESH,
        )

    def three_copy(o):
        return pltpu.make_async_remote_copy(
            src_ref=full.at[lb], dst_ref=full.at[lb],
            send_sem=fs.at[o - 1], recv_sem=f_r.at[o - 1],
            device_id=slab_peer(o), device_id_type=MESH,
        )

    def three_arrival(o):
        other = lax.rem(lb + n_lb - o, n_lb)
        return pltpu.make_async_remote_copy(
            src_ref=full.at[other], dst_ref=full.at[other],
            send_sem=fs.at[o - 1], recv_sem=f_r.at[o - 1],
            device_id=slab_peer(o), device_id_type=MESH,
        )

    for o in range(1, n_lb):
        one_copy(o).start()

    def trailing(i, c):
        scan_steps(i)
        sweep(i - hops)
        return c

    lax.fori_loop(chunks, chunks + 1, trailing, 0)
    total = slots[lb]
    for o in range(1, n_lb):
        one_copy(o).wait_recv()
        total = total + got_one[o - 1]
    part[...] = total

    def start_two(o, c):
        two_copy(o).start()
        return c

    lax.fori_loop(1, tiles, start_two, 0)
    lax.fori_loop(chunks + 1, chunks + 2, trailing, 0)

    def add_two(o, c):
        two_copy(o).wait_recv()
        return c + got_two[o - 1]

    total = lax.fori_loop(1, tiles, add_two, part[...])
    full[lb] = total * (1.0 / (tiles * slab * n_lb))
    for o in range(1, n_lb):
        three_copy(o).start()

    lax.fori_loop(chunks + 2, chunks + hops, trailing, 0)
    for o in range(1, n_lb):
        three_arrival(o).wait_recv()
    spread_share = jnp.zeros((48, 1024), jnp.float32)
    for g in range(n_lb):
        spread_share = spread_share + lax.dot_general(
            three(full[g]),
            hot[:, g * span_slots : (g + 1) * span_slots],
            (((1,), (1,)), ((), ())),
            preferred_element_type=jnp.float32,
        )
    spread_share = together(spread_share)
    for x in range(8):
        share[pl.ds(x, fields, stride=8), :] = spread_share[:fields, x * 128 : (x + 1) * 128]

    def drain_store(f, c):
        store(f).wait()
        return c

    lax.fori_loop(0, chunks, drain_store, 0)

    def drain(f, c):
        for step in range(STEPS):
            for side in range(sides):
                y_copy(step, f, side).wait_send()
            for side in range(2):
                x_copy(step, f, side).wait_send()

        @pl.when(lb < n_lb - 1)
        def _():
            scan_copy(f, True).wait_send()

        @pl.when(lb > 0)
        def _():
            scan_copy(f, False).wait_send()

        return c

    lax.fori_loop(0, chunks, drain, 0)
    for o in range(1, n_lb):
        one_copy(o).wait_send()
        three_copy(o).wait_send()

    def drain_two(o, c):
        two_copy(o).wait_send()
        return c

    lax.fori_loop(1, tiles, drain_two, 0)


def local(atmosphere_state, diffusivity, mixing, relaxation, forcing, span_map, cost_class):
    fields, slab, width_x, width_y = atmosphere_state.shape
    n_ex, n_ey, n_lb = (lax.axis_size(a) for a in ("ex", "ey", "lb"))
    levels = slab * n_lb
    dims = (n_ex, n_ey, n_lb, fields, slab)
    rows = slab * 8
    tiles = n_ex * n_ey
    sides = 1 if n_ey == 2 else 2
    weight, shifts = operator_tables(width_x, width_y)
    hbm = pl.BlockSpec(memory_space=pltpu.HBM)
    f32 = jnp.float32
    dma = pltpu.SemaphoreType.DMA
    wide = 1024 // n_lb
    volume = (fields, slab, 8, 128)
    physics, share = pl.pallas_call(
        functools.partial(main_kernel, dims),
        out_shape=[
            jax.ShapeDtypeStruct(volume, f32),
            jax.ShapeDtypeStruct((fields * 8, 128), f32),
        ],
        in_specs=[hbm] * 9,
        out_specs=[hbm, pl.BlockSpec(memory_space=pltpu.VMEM)],
        scratch_shapes=[
            pltpu.VMEM(volume, f32),
            pltpu.VMEM((8, 128), jnp.int32),
            pltpu.VMEM((1, 1024), jnp.int32),
            pltpu.VMEM((256, 256), f32),
            pltpu.VMEM((2, 256, 256), jnp.bfloat16),
            pltpu.VMEM((7, 8, 128), f32),
            pltpu.SMEM((fields,), f32),
            pltpu.VMEM((1, levels - 1), f32),
            pltpu.VMEM((1, levels), f32),
            pltpu.VMEM((fields, levels), f32),
            pltpu.VMEM((24, levels), f32),
            pltpu.VMEM((80, levels), f32),
            pltpu.VMEM((16, levels), f32),
            pltpu.VMEM((SUBSTEPS * 8, levels), f32),
            pltpu.VMEM((8, levels), f32),
            pltpu.SMEM((80, levels), f32),
            pltpu.SMEM((16, levels), f32),
            pltpu.SMEM((SUBSTEPS * 8, levels), f32),
            pltpu.SMEM((8, levels), f32),
            pltpu.SMEM((24, levels), f32),
            pltpu.VMEM(volume, f32),
            pltpu.VMEM(volume, f32),
            pltpu.VMEM((slab, 8, 128), f32),
            pltpu.VMEM((slab, 8, 128), f32),
            pltpu.VMEM((slab, 8, 128), f32),
            pltpu.VMEM((8, 128), f32),
            pltpu.VMEM((fields, rows, 128), f32),
            pltpu.VMEM((STEPS, fields, rows, 128), f32),
            pltpu.VMEM((STEPS, sides, fields, rows, 128), f32),
            pltpu.VMEM((STEPS, 2, fields, slab, 128), f32),
            pltpu.VMEM((STEPS, 2, fields, slab, 128), f32),
            pltpu.VMEM((slab, 8, 128), f32),
        ]
        + [pltpu.VMEM((fields, SUBSTEPS, 8, 128), f32)] * 6
        + [
            pltpu.VMEM((128, 128), f32),
            pltpu.VMEM((1024, 1024), jnp.bfloat16),
            pltpu.VMEM((n_lb, 16, wide), f32),
            pltpu.VMEM((n_lb - 1, 16, wide), f32),
            pltpu.VMEM((16, wide), f32),
            pltpu.VMEM((tiles - 1, 16, wide), f32),
            pltpu.VMEM((n_lb, 16, wide), f32),
            dma((fields,)),
            dma((8,)),
            dma((5,)),
            dma((STEPS, sides, fields)),
            dma((STEPS, sides, fields)),
            dma((STEPS, 2, fields)),
            dma((STEPS, 2, fields)),
            dma((fields,)),
            dma((fields,)),
            dma((fields,)),
            dma((fields,)),
            dma((n_lb - 1,)),
            dma((n_lb - 1,)),
            dma((tiles - 1,)),
            dma((tiles - 1,)),
            dma((n_lb - 1,)),
            dma((n_lb - 1,)),
        ],
        compiler_params=pltpu.CompilerParams(
            collective_id=0, has_side_effects=True, vmem_limit_bytes=VMEM_MIB * 1024 * 1024
        ),
    )(
        atmosphere_state, cost_class, span_map.reshape(1, width_x * width_y),
        jnp.asarray(weight), jnp.asarray(shifts), diffusivity,
        mixing.reshape(1, levels - 1), relaxation.reshape(1, levels), forcing,
    )
    return physics - share.reshape(fields, 1, 8, 128)


def solution(mesh):
    return jax.shard_map(
        local,
        mesh=mesh,
        in_specs=(
            P(None, "lb", "ex", "ey"),
            P(),
            P(),
            P(),
            P(),
            P("ex", "ey", None),
            P("ex", "ey"),
        ),
        out_specs=P(None, "lb", "ex", "ey"),
        check_vma=False,
    )
```

```python
import functools
import math

import jax
import jax.numpy as jnp
import numpy as np
from jax import lax
from jax.experimental import pallas as pl
from jax.experimental.pallas import tpu as pltpu
from jax.sharding import PartitionSpec as P

STEPS = 2
SUBSTEPS = 4
MESH = pl.DeviceIdType.MESH
SKEW = 2
VMEM_MIB = 63


def second_table():
    inner_root = 1.0 / math.sqrt(5.0)
    gll_nodes = np.array([-1.0, -inner_root, inner_root, 1.0])
    weights = np.array(
        [
            np.prod(
                [gll_nodes[target] - gll_nodes[source] for source in range(4) if source != target]
            )
            for target in range(4)
        ]
    )
    first_table = np.zeros((4, 4))
    for target in range(4):
        for source in range(4):
            if source != target:
                first_table[target, source] = weights[target] / (
                    weights[source] * (gll_nodes[target] - gll_nodes[source])
                )
    for target in range(4):
        first_table[target, target] = -first_table[target].sum()
    return (first_table @ first_table).astype(np.float32)


def operator_tables(width_x, width_y):
    second = second_table()
    along = np.kron(np.eye(width_y // 4), second.T).astype(np.float64)
    edge = np.zeros((width_y, width_y))
    for y in range(width_y):
        if y % 4 == 3:
            edge[y, y] = 0.5
            if y + 1 < width_y:
                edge[y + 1, y] = 0.5
        elif y % 4 == 0:
            edge[y, y] = 0.5
            if y > 0:
                edge[y - 1, y] = 0.5
        else:
            edge[y, y] = 1.0
    rim = np.zeros((width_y, width_y))
    rim[0, width_y - 1] = 0.5
    rim[width_y - 1, 0] = 0.5
    both = np.concatenate([edge, rim], axis=1)
    weight = np.concatenate([along @ both, both], axis=0).astype(np.float32)
    shifts = np.zeros((7, width_x, width_y), np.float32)
    for x in range(width_x):
        for d in range(-3, 4):
            if 0 <= x % 4 + d < 4:
                shifts[d + 3, x, :] = second[x % 4, x % 4 + d]
    return weight, shifts


def series_mul(u, v):
    return [sum(u[i] * v[k - i] for i in range(k + 1)) for k in range(len(u))]


def series_inverse(u):
    first = 1.0 / u[0]
    out = [first]
    for k in range(1, len(u)):
        out.append(-first * sum(u[i] * out[k - i] for i in range(1, k + 1)))
    return out


def prepare(slab, count, params, mix_in, relax_in, push_in, u_out, sum_out, v_out, coef_out):
    levels = relax_in.shape[1]
    fields = push_in.shape[0]
    shape = (8, levels)
    params[...] = jnp.zeros_like(params)
    params[0:1, 0 : levels - 1] = mix_in[...]
    params[8 : 8 + fields, :] = push_in[...]
    params[23:24, :] = jnp.ones((1, levels), jnp.float32)
    hi = jnp.broadcast_to(params[0:1, :], shape)
    lo = pltpu.roll(hi, 1, 1)
    rel = jnp.broadcast_to(relax_in[...], shape)
    params[1:2, :] = relax_in[...]
    params[2:3, :] = lo[0:1, :]
    lane = lax.broadcasted_iota(jnp.int32, shape, 1)
    row = lax.broadcasted_iota(jnp.int32, shape, 0)
    diag = 1.0 + rel + lo + hi

    def back(x, s):
        return pltpu.roll(x, s, 1)

    def ahead(x, s):
        return pltpu.roll(x, levels - s, 1)

    def reduce_system(a, b, c, extent):
        stages = []
        s = 1
        while s < extent:
            alpha = -a / back(b, s)
            gamma = -c / ahead(b, s)
            b = b + alpha * back(c, s) + gamma * ahead(a, s)
            a = alpha * back(a, s)
            c = gamma * ahead(c, s)
            stages.append((s, alpha, gamma))
            s *= 2
        return stages, 1.0 / b

    def solve(system, d):
        stages, inverse = system
        for s, alpha, gamma in stages:
            d = d + alpha * back(d, s) + gamma * ahead(d, s)
        return d * inverse

    whole = reduce_system(-lo, diag, -hi, levels)
    cut = reduce_system(
        jnp.where(lane % slab == 0, 0.0, -lo),
        diag,
        jnp.where(lane % slab == slab - 1, 0.0, -hi),
        slab,
    )
    push = [params[8:16, :], jnp.where(row == 7, 0.0, params[16:24, :])]
    held = [params[8:16, :], params[16:24, :]]
    sums = [jnp.zeros(shape, jnp.float32)] * 2
    for k in range(SUBSTEPS + 1):
        for h in range(2):
            u_out[k * 16 + h * 8 : k * 16 + h * 8 + 8, :] = held[h]
            sums[h] = jnp.where(lane == k, jnp.sum(held[h], axis=1, keepdims=True), sums[h])
        if k < SUBSTEPS:
            held = [solve(whole, held[h]) + push[h] for h in range(2)]

    sum_out[0:8, :] = sums[0]
    sum_out[8:16, :] = sums[1]
    spot = jnp.where(row < 4, row * slab + slab - 1, (row - 4) * slab)
    tips = jnp.where((lane == spot) & (row % 4 < count), 1.0, 0.0)
    other = pltpu.roll(tips, 4, 0)

    def total(x):
        return jnp.broadcast_to(jnp.sum(x, axis=1, keepdims=True), shape)

    mix = total(jnp.where(row < 4, lo, hi) * other)
    near, far = [], []
    v = tips
    for k in range(SUBSTEPS):
        v = solve(cut, v)
        v_out[k * 8 : k * 8 + 8, :] = v
        near.append(total(v * tips))
        far.append(total(v * other))
    facing = [pltpu.roll(x, 4, 0) for x in near]
    square = mix * mix
    far_far = series_mul(far, far)

    def beside(z):
        return [jnp.where(row < 4, pltpu.roll(x, 1, 0), pltpu.roll(x, 7, 0)) for x in z]

    def gain(u, v):
        product = series_mul(u, v)
        return series_inverse(
            [(1.0 if k == 0 else 0.0) - square * x for k, x in enumerate(product)]
        )

    z = near
    for _ in range(count - 1):
        zn = beside(z)
        change = series_mul(series_mul(far_far, zn), gain(zn, facing))
        z = [x + square * y for x, y in zip(near, change)]
    zn = beside(z)
    first = [mix * x for x in series_mul(far, gain(zn, facing))]
    next_ = [mix * x for x in series_mul(first, zn)]
    edge = gain(zn, [pltpu.roll(x, 4, 0) for x in z])
    edge_one = [mix * x for x in edge]
    edge_two = [mix * x for x in series_mul(edge_one, zn)]
    packed = jnp.zeros(shape, jnp.float32)
    for g, part in enumerate((first, next_, edge_one, edge_two)):
        for k in range(SUBSTEPS):
            packed = jnp.where(lane == g * SUBSTEPS + k, part[k], packed)
    coef_out[...] = packed


def main_kernel(
    dims,
    state_h, classes_h, span_h, w_h, shifts_h, rate_h, mix_h, relax_h, push_h,
    out, share,
    state, classes, span, table, weight, shifts, rate, mix_v, relax_v, push_v,
    params, u_v, sum_v, v_v, coef_v, u_s, sum_s, v_s, coef_s, own_s,
    moved, swept, carry, scale, link, middle_scale,
    lap, hy_out, hy_in, x_out, x_in, weights, p_loc, q_loc, p_out, p_in, q_out, q_in,
    tend, hot, slots, got_one, part, got_two, full,
    state_sem, in_sem, table_sem,
    ys, yr, xs, xr, ps, pr, qs, qr, os, o_r, ts, t_r, fs, f_r,
):
    n_ex, n_ey, n_lb, fields, slab = dims
    rows = slab * 8
    tiles = n_ex * n_ey
    ex, ey, lb = lax.axis_index("ex"), lax.axis_index("ey"), lax.axis_index("lb")
    tile = ex * n_ey + ey
    sides = 1 if n_ey == 2 else 2
    size = 3 if fields % 3 == 0 else 1
    chunks = fields // size

    def tile_peer(o):
        t = lax.rem(tile + o, tiles)
        return (t // n_ey, lax.rem(t, n_ey), lb)

    def slab_peer(o):
        return (ex, ey, lax.rem(lb + o, n_lb))

    barrier = pltpu.get_barrier_semaphore()

    def greet_tiles(o, c):
        pl.semaphore_signal(barrier, inc=1, device_id=tile_peer(o), device_id_type=MESH)
        return c

    def greet_slabs(o, c):
        pl.semaphore_signal(barrier, inc=1, device_id=slab_peer(o), device_id_type=MESH)
        return c

    loads = [
        pltpu.make_async_copy(a, b, in_sem.at[i])
        for i, (a, b) in enumerate(
            (
                (shifts_h, shifts), (w_h, table), (classes_h, classes), (span_h, span),
                (rate_h, rate), (mix_h, mix_v), (relax_h, relax_v), (push_h, push_v),
            )
        )
    ]

    def chunk(f):
        return pl.ds(f * size, size)

    def load_state(f):
        return pltpu.make_async_copy(state_h.at[chunk(f)], state.at[chunk(f)], state_sem.at[f])

    def fetch(f, c):
        load_state(f).start()
        return c

    for copy in loads:
        copy.start()
    lax.fori_loop(0, chunks, fetch, 0)
    lax.fori_loop(1, tiles, greet_tiles, 0)
    lax.fori_loop(1, n_lb, greet_slabs, 0)

    row_x = lax.broadcasted_iota(jnp.int32, (8, 128), 0)
    lane = lax.broadcasted_iota(jnp.int32, (8, 128), 1)
    def derive(f, source, step):
        s = source[chunk(f)].reshape(size * slab, 8, 128)
        along = shifts[3][None] * s
        for d in (-3, -2, -1, 1, 2, 3):
            along = along + shifts[d + 3][None] * pltpu.roll(s, (8 - d) % 8, 1)
        both = jnp.concatenate(
            [s.reshape(size * rows, 128), along.reshape(size * rows, 128)], axis=1
        )
        high = both.astype(jnp.bfloat16)
        low = (both - high.astype(jnp.float32)).astype(jnp.bfloat16)
        result = (
            jnp.dot(high, weight[0], preferred_element_type=jnp.float32)
            + jnp.dot(low, weight[0], preferred_element_type=jnp.float32)
            + jnp.dot(high, weight[1], preferred_element_type=jnp.float32)
        )
        lap[chunk(f)] = result[:, :128].reshape(size, rows, 128)
        hy_out[step, chunk(f)] = result[:, 128:].reshape(size, rows, 128)

    def y_copy(step, f, side):
        peer = lax.rem(ey + (1 if side == 0 else n_ey - 1), n_ey)
        return pltpu.make_async_remote_copy(
            src_ref=hy_out.at[step, chunk(f)],
            dst_ref=hy_in.at[step, side, chunk(f)],
            send_sem=ys.at[step, side, f],
            recv_sem=yr.at[step, side, f],
            device_id=(ex, peer, lb),
            device_id_type=MESH,
        )

    def x_copy(step, f, side):
        peer = lax.rem(ex + (1 if side == 0 else n_ex - 1), n_ex)
        return pltpu.make_async_remote_copy(
            src_ref=x_out.at[step, side, chunk(f)],
            dst_ref=x_in.at[step, side, chunk(f)],
            send_sem=xs.at[step, side, f],
            recv_sem=xr.at[step, side, f],
            device_id=(peer, ey, lb),
            device_id_type=MESH,
        )

    def start_y(f, step):
        for side in range(sides):
            y_copy(step, f, side).start()

    def spread(f, step):
        for side in range(sides):
            y_copy(step, f, side).wait_recv()
        shape = (size * slab, 8, 128)
        value = lap[chunk(f)].reshape(shape)
        if sides == 1:
            value = value + hy_in[step, 0, chunk(f)].reshape(shape)
        else:
            value = value + jnp.where(lane == 0, hy_in[step, 0, chunk(f)].reshape(shape), 0.0)
            value = value + jnp.where(lane == 127, hy_in[step, 1, chunk(f)].reshape(shape), 0.0)
        lap[chunk(f)] = value.reshape(size, rows, 128)
        for i in range(size):
            x_out[step, 0, f * size + i] = lap[f * size + i, pl.ds(7, slab, stride=8), :]
            x_out[step, 1, f * size + i] = lap[f * size + i, pl.ds(0, slab, stride=8), :]
        x_copy(step, f, 0).start()
        x_copy(step, f, 1).start()

    def advance(f, source, step):
        x_copy(step, f, 0).wait_recv()
        x_copy(step, f, 1).wait_recv()
        joins = (row_x == 0) | (row_x == 3) | (row_x == 4) | (row_x == 7)
        for i in range(size):
            g = f * size + i
            value = lap[g].reshape(slab, 8, 128)
            before = pltpu.roll(value, 1, 1)
            after = pltpu.roll(value, 7, 1)
            first = jnp.broadcast_to(x_in[step, 0, g][:, None, :], (slab, 8, 128))
            last = jnp.broadcast_to(x_in[step, 1, g][:, None, :], (slab, 8, 128))
            partner = jnp.where(
                row_x == 0,
                first,
                jnp.where(row_x == 7, last, jnp.where(row_x == 3, after, before)),
            )
            edged = jnp.where(joins, 0.5 * (value + partner), value)
            moved[g] = source[g] + rate[g] * edged

    for copy in loads[:2]:
        copy.wait()
    split = table[...].astype(jnp.bfloat16)
    weight[0] = split
    weight[1] = (table[...] - split.astype(jnp.float32)).astype(jnp.bfloat16)
    load_state(0).wait()
    derive(0, state, 0)
    pl.semaphore_wait(barrier, tiles - 1 + n_lb - 1)
    start_y(0, 0)

    def open_rest(f, c):
        load_state(f).wait()
        derive(f, state, 0)
        start_y(f, 0)
        spread(f - 1, 0)
        return c

    lax.fori_loop(1, chunks, open_rest, 0)
    spread(chunks - 1, 0)
    for copy in loads[2:]:
        copy.wait()
    prepare(slab, n_lb, params, mix_v, relax_v, push_v, u_v, sum_v, v_v, coef_v)
    own_v = ((u_v, u_s), (sum_v, sum_s), (v_v, v_s), (coef_v, coef_s), (params, own_s))
    tables = [pltpu.make_async_copy(a, b, table_sem.at[i]) for i, (a, b) in enumerate(own_v)]
    for copy in tables:
        copy.start()
    cls = classes[...]
    for x in range(8):
        mine = lax.broadcasted_iota(jnp.int32, (128, 1024), 0) + x * 128
        hot[x * 128 : (x + 1) * 128, :] = (
            (mine == span[...]).astype(jnp.float32).astype(jnp.bfloat16)
        )
    for copy in tables:
        copy.wait()

    half = slab // 2

    def factor(i, previous):
        found = []
        for side, before in enumerate(previous):
            l = i if side == 0 else slab - 1 - i
            at = lb * slab + l
            low, high = own_s[2, at], own_s[0, at]
            outer, inner = (low, high) if side == 0 else (high, low)
            ratio = jnp.where(i == 0, 0.0, outer) * before
            inverse = 1.0 / (1.0 + own_s[1, at] + low + high - jnp.where(i == 0, 0.0, outer) * ratio)
            carry[l] = ratio
            scale[l] = inverse
            link[l] = inner * inverse
            found.append(inverse)
        return tuple(found)

    lax.fori_loop(0, half, factor, (jnp.zeros((8, 128), jnp.float32),) * 2)
    middle_scale[...] = 1.0 / (1.0 - link[half - 1] * link[half])

    def set_weight(l, c):
        at = lb * slab + l
        w = [u_s[k * 16 + 15, at] - 1.0 for k in range(1, 5)]
        weights[l] = jnp.where(
            cls == 0, w[0], jnp.where(cls == 1, w[1], jnp.where(cls == 2, w[2], w[3]))
        )
        return c

    lax.fori_loop(0, slab, set_weight, 0)
    def middle(f, c):
        advance(f, state, 0)
        derive(f, moved, 1)
        start_y(f, 1)

        @pl.when(f > 0)
        def _():
            spread(f - 1, 1)

        return c

    lax.fori_loop(0, chunks, middle, 0)
    spread(chunks - 1, 1)

    def pick(group, k, base):
        return coef_s[base + lb, group * SUBSTEPS + k]

    def convolve(group, base, k, value):
        out = pick(group, 0, base) * value[k]
        for i in range(1, k + 1):
            out = out + pick(group, i, base) * value[k - i]
        return out

    def scan_copy(f, down):
        if down:
            return pltpu.make_async_remote_copy(
                src_ref=p_out.at[chunk(f)], dst_ref=p_in.at[chunk(f)],
                send_sem=ps.at[f], recv_sem=pr.at[f],
                device_id=(ex, ey, lax.rem(lb + 1, n_lb)), device_id_type=MESH,
            )
        return pltpu.make_async_remote_copy(
            src_ref=q_out.at[chunk(f)], dst_ref=q_in.at[chunk(f)],
            send_sem=qs.at[f], recv_sem=qr.at[f],
            device_id=(ex, ey, lax.rem(lb + n_lb - 1, n_lb)), device_id_type=MESH,
        )

    def scan_step(f, down):
        arrives = lb > 0 if down else lb < n_lb - 1
        leaves = lb < n_lb - 1 if down else lb > 0
        inward, outward = (p_in, p_out) if down else (q_in, q_out)
        same, opposite = (p_loc, q_loc) if down else (q_loc, p_loc)
        base = 0 if down else 4

        @pl.when((f >= 0) & (f < chunks))
        def _():
            @pl.when(arrives)
            def _():
                scan_copy(f, down).wait_recv()
                own = [same[chunk(f), k] for k in range(SUBSTEPS)]
                facing = [opposite[chunk(f), k] for k in range(SUBSTEPS)]
                coming = [inward[chunk(f), k] for k in range(SUBSTEPS)]
                for k in range(SUBSTEPS):
                    outward[chunk(f), k] = (
                        own[k] + convolve(0, base, k, coming) + convolve(1, base, k, facing)
                    )

            @pl.when(jnp.logical_not(arrives))
            def _():
                for k in range(SUBSTEPS):
                    outward[chunk(f), k] = same[chunk(f), k]

            @pl.when(leaves)
            def _():
                scan_copy(f, down).start()

    def scan_steps(i):
        scan_step(i - lb * SKEW, True)
        scan_step(i - (n_lb - 1 - lb) * SKEW, False)

    def summarise(f):
        zero = jnp.zeros((size, 8, 128), jnp.float32)

        def level(l, c):
            x = moved[chunk(f), l]
            at = lb * slab + l
            out = [c[k] + v_s[k * 8 + lb, at] * x for k in range(4)]
            out += [c[4 + k] + v_s[k * 8 + 4 + lb, at] * x for k in range(4)]
            out.append(c[8] + weights[l][None] * x)
            return tuple(out)

        sums = lax.fori_loop(0, slab, level, (zero,) * 9, unroll=4)
        for k in range(SUBSTEPS):
            p_loc[chunk(f), k] = sums[k]
            q_loc[chunk(f), k] = sums[4 + k]
        for i in range(size):
            g = f * size + i
            h = [sum_s[g, k] * (1.0 / n_lb) for k in range(4)]
            extra = jnp.where(
                cls == 0, h[0], jnp.where(cls == 1, h[1], jnp.where(cls == 2, h[2], h[3]))
            )
            tend[pl.ds(pl.multiple_of(g * 8, 8), 8), :] = sums[8][i] + extra

    tend[fields * 8 : 128, :] = jnp.zeros((128 - fields * 8, 128), jnp.float32)

    @pl.when(lb == 0)
    def _():
        p_in[...] = jnp.zeros_like(p_in)

    @pl.when(lb == n_lb - 1)
    def _():
        q_in[...] = jnp.zeros_like(q_in)

    def store(f):
        return pltpu.make_async_copy(
            moved.at[chunk(f)], out.at[chunk(f)], state_sem.at[f]
        )

    def sweep(g):
        group = size
        start = g * size
        at = chunk(g)
        above = [p_in[at, k] for k in range(SUBSTEPS)]
        below = [q_in[at, k] for k in range(SUBSTEPS)]
        own_p = [p_out[at, k] for k in range(SUBSTEPS)]
        own_q = [q_out[at, k] for k in range(SUBSTEPS)]
        for k in range(SUBSTEPS):
            p_loc[at, k] = convolve(2, 0, k, above) + convolve(3, 0, k, own_q)
            q_loc[at, k] = convolve(2, 4, k, below) + convolve(3, 4, k, own_p)

        def push(f, l):
            h = [u_s[k * 16 + f, lb * slab + l] for k in range(4)]
            return jnp.where(
                cls == 0, h[0], jnp.where(cls == 1, h[1], jnp.where(cls == 2, h[2], h[3]))
            )

        def keep(k, l, y):
            if k > 0:
                y = jnp.where(cls >= k, y, moved[at, l])
            if k < SUBSTEPS - 1:
                moved[at, l] = y
            else:
                for f in range(group):
                    moved[start + f, l] = y[f] + push(start + f, l)

        for k in range(SUBSTEPS):

            def inward(i, z):
                top, low = i, slab - 1 - i
                above = moved[at, top] + carry[top][None] * z[0]
                below = moved[at, low] + carry[low][None] * z[1]
                swept[at, top] = above
                swept[at, low] = below
                return above, below

            first = moved[at, 0] + p_loc[at, k]
            last = moved[at, slab - 1] + q_loc[at, k]
            swept[at, 0] = first
            swept[at, slab - 1] = last
            first, last = lax.fori_loop(1, half, inward, (first, last), unroll=5)
            first = first * scale[half - 1][None]
            last = last * scale[half][None]
            above = (first + link[half - 1][None] * last) * middle_scale[...][None]
            below = last + link[half][None] * above
            keep(k, half - 1, above)
            keep(k, half, below)

            def outward(i, y, k=k):
                top, low = half - 1 - i, half + i
                above = swept[at, top] * scale[top][None] + link[top][None] * y[0]
                below = swept[at, low] * scale[low][None] + link[low][None] * y[1]
                keep(k, top, above)
                keep(k, low, below)
                return above, below

            lax.fori_loop(1, half, outward, (above, below), unroll=5 if k < SUBSTEPS - 1 else 3)
        store(g).start()

    def closing(i, c):
        advance(i, moved, 1)
        summarise(i)
        scan_steps(i)
        return c

    hops = (n_lb - 1) * SKEW

    lax.fori_loop(0, chunks, closing, 0)

    def three(value):
        a = value.astype(jnp.bfloat16)
        rest = value - a.astype(jnp.float32)
        b = rest.astype(jnp.bfloat16)
        last = (rest - b.astype(jnp.float32)).astype(jnp.bfloat16)
        return jnp.concatenate([a, b, last], axis=0)

    def together(value):
        return value[:16] + value[16:32] + value[32:]

    span_slots = 1024 // n_lb
    gathered = jnp.zeros((48, 1024), jnp.float32)
    for x in range(0, 8, 2):
        pair = [three(tend[pl.ds(x + i, 16, stride=8), :]) for i in range(2)]
        gathered = gathered + jnp.dot(
            jnp.concatenate(pair, axis=1),
            hot[x * 128 : (x + 2) * 128, :],
            preferred_element_type=jnp.float32,
        )
    gathered = together(gathered)
    for g in range(n_lb):
        slots[g] = gathered[:, g * span_slots : (g + 1) * span_slots]

    def one_copy(o):
        return pltpu.make_async_remote_copy(
            src_ref=slots.at[lax.rem(lb + o, n_lb)], dst_ref=got_one.at[o - 1],
            send_sem=os.at[o - 1], recv_sem=o_r.at[o - 1],
            device_id=slab_peer(o), device_id_type=MESH,
        )

    def two_copy(o):
        return pltpu.make_async_remote_copy(
            src_ref=part, dst_ref=got_two.at[o - 1],
            send_sem=ts.at[o - 1], recv_sem=t_r.at[o - 1],
            device_id=tile_peer(o), device_id_type=MESH,
        )

    def three_copy(o):
        return pltpu.make_async_remote_copy(
            src_ref=full.at[lb], dst_ref=full.at[lb],
            send_sem=fs.at[o - 1], recv_sem=f_r.at[o - 1],
            device_id=slab_peer(o), device_id_type=MESH,
        )

    def three_arrival(o):
        other = lax.rem(lb + n_lb - o, n_lb)
        return pltpu.make_async_remote_copy(
            src_ref=full.at[other], dst_ref=full.at[other],
            send_sem=fs.at[o - 1], recv_sem=f_r.at[o - 1],
            device_id=slab_peer(o), device_id_type=MESH,
        )

    for o in range(1, n_lb):
        one_copy(o).start()

    def trailing(i, c):
        scan_steps(i)

        @pl.when(i >= hops)
        def _():
            sweep(i - hops)

        return c

    lax.fori_loop(chunks, chunks + 2, trailing, 0)
    total = slots[lb]
    for o in range(1, n_lb):
        one_copy(o).wait_recv()
        total = total + got_one[o - 1]
    part[...] = total

    def start_two(o, c):
        two_copy(o).start()
        return c

    lax.fori_loop(1, tiles, start_two, 0)
    lax.fori_loop(chunks + 2, chunks + 4, trailing, 0)

    def add_two(o, c):
        two_copy(o).wait_recv()
        return c + got_two[o - 1]

    total = lax.fori_loop(1, tiles, add_two, part[...])
    full[lb] = total * (1.0 / (tiles * slab * n_lb))
    for o in range(1, n_lb):
        three_copy(o).start()

    lax.fori_loop(chunks + 4, chunks + hops, trailing, 0)
    for o in range(1, n_lb):
        three_arrival(o).wait_recv()
    spread_share = jnp.zeros((48, 1024), jnp.float32)
    for g in range(n_lb):
        spread_share = spread_share + lax.dot_general(
            three(full[g]),
            hot[:, g * span_slots : (g + 1) * span_slots],
            (((1,), (1,)), ((), ())),
            preferred_element_type=jnp.float32,
        )
    spread_share = together(spread_share)
    for x in range(8):
        share[pl.ds(x, fields, stride=8), :] = spread_share[:fields, x * 128 : (x + 1) * 128]

    def drain_store(f, c):
        store(f).wait()
        return c

    lax.fori_loop(0, chunks, drain_store, 0)

    def drain(f, c):
        for step in range(STEPS):
            for side in range(sides):
                y_copy(step, f, side).wait_send()
            for side in range(2):
                x_copy(step, f, side).wait_send()

        @pl.when(lb < n_lb - 1)
        def _():
            scan_copy(f, True).wait_send()

        @pl.when(lb > 0)
        def _():
            scan_copy(f, False).wait_send()

        return c

    lax.fori_loop(0, chunks, drain, 0)
    for o in range(1, n_lb):
        one_copy(o).wait_send()
        three_copy(o).wait_send()

    def drain_two(o, c):
        two_copy(o).wait_send()
        return c

    lax.fori_loop(1, tiles, drain_two, 0)


def local(atmosphere_state, diffusivity, mixing, relaxation, forcing, span_map, cost_class):
    fields, slab, width_x, width_y = atmosphere_state.shape
    n_ex, n_ey, n_lb = (lax.axis_size(a) for a in ("ex", "ey", "lb"))
    levels = slab * n_lb
    dims = (n_ex, n_ey, n_lb, fields, slab)
    rows = slab * 8
    tiles = n_ex * n_ey
    sides = 1 if n_ey == 2 else 2
    weight, shifts = operator_tables(width_x, width_y)
    hbm = pl.BlockSpec(memory_space=pltpu.HBM)
    f32 = jnp.float32
    dma = pltpu.SemaphoreType.DMA
    wide = 1024 // n_lb
    volume = (fields, slab, 8, 128)
    physics, share = pl.pallas_call(
        functools.partial(main_kernel, dims),
        out_shape=[
            jax.ShapeDtypeStruct(volume, f32),
            jax.ShapeDtypeStruct((fields * 8, 128), f32),
        ],
        in_specs=[hbm] * 9,
        out_specs=[hbm, pl.BlockSpec(memory_space=pltpu.VMEM)],
        scratch_shapes=[
            pltpu.VMEM(volume, f32),
            pltpu.VMEM((8, 128), jnp.int32),
            pltpu.VMEM((1, 1024), jnp.int32),
            pltpu.VMEM((256, 256), f32),
            pltpu.VMEM((2, 256, 256), jnp.bfloat16),
            pltpu.VMEM((7, 8, 128), f32),
            pltpu.SMEM((fields,), f32),
            pltpu.VMEM((1, levels - 1), f32),
            pltpu.VMEM((1, levels), f32),
            pltpu.VMEM((fields, levels), f32),
            pltpu.VMEM((24, levels), f32),
            pltpu.VMEM((80, levels), f32),
            pltpu.VMEM((16, levels), f32),
            pltpu.VMEM((SUBSTEPS * 8, levels), f32),
            pltpu.VMEM((8, levels), f32),
            pltpu.SMEM((80, levels), f32),
            pltpu.SMEM((16, levels), f32),
            pltpu.SMEM((SUBSTEPS * 8, levels), f32),
            pltpu.SMEM((8, levels), f32),
            pltpu.SMEM((24, levels), f32),
            pltpu.VMEM(volume, f32),
            pltpu.VMEM(volume, f32),
            pltpu.VMEM((slab, 8, 128), f32),
            pltpu.VMEM((slab, 8, 128), f32),
            pltpu.VMEM((slab, 8, 128), f32),
            pltpu.VMEM((8, 128), f32),
            pltpu.VMEM((fields, rows, 128), f32),
            pltpu.VMEM((STEPS, fields, rows, 128), f32),
            pltpu.VMEM((STEPS, sides, fields, rows, 128), f32),
            pltpu.VMEM((STEPS, 2, fields, slab, 128), f32),
            pltpu.VMEM((STEPS, 2, fields, slab, 128), f32),
            pltpu.VMEM((slab, 8, 128), f32),
        ]
        + [pltpu.VMEM((fields, SUBSTEPS, 8, 128), f32)] * 6
        + [
            pltpu.VMEM((128, 128), f32),
            pltpu.VMEM((1024, 1024), jnp.bfloat16),
            pltpu.VMEM((n_lb, 16, wide), f32),
            pltpu.VMEM((n_lb - 1, 16, wide), f32),
            pltpu.VMEM((16, wide), f32),
            pltpu.VMEM((tiles - 1, 16, wide), f32),
            pltpu.VMEM((n_lb, 16, wide), f32),
            dma((fields,)),
            dma((8,)),
            dma((5,)),
            dma((STEPS, sides, fields)),
            dma((STEPS, sides, fields)),
            dma((STEPS, 2, fields)),
            dma((STEPS, 2, fields)),
            dma((fields,)),
            dma((fields,)),
            dma((fields,)),
            dma((fields,)),
            dma((n_lb - 1,)),
            dma((n_lb - 1,)),
            dma((tiles - 1,)),
            dma((tiles - 1,)),
            dma((n_lb - 1,)),
            dma((n_lb - 1,)),
        ],
        compiler_params=pltpu.CompilerParams(
            collective_id=0, has_side_effects=True, vmem_limit_bytes=VMEM_MIB * 1024 * 1024
        ),
    )(
        atmosphere_state, cost_class, span_map.reshape(1, width_x * width_y),
        jnp.asarray(weight), jnp.asarray(shifts), diffusivity,
        mixing.reshape(1, levels - 1), relaxation.reshape(1, levels), forcing,
    )
    return physics - share.reshape(fields, 1, 8, 128)


def solution(mesh):
    return jax.shard_map(
        local,
        mesh=mesh,
        in_specs=(
            P(None, "lb", "ex", "ey"),
            P(),
            P(),
            P(),
            P(),
            P("ex", "ey", None),
            P("ex", "ey"),
        ),
        out_specs=P(None, "lb", "ex", "ey"),
        check_vma=False,
    )
```

```python
import functools
import math

import jax
import jax.numpy as jnp
import numpy as np
from jax import lax
from jax.experimental import pallas as pl
from jax.experimental.pallas import tpu as pltpu
from jax.sharding import PartitionSpec as P

STEPS = 2
SUBSTEPS = 4
MESH = pl.DeviceIdType.MESH
SKEW = 3
VMEM_MIB = 63


def second_table():
    inner_root = 1.0 / math.sqrt(5.0)
    gll_nodes = np.array([-1.0, -inner_root, inner_root, 1.0])
    weights = np.array(
        [
            np.prod(
                [gll_nodes[target] - gll_nodes[source] for source in range(4) if source != target]
            )
            for target in range(4)
        ]
    )
    first_table = np.zeros((4, 4))
    for target in range(4):
        for source in range(4):
            if source != target:
                first_table[target, source] = weights[target] / (
                    weights[source] * (gll_nodes[target] - gll_nodes[source])
                )
    for target in range(4):
        first_table[target, target] = -first_table[target].sum()
    return (first_table @ first_table).astype(np.float32)


def operator_tables(width_x, width_y):
    second = second_table()
    along = np.kron(np.eye(width_y // 4), second.T).astype(np.float64)
    edge = np.zeros((width_y, width_y))
    for y in range(width_y):
        if y % 4 == 3:
            edge[y, y] = 0.5
            if y + 1 < width_y:
                edge[y + 1, y] = 0.5
        elif y % 4 == 0:
            edge[y, y] = 0.5
            if y > 0:
                edge[y - 1, y] = 0.5
        else:
            edge[y, y] = 1.0
    rim = np.zeros((width_y, width_y))
    rim[0, width_y - 1] = 0.5
    rim[width_y - 1, 0] = 0.5
    both = np.concatenate([edge, rim], axis=1)
    weight = np.concatenate([along @ both, both], axis=0).astype(np.float32)
    shifts = np.zeros((7, width_x, width_y), np.float32)
    for x in range(width_x):
        for d in range(-3, 4):
            if 0 <= x % 4 + d < 4:
                shifts[d + 3, x, :] = second[x % 4, x % 4 + d]
    return weight, shifts


def series_mul(u, v):
    return [sum(u[i] * v[k - i] for i in range(k + 1)) for k in range(len(u))]


def series_inverse(u):
    first = 1.0 / u[0]
    out = [first]
    for k in range(1, len(u)):
        out.append(-first * sum(u[i] * out[k - i] for i in range(1, k + 1)))
    return out


def prepare(slab, count, params, mix_in, relax_in, push_in, u_out, sum_out, v_out, coef_out):
    levels = relax_in.shape[1]
    fields = push_in.shape[0]
    shape = (8, levels)
    params[...] = jnp.zeros_like(params)
    params[0:1, 0 : levels - 1] = mix_in[...]
    params[8 : 8 + fields, :] = push_in[...]
    params[23:24, :] = jnp.ones((1, levels), jnp.float32)
    hi = jnp.broadcast_to(params[0:1, :], shape)
    lo = pltpu.roll(hi, 1, 1)
    rel = jnp.broadcast_to(relax_in[...], shape)
    params[1:2, :] = relax_in[...]
    params[2:3, :] = lo[0:1, :]
    lane = lax.broadcasted_iota(jnp.int32, shape, 1)
    row = lax.broadcasted_iota(jnp.int32, shape, 0)
    diag = 1.0 + rel + lo + hi

    def back(x, s):
        return pltpu.roll(x, s, 1)

    def ahead(x, s):
        return pltpu.roll(x, levels - s, 1)

    def reduce_system(a, b, c, extent):
        stages = []
        s = 1
        while s < extent:
            alpha = -a / back(b, s)
            gamma = -c / ahead(b, s)
            b = b + alpha * back(c, s) + gamma * ahead(a, s)
            a = alpha * back(a, s)
            c = gamma * ahead(c, s)
            stages.append((s, alpha, gamma))
            s *= 2
        return stages, 1.0 / b

    def solve(system, d):
        stages, inverse = system
        for s, alpha, gamma in stages:
            d = d + alpha * back(d, s) + gamma * ahead(d, s)
        return d * inverse

    whole = reduce_system(-lo, diag, -hi, levels)
    cut = reduce_system(
        jnp.where(lane % slab == 0, 0.0, -lo),
        diag,
        jnp.where(lane % slab == slab - 1, 0.0, -hi),
        slab,
    )
    push = [params[8:16, :], jnp.where(row == 7, 0.0, params[16:24, :])]
    held = [params[8:16, :], params[16:24, :]]
    sums = [jnp.zeros(shape, jnp.float32)] * 2
    for k in range(SUBSTEPS + 1):
        for h in range(2):
            u_out[k * 16 + h * 8 : k * 16 + h * 8 + 8, :] = held[h]
            sums[h] = jnp.where(lane == k, jnp.sum(held[h], axis=1, keepdims=True), sums[h])
        if k < SUBSTEPS:
            held = [solve(whole, held[h]) + push[h] for h in range(2)]

    sum_out[0:8, :] = sums[0]
    sum_out[8:16, :] = sums[1]
    spot = jnp.where(row < 4, row * slab + slab - 1, (row - 4) * slab)
    tips = jnp.where((lane == spot) & (row % 4 < count), 1.0, 0.0)
    other = pltpu.roll(tips, 4, 0)

    def total(x):
        return jnp.broadcast_to(jnp.sum(x, axis=1, keepdims=True), shape)

    mix = total(jnp.where(row < 4, lo, hi) * other)
    near, far = [], []
    v = tips
    for k in range(SUBSTEPS):
        v = solve(cut, v)
        v_out[k * 8 : k * 8 + 8, :] = v
        near.append(total(v * tips))
        far.append(total(v * other))
    facing = [pltpu.roll(x, 4, 0) for x in near]
    square = mix * mix
    far_far = series_mul(far, far)

    def beside(z):
        return [jnp.where(row < 4, pltpu.roll(x, 1, 0), pltpu.roll(x, 7, 0)) for x in z]

    def gain(u, v):
        product = series_mul(u, v)
        return series_inverse(
            [(1.0 if k == 0 else 0.0) - square * x for k, x in enumerate(product)]
        )

    z = near
    for _ in range(count - 1):
        zn = beside(z)
        change = series_mul(series_mul(far_far, zn), gain(zn, facing))
        z = [x + square * y for x, y in zip(near, change)]
    zn = beside(z)
    first = [mix * x for x in series_mul(far, gain(zn, facing))]
    next_ = [mix * x for x in series_mul(first, zn)]
    edge = gain(zn, [pltpu.roll(x, 4, 0) for x in z])
    edge_one = [mix * x for x in edge]
    edge_two = [mix * x for x in series_mul(edge_one, zn)]
    packed = jnp.zeros(shape, jnp.float32)
    for g, part in enumerate((first, next_, edge_one, edge_two)):
        for k in range(SUBSTEPS):
            packed = jnp.where(lane == g * SUBSTEPS + k, part[k], packed)
    coef_out[...] = packed


def main_kernel(
    dims,
    state_h, classes_h, span_h, w_h, shifts_h, rate_h, mix_h, relax_h, push_h,
    out, share,
    state, classes, span, table, weight, shifts, rate, mix_v, relax_v, push_v,
    params, u_v, sum_v, v_v, coef_v, u_s, sum_s, v_s, coef_s, own_s,
    moved, swept, carry, scale, link, middle_scale,
    lap, hy_out, hy_in, x_out, x_in, weights, p_loc, q_loc, p_out, p_in, q_out, q_in,
    tend, hot, slots, got_one, part, got_two, full,
    state_sem, in_sem, table_sem,
    ys, yr, xs, xr, ps, pr, qs, qr, os, o_r, ts, t_r, fs, f_r,
):
    n_ex, n_ey, n_lb, fields, slab = dims
    rows = slab * 8
    tiles = n_ex * n_ey
    ex, ey, lb = lax.axis_index("ex"), lax.axis_index("ey"), lax.axis_index("lb")
    tile = ex * n_ey + ey
    sides = 1 if n_ey == 2 else 2
    size = 3 if fields % 3 == 0 else 1
    chunks = fields // size

    def tile_peer(o):
        t = lax.rem(tile + o, tiles)
        return (t // n_ey, lax.rem(t, n_ey), lb)

    def slab_peer(o):
        return (ex, ey, lax.rem(lb + o, n_lb))

    barrier = pltpu.get_barrier_semaphore()

    def greet_tiles(o, c):
        pl.semaphore_signal(barrier, inc=1, device_id=tile_peer(o), device_id_type=MESH)
        return c

    def greet_slabs(o, c):
        pl.semaphore_signal(barrier, inc=1, device_id=slab_peer(o), device_id_type=MESH)
        return c

    loads = [
        pltpu.make_async_copy(a, b, in_sem.at[i])
        for i, (a, b) in enumerate(
            (
                (shifts_h, shifts), (w_h, table), (classes_h, classes), (span_h, span),
                (rate_h, rate), (mix_h, mix_v), (relax_h, relax_v), (push_h, push_v),
            )
        )
    ]

    def chunk(f):
        return pl.ds(f * size, size)

    def load_state(f):
        return pltpu.make_async_copy(state_h.at[chunk(f)], state.at[chunk(f)], state_sem.at[f])

    def fetch(f, c):
        load_state(f).start()
        return c

    for copy in loads:
        copy.start()
    lax.fori_loop(0, chunks, fetch, 0)
    lax.fori_loop(1, tiles, greet_tiles, 0)
    lax.fori_loop(1, n_lb, greet_slabs, 0)

    row_x = lax.broadcasted_iota(jnp.int32, (8, 128), 0)
    lane = lax.broadcasted_iota(jnp.int32, (8, 128), 1)
    def derive(f, source, step):
        s = source[chunk(f)].reshape(size * slab, 8, 128)
        along = shifts[3][None] * s
        for d in (-3, -2, -1, 1, 2, 3):
            along = along + shifts[d + 3][None] * pltpu.roll(s, (8 - d) % 8, 1)
        both = jnp.concatenate(
            [s.reshape(size * rows, 128), along.reshape(size * rows, 128)], axis=1
        )
        high = both.astype(jnp.bfloat16)
        low = (both - high.astype(jnp.float32)).astype(jnp.bfloat16)
        result = (
            jnp.dot(high, weight[0], preferred_element_type=jnp.float32)
            + jnp.dot(low, weight[0], preferred_element_type=jnp.float32)
            + jnp.dot(high, weight[1], preferred_element_type=jnp.float32)
        )
        lap[chunk(f)] = result[:, :128].reshape(size, rows, 128)
        hy_out[step, chunk(f)] = result[:, 128:].reshape(size, rows, 128)

    def y_copy(step, f, side):
        peer = lax.rem(ey + (1 if side == 0 else n_ey - 1), n_ey)
        return pltpu.make_async_remote_copy(
            src_ref=hy_out.at[step, chunk(f)],
            dst_ref=hy_in.at[step, side, chunk(f)],
            send_sem=ys.at[step, side, f],
            recv_sem=yr.at[step, side, f],
            device_id=(ex, peer, lb),
            device_id_type=MESH,
        )

    def x_copy(step, f, side):
        peer = lax.rem(ex + (1 if side == 0 else n_ex - 1), n_ex)
        return pltpu.make_async_remote_copy(
            src_ref=x_out.at[step, side, chunk(f)],
            dst_ref=x_in.at[step, side, chunk(f)],
            send_sem=xs.at[step, side, f],
            recv_sem=xr.at[step, side, f],
            device_id=(peer, ey, lb),
            device_id_type=MESH,
        )

    def start_y(f, step):
        for side in range(sides):
            y_copy(step, f, side).start()

    def spread(f, step):
        for side in range(sides):
            y_copy(step, f, side).wait_recv()
        shape = (size * slab, 8, 128)
        value = lap[chunk(f)].reshape(shape)
        if sides == 1:
            value = value + hy_in[step, 0, chunk(f)].reshape(shape)
        else:
            value = value + jnp.where(lane == 0, hy_in[step, 0, chunk(f)].reshape(shape), 0.0)
            value = value + jnp.where(lane == 127, hy_in[step, 1, chunk(f)].reshape(shape), 0.0)
        lap[chunk(f)] = value.reshape(size, rows, 128)
        for i in range(size):
            x_out[step, 0, f * size + i] = lap[f * size + i, pl.ds(7, slab, stride=8), :]
            x_out[step, 1, f * size + i] = lap[f * size + i, pl.ds(0, slab, stride=8), :]
        x_copy(step, f, 0).start()
        x_copy(step, f, 1).start()

    def advance(f, source, step):
        x_copy(step, f, 0).wait_recv()
        x_copy(step, f, 1).wait_recv()
        joins = (row_x == 0) | (row_x == 3) | (row_x == 4) | (row_x == 7)
        for i in range(size):
            g = f * size + i
            value = lap[g].reshape(slab, 8, 128)
            before = pltpu.roll(value, 1, 1)
            after = pltpu.roll(value, 7, 1)
            first = jnp.broadcast_to(x_in[step, 0, g][:, None, :], (slab, 8, 128))
            last = jnp.broadcast_to(x_in[step, 1, g][:, None, :], (slab, 8, 128))
            partner = jnp.where(
                row_x == 0,
                first,
                jnp.where(row_x == 7, last, jnp.where(row_x == 3, after, before)),
            )
            edged = jnp.where(joins, 0.5 * (value + partner), value)
            moved[g] = source[g] + rate[g] * edged

    for copy in loads[:2]:
        copy.wait()
    split = table[...].astype(jnp.bfloat16)
    weight[0] = split
    weight[1] = (table[...] - split.astype(jnp.float32)).astype(jnp.bfloat16)
    load_state(0).wait()
    derive(0, state, 0)
    pl.semaphore_wait(barrier, tiles - 1 + n_lb - 1)
    start_y(0, 0)

    def open_rest(f, c):
        load_state(f).wait()
        derive(f, state, 0)
        start_y(f, 0)
        spread(f - 1, 0)
        return c

    lax.fori_loop(1, chunks, open_rest, 0)
    spread(chunks - 1, 0)
    for copy in loads[2:]:
        copy.wait()
    prepare(slab, n_lb, params, mix_v, relax_v, push_v, u_v, sum_v, v_v, coef_v)
    own_v = ((u_v, u_s), (sum_v, sum_s), (v_v, v_s), (coef_v, coef_s), (params, own_s))
    tables = [pltpu.make_async_copy(a, b, table_sem.at[i]) for i, (a, b) in enumerate(own_v)]
    for copy in tables:
        copy.start()
    cls = classes[...]
    for x in range(8):
        mine = lax.broadcasted_iota(jnp.int32, (128, 1024), 0) + x * 128
        hot[x * 128 : (x + 1) * 128, :] = (
            (mine == span[...]).astype(jnp.float32).astype(jnp.bfloat16)
        )
    for copy in tables:
        copy.wait()

    half = slab // 2

    def factor(i, previous):
        found = []
        for side, before in enumerate(previous):
            l = i if side == 0 else slab - 1 - i
            at = lb * slab + l
            low, high = own_s[2, at], own_s[0, at]
            outer, inner = (low, high) if side == 0 else (high, low)
            ratio = jnp.where(i == 0, 0.0, outer) * before
            inverse = 1.0 / (1.0 + own_s[1, at] + low + high - jnp.where(i == 0, 0.0, outer) * ratio)
            carry[l] = ratio
            scale[l] = inverse
            link[l] = inner * inverse
            found.append(inverse)
        return tuple(found)

    lax.fori_loop(0, half, factor, (jnp.zeros((8, 128), jnp.float32),) * 2)
    middle_scale[...] = 1.0 / (1.0 - link[half - 1] * link[half])

    def set_weight(l, c):
        at = lb * slab + l
        w = [u_s[k * 16 + 15, at] - 1.0 for k in range(1, 5)]
        weights[l] = jnp.where(
            cls == 0, w[0], jnp.where(cls == 1, w[1], jnp.where(cls == 2, w[2], w[3]))
        )
        return c

    lax.fori_loop(0, slab, set_weight, 0)
    def middle(f, c):
        advance(f, state, 0)
        derive(f, moved, 1)
        start_y(f, 1)

        @pl.when(f > 0)
        def _():
            spread(f - 1, 1)

        return c

    lax.fori_loop(0, chunks, middle, 0)
    spread(chunks - 1, 1)

    def pick(group, k, base):
        return coef_s[base + lb, group * SUBSTEPS + k]

    def convolve(group, base, k, value):
        out = pick(group, 0, base) * value[k]
        for i in range(1, k + 1):
            out = out + pick(group, i, base) * value[k - i]
        return out

    def scan_copy(f, down):
        if down:
            return pltpu.make_async_remote_copy(
                src_ref=p_out.at[chunk(f)], dst_ref=p_in.at[chunk(f)],
                send_sem=ps.at[f], recv_sem=pr.at[f],
                device_id=(ex, ey, lax.rem(lb + 1, n_lb)), device_id_type=MESH,
            )
        return pltpu.make_async_remote_copy(
            src_ref=q_out.at[chunk(f)], dst_ref=q_in.at[chunk(f)],
            send_sem=qs.at[f], recv_sem=qr.at[f],
            device_id=(ex, ey, lax.rem(lb + n_lb - 1, n_lb)), device_id_type=MESH,
        )

    def scan_step(f, down):
        arrives = lb > 0 if down else lb < n_lb - 1
        leaves = lb < n_lb - 1 if down else lb > 0
        inward, outward = (p_in, p_out) if down else (q_in, q_out)
        same, opposite = (p_loc, q_loc) if down else (q_loc, p_loc)
        base = 0 if down else 4

        @pl.when((f >= 0) & (f < chunks))
        def _():
            @pl.when(arrives)
            def _():
                scan_copy(f, down).wait_recv()
                own = [same[chunk(f), k] for k in range(SUBSTEPS)]
                facing = [opposite[chunk(f), k] for k in range(SUBSTEPS)]
                coming = [inward[chunk(f), k] for k in range(SUBSTEPS)]
                for k in range(SUBSTEPS):
                    outward[chunk(f), k] = (
                        own[k] + convolve(0, base, k, coming) + convolve(1, base, k, facing)
                    )

            @pl.when(jnp.logical_not(arrives))
            def _():
                for k in range(SUBSTEPS):
                    outward[chunk(f), k] = same[chunk(f), k]

            @pl.when(leaves)
            def _():
                scan_copy(f, down).start()

    def scan_steps(i):
        scan_step(i - lb * SKEW, True)
        scan_step(i - (n_lb - 1 - lb) * SKEW, False)

    def summarise(f):
        zero = jnp.zeros((size, 8, 128), jnp.float32)

        def level(l, c):
            x = moved[chunk(f), l]
            at = lb * slab + l
            out = [c[k] + v_s[k * 8 + lb, at] * x for k in range(4)]
            out += [c[4 + k] + v_s[k * 8 + 4 + lb, at] * x for k in range(4)]
            out.append(c[8] + weights[l][None] * x)
            return tuple(out)

        sums = lax.fori_loop(0, slab, level, (zero,) * 9, unroll=4)
        for k in range(SUBSTEPS):
            p_loc[chunk(f), k] = sums[k]
            q_loc[chunk(f), k] = sums[4 + k]
        for i in range(size):
            g = f * size + i
            h = [sum_s[g, k] * (1.0 / n_lb) for k in range(4)]
            extra = jnp.where(
                cls == 0, h[0], jnp.where(cls == 1, h[1], jnp.where(cls == 2, h[2], h[3]))
            )
            tend[pl.ds(pl.multiple_of(g * 8, 8), 8), :] = sums[8][i] + extra

    tend[fields * 8 : 128, :] = jnp.zeros((128 - fields * 8, 128), jnp.float32)

    @pl.when(lb == 0)
    def _():
        p_in[...] = jnp.zeros_like(p_in)

    @pl.when(lb == n_lb - 1)
    def _():
        q_in[...] = jnp.zeros_like(q_in)

    def store(f):
        return pltpu.make_async_copy(
            moved.at[chunk(f)], out.at[chunk(f)], state_sem.at[f]
        )

    def sweep(g):
        group = size
        start = g * size
        at = chunk(g)
        above = [p_in[at, k] for k in range(SUBSTEPS)]
        below = [q_in[at, k] for k in range(SUBSTEPS)]
        own_p = [p_out[at, k] for k in range(SUBSTEPS)]
        own_q = [q_out[at, k] for k in range(SUBSTEPS)]
        for k in range(SUBSTEPS):
            p_loc[at, k] = convolve(2, 0, k, above) + convolve(3, 0, k, own_q)
            q_loc[at, k] = convolve(2, 4, k, below) + convolve(3, 4, k, own_p)

        def push(f, l):
            h = [u_s[k * 16 + f, lb * slab + l] for k in range(4)]
            return jnp.where(
                cls == 0, h[0], jnp.where(cls == 1, h[1], jnp.where(cls == 2, h[2], h[3]))
            )

        def keep(k, l, y):
            if k > 0:
                y = jnp.where(cls >= k, y, moved[at, l])
            if k < SUBSTEPS - 1:
                moved[at, l] = y
            else:
                for f in range(group):
                    moved[start + f, l] = y[f] + push(start + f, l)

        for k in range(SUBSTEPS):

            def inward(i, z):
                top, low = i, slab - 1 - i
                above = moved[at, top] + carry[top][None] * z[0]
                below = moved[at, low] + carry[low][None] * z[1]
                swept[at, top] = above
                swept[at, low] = below
                return above, below

            first = moved[at, 0] + p_loc[at, k]
            last = moved[at, slab - 1] + q_loc[at, k]
            swept[at, 0] = first
            swept[at, slab - 1] = last
            first, last = lax.fori_loop(1, half, inward, (first, last), unroll=5)
            first = first * scale[half - 1][None]
            last = last * scale[half][None]
            above = (first + link[half - 1][None] * last) * middle_scale[...][None]
            below = last + link[half][None] * above
            keep(k, half - 1, above)
            keep(k, half, below)

            def outward(i, y, k=k):
                top, low = half - 1 - i, half + i
                above = swept[at, top] * scale[top][None] + link[top][None] * y[0]
                below = swept[at, low] * scale[low][None] + link[low][None] * y[1]
                keep(k, top, above)
                keep(k, low, below)
                return above, below

            lax.fori_loop(1, half, outward, (above, below), unroll=5 if k < SUBSTEPS - 1 else 3)
        store(g).start()

    def closing(i, c):
        advance(i, moved, 1)
        summarise(i)
        scan_steps(i)
        return c

    hops = (n_lb - 1) * SKEW

    lax.fori_loop(0, chunks, closing, 0)

    def three(value):
        a = value.astype(jnp.bfloat16)
        rest = value - a.astype(jnp.float32)
        b = rest.astype(jnp.bfloat16)
        last = (rest - b.astype(jnp.float32)).astype(jnp.bfloat16)
        return jnp.concatenate([a, b, last], axis=0)

    def together(value):
        return value[:16] + value[16:32] + value[32:]

    span_slots = 1024 // n_lb
    gathered = jnp.zeros((48, 1024), jnp.float32)
    for x in range(0, 8, 2):
        pair = [three(tend[pl.ds(x + i, 16, stride=8), :]) for i in range(2)]
        gathered = gathered + jnp.dot(
            jnp.concatenate(pair, axis=1),
            hot[x * 128 : (x + 2) * 128, :],
            preferred_element_type=jnp.float32,
        )
    gathered = together(gathered)
    for g in range(n_lb):
        slots[g] = gathered[:, g * span_slots : (g + 1) * span_slots]

    def one_copy(o):
        return pltpu.make_async_remote_copy(
            src_ref=slots.at[lax.rem(lb + o, n_lb)], dst_ref=got_one.at[o - 1],
            send_sem=os.at[o - 1], recv_sem=o_r.at[o - 1],
            device_id=slab_peer(o), device_id_type=MESH,
        )

    def two_copy(o):
        return pltpu.make_async_remote_copy(
            src_ref=part, dst_ref=got_two.at[o - 1],
            send_sem=ts.at[o - 1], recv_sem=t_r.at[o - 1],
            device_id=tile_peer(o), device_id_type=MESH,
        )

    def three_copy(o):
        return pltpu.make_async_remote_copy(
            src_ref=full.at[lb], dst_ref=full.at[lb],
            send_sem=fs.at[o - 1], recv_sem=f_r.at[o - 1],
            device_id=slab_peer(o), device_id_type=MESH,
        )

    def three_arrival(o):
        other = lax.rem(lb + n_lb - o, n_lb)
        return pltpu.make_async_remote_copy(
            src_ref=full.at[other], dst_ref=full.at[other],
            send_sem=fs.at[o - 1], recv_sem=f_r.at[o - 1],
            device_id=slab_peer(o), device_id_type=MESH,
        )

    for o in range(1, n_lb):
        one_copy(o).start()

    def trailing(i, c):
        scan_steps(i)

        @pl.when(i >= hops)
        def _():
            sweep(i - hops)

        return c

    lax.fori_loop(chunks, chunks + 2, trailing, 0)
    total = slots[lb]
    for o in range(1, n_lb):
        one_copy(o).wait_recv()
        total = total + got_one[o - 1]
    part[...] = total

    def start_two(o, c):
        two_copy(o).start()
        return c

    lax.fori_loop(1, tiles, start_two, 0)
    lax.fori_loop(chunks + 2, chunks + 4, trailing, 0)

    def add_two(o, c):
        two_copy(o).wait_recv()
        return c + got_two[o - 1]

    total = lax.fori_loop(1, tiles, add_two, part[...])
    full[lb] = total * (1.0 / (tiles * slab * n_lb))
    for o in range(1, n_lb):
        three_copy(o).start()

    lax.fori_loop(chunks + 4, chunks + hops, trailing, 0)
    for o in range(1, n_lb):
        three_arrival(o).wait_recv()
    spread_share = jnp.zeros((48, 1024), jnp.float32)
    for g in range(n_lb):
        spread_share = spread_share + lax.dot_general(
            three(full[g]),
            hot[:, g * span_slots : (g + 1) * span_slots],
            (((1,), (1,)), ((), ())),
            preferred_element_type=jnp.float32,
        )
    spread_share = together(spread_share)
    for x in range(8):
        share[pl.ds(x, fields, stride=8), :] = spread_share[:fields, x * 128 : (x + 1) * 128]

    def drain_store(f, c):
        store(f).wait()
        return c

    lax.fori_loop(0, chunks, drain_store, 0)

    def drain(f, c):
        for step in range(STEPS):
            for side in range(sides):
                y_copy(step, f, side).wait_send()
            for side in range(2):
                x_copy(step, f, side).wait_send()

        @pl.when(lb < n_lb - 1)
        def _():
            scan_copy(f, True).wait_send()

        @pl.when(lb > 0)
        def _():
            scan_copy(f, False).wait_send()

        return c

    lax.fori_loop(0, chunks, drain, 0)
    for o in range(1, n_lb):
        one_copy(o).wait_send()
        three_copy(o).wait_send()

    def drain_two(o, c):
        two_copy(o).wait_send()
        return c

    lax.fori_loop(1, tiles, drain_two, 0)


def local(atmosphere_state, diffusivity, mixing, relaxation, forcing, span_map, cost_class):
    fields, slab, width_x, width_y = atmosphere_state.shape
    n_ex, n_ey, n_lb = (lax.axis_size(a) for a in ("ex", "ey", "lb"))
    levels = slab * n_lb
    dims = (n_ex, n_ey, n_lb, fields, slab)
    rows = slab * 8
    tiles = n_ex * n_ey
    sides = 1 if n_ey == 2 else 2
    weight, shifts = operator_tables(width_x, width_y)
    hbm = pl.BlockSpec(memory_space=pltpu.HBM)
    f32 = jnp.float32
    dma = pltpu.SemaphoreType.DMA
    wide = 1024 // n_lb
    volume = (fields, slab, 8, 128)
    physics, share = pl.pallas_call(
        functools.partial(main_kernel, dims),
        out_shape=[
            jax.ShapeDtypeStruct(volume, f32),
            jax.ShapeDtypeStruct((fields * 8, 128), f32),
        ],
        in_specs=[hbm] * 9,
        out_specs=[hbm, pl.BlockSpec(memory_space=pltpu.VMEM)],
        scratch_shapes=[
            pltpu.VMEM(volume, f32),
            pltpu.VMEM((8, 128), jnp.int32),
            pltpu.VMEM((1, 1024), jnp.int32),
            pltpu.VMEM((256, 256), f32),
            pltpu.VMEM((2, 256, 256), jnp.bfloat16),
            pltpu.VMEM((7, 8, 128), f32),
            pltpu.SMEM((fields,), f32),
            pltpu.VMEM((1, levels - 1), f32),
            pltpu.VMEM((1, levels), f32),
            pltpu.VMEM((fields, levels), f32),
            pltpu.VMEM((24, levels), f32),
            pltpu.VMEM((80, levels), f32),
            pltpu.VMEM((16, levels), f32),
            pltpu.VMEM((SUBSTEPS * 8, levels), f32),
            pltpu.VMEM((8, levels), f32),
            pltpu.SMEM((80, levels), f32),
            pltpu.SMEM((16, levels), f32),
            pltpu.SMEM((SUBSTEPS * 8, levels), f32),
            pltpu.SMEM((8, levels), f32),
            pltpu.SMEM((24, levels), f32),
            pltpu.VMEM(volume, f32),
            pltpu.VMEM(volume, f32),
            pltpu.VMEM((slab, 8, 128), f32),
            pltpu.VMEM((slab, 8, 128), f32),
            pltpu.VMEM((slab, 8, 128), f32),
            pltpu.VMEM((8, 128), f32),
            pltpu.VMEM((fields, rows, 128), f32),
            pltpu.VMEM((STEPS, fields, rows, 128), f32),
            pltpu.VMEM((STEPS, sides, fields, rows, 128), f32),
            pltpu.VMEM((STEPS, 2, fields, slab, 128), f32),
            pltpu.VMEM((STEPS, 2, fields, slab, 128), f32),
            pltpu.VMEM((slab, 8, 128), f32),
        ]
        + [pltpu.VMEM((fields, SUBSTEPS, 8, 128), f32)] * 6
        + [
            pltpu.VMEM((128, 128), f32),
            pltpu.VMEM((1024, 1024), jnp.bfloat16),
            pltpu.VMEM((n_lb, 16, wide), f32),
            pltpu.VMEM((n_lb - 1, 16, wide), f32),
            pltpu.VMEM((16, wide), f32),
            pltpu.VMEM((tiles - 1, 16, wide), f32),
            pltpu.VMEM((n_lb, 16, wide), f32),
            dma((fields,)),
            dma((8,)),
            dma((5,)),
            dma((STEPS, sides, fields)),
            dma((STEPS, sides, fields)),
            dma((STEPS, 2, fields)),
            dma((STEPS, 2, fields)),
            dma((fields,)),
            dma((fields,)),
            dma((fields,)),
            dma((fields,)),
            dma((n_lb - 1,)),
            dma((n_lb - 1,)),
            dma((tiles - 1,)),
            dma((tiles - 1,)),
            dma((n_lb - 1,)),
            dma((n_lb - 1,)),
        ],
        compiler_params=pltpu.CompilerParams(
            collective_id=0, has_side_effects=True, vmem_limit_bytes=VMEM_MIB * 1024 * 1024
        ),
    )(
        atmosphere_state, cost_class, span_map.reshape(1, width_x * width_y),
        jnp.asarray(weight), jnp.asarray(shifts), diffusivity,
        mixing.reshape(1, levels - 1), relaxation.reshape(1, levels), forcing,
    )
    return subtract(physics, share.reshape(fields, 8, 128))


def subtract_kernel(physics, share, out):
    out[...] = physics[...] - share[...][:, None]


def subtract(physics, share):
    fields, slab = physics.shape[:2]
    size = 3 if fields % 3 == 0 else 1
    block = pl.BlockSpec((size, slab, 8, 128), lambda i: (i, 0, 0, 0))
    return pl.pallas_call(
        subtract_kernel,
        out_shape=jax.ShapeDtypeStruct(physics.shape, physics.dtype),
        grid=(fields // size,),
        in_specs=[block, pl.BlockSpec((size, 8, 128), lambda i: (i, 0, 0))],
        out_specs=block,
        compiler_params=pltpu.CompilerParams(vmem_limit_bytes=VMEM_MIB * 1024 * 1024),
    )(physics, share)


def solution(mesh):
    return jax.shard_map(
        local,
        mesh=mesh,
        in_specs=(
            P(None, "lb", "ex", "ey"),
            P(),
            P(),
            P(),
            P(),
            P("ex", "ey", None),
            P("ex", "ey"),
        ),
        out_specs=P(None, "lb", "ex", "ey"),
        check_vma=False,
    )
```

```python
import functools
import math

import jax
import jax.numpy as jnp
import numpy as np
from jax import lax
from jax.experimental import pallas as pl
from jax.experimental.pallas import tpu as pltpu
from jax.sharding import PartitionSpec as P

STEPS = 2
SUBSTEPS = 4
MESH = pl.DeviceIdType.MESH
SKEW = 1
VMEM_MIB = 63


def second_table():
    inner_root = 1.0 / math.sqrt(5.0)
    gll_nodes = np.array([-1.0, -inner_root, inner_root, 1.0])
    weights = np.array(
        [
            np.prod(
                [gll_nodes[target] - gll_nodes[source] for source in range(4) if source != target]
            )
            for target in range(4)
        ]
    )
    first_table = np.zeros((4, 4))
    for target in range(4):
        for source in range(4):
            if source != target:
                first_table[target, source] = weights[target] / (
                    weights[source] * (gll_nodes[target] - gll_nodes[source])
                )
    for target in range(4):
        first_table[target, target] = -first_table[target].sum()
    return (first_table @ first_table).astype(np.float32)


def operator_tables(width_x, width_y):
    second = second_table()
    along = np.kron(np.eye(width_y // 4), second.T).astype(np.float64)
    edge = np.zeros((width_y, width_y))
    for y in range(width_y):
        if y % 4 == 3:
            edge[y, y] = 0.5
            if y + 1 < width_y:
                edge[y + 1, y] = 0.5
        elif y % 4 == 0:
            edge[y, y] = 0.5
            if y > 0:
                edge[y - 1, y] = 0.5
        else:
            edge[y, y] = 1.0
    rim = np.zeros((width_y, width_y))
    rim[0, width_y - 1] = 0.5
    rim[width_y - 1, 0] = 0.5
    both = np.concatenate([edge, rim], axis=1)
    weight = np.concatenate([along @ both, both], axis=0).astype(np.float32)
    shifts = np.zeros((7, width_x, width_y), np.float32)
    for x in range(width_x):
        for d in range(-3, 4):
            if 0 <= x % 4 + d < 4:
                shifts[d + 3, x, :] = second[x % 4, x % 4 + d]
    return weight, shifts


def series_mul(u, v):
    return [sum(u[i] * v[k - i] for i in range(k + 1)) for k in range(len(u))]


def series_inverse(u):
    first = 1.0 / u[0]
    out = [first]
    for k in range(1, len(u)):
        out.append(-first * sum(u[i] * out[k - i] for i in range(1, k + 1)))
    return out


def prepare(slab, count, params, mix_in, relax_in, push_in, u_out, sum_out, v_out, coef_out):
    levels = relax_in.shape[1]
    fields = push_in.shape[0]
    shape = (8, levels)
    params[...] = jnp.zeros_like(params)
    params[0:1, 0 : levels - 1] = mix_in[...]
    params[8 : 8 + fields, :] = push_in[...]
    params[23:24, :] = jnp.ones((1, levels), jnp.float32)
    hi = jnp.broadcast_to(params[0:1, :], shape)
    lo = pltpu.roll(hi, 1, 1)
    rel = jnp.broadcast_to(relax_in[...], shape)
    params[1:2, :] = relax_in[...]
    params[2:3, :] = lo[0:1, :]
    lane = lax.broadcasted_iota(jnp.int32, shape, 1)
    row = lax.broadcasted_iota(jnp.int32, shape, 0)
    diag = 1.0 + rel + lo + hi

    def back(x, s):
        return pltpu.roll(x, s, 1)

    def ahead(x, s):
        return pltpu.roll(x, levels - s, 1)

    def reduce_system(a, b, c, extent):
        stages = []
        s = 1
        while s < extent:
            alpha = -a / back(b, s)
            gamma = -c / ahead(b, s)
            b = b + alpha * back(c, s) + gamma * ahead(a, s)
            a = alpha * back(a, s)
            c = gamma * ahead(c, s)
            stages.append((s, alpha, gamma))
            s *= 2
        return stages, 1.0 / b

    def solve(system, d):
        stages, inverse = system
        for s, alpha, gamma in stages:
            d = d + alpha * back(d, s) + gamma * ahead(d, s)
        return d * inverse

    whole = reduce_system(-lo, diag, -hi, levels)
    cut = reduce_system(
        jnp.where(lane % slab == 0, 0.0, -lo),
        diag,
        jnp.where(lane % slab == slab - 1, 0.0, -hi),
        slab,
    )
    push = [params[8:16, :], jnp.where(row == 7, 0.0, params[16:24, :])]
    held = [params[8:16, :], params[16:24, :]]
    sums = [jnp.zeros(shape, jnp.float32)] * 2
    for k in range(SUBSTEPS + 1):
        for h in range(2):
            u_out[k * 16 + h * 8 : k * 16 + h * 8 + 8, :] = held[h]
            sums[h] = jnp.where(lane == k, jnp.sum(held[h], axis=1, keepdims=True), sums[h])
        if k < SUBSTEPS:
            held = [solve(whole, held[h]) + push[h] for h in range(2)]

    sum_out[0:8, :] = sums[0]
    sum_out[8:16, :] = sums[1]
    spot = jnp.where(row < 4, row * slab + slab - 1, (row - 4) * slab)
    tips = jnp.where((lane == spot) & (row % 4 < count), 1.0, 0.0)
    other = pltpu.roll(tips, 4, 0)

    def total(x):
        return jnp.broadcast_to(jnp.sum(x, axis=1, keepdims=True), shape)

    mix = total(jnp.where(row < 4, lo, hi) * other)
    near, far = [], []
    v = tips
    for k in range(SUBSTEPS):
        v = solve(cut, v)
        v_out[k * 8 : k * 8 + 8, :] = v
        near.append(total(v * tips))
        far.append(total(v * other))
    facing = [pltpu.roll(x, 4, 0) for x in near]
    square = mix * mix
    far_far = series_mul(far, far)

    def beside(z):
        return [jnp.where(row < 4, pltpu.roll(x, 1, 0), pltpu.roll(x, 7, 0)) for x in z]

    def gain(u, v):
        product = series_mul(u, v)
        return series_inverse(
            [(1.0 if k == 0 else 0.0) - square * x for k, x in enumerate(product)]
        )

    z = near
    for _ in range(count - 1):
        zn = beside(z)
        change = series_mul(series_mul(far_far, zn), gain(zn, facing))
        z = [x + square * y for x, y in zip(near, change)]
    zn = beside(z)
    first = [mix * x for x in series_mul(far, gain(zn, facing))]
    next_ = [mix * x for x in series_mul(first, zn)]
    edge = gain(zn, [pltpu.roll(x, 4, 0) for x in z])
    edge_one = [mix * x for x in edge]
    edge_two = [mix * x for x in series_mul(edge_one, zn)]
    packed = jnp.zeros(shape, jnp.float32)
    for g, part in enumerate((first, next_, edge_one, edge_two)):
        for k in range(SUBSTEPS):
            packed = jnp.where(lane == g * SUBSTEPS + k, part[k], packed)
    coef_out[...] = packed


def main_kernel(
    dims,
    state_h, classes_h, span_h, w_h, shifts_h, rate_h, mix_h, relax_h, push_h,
    out, share,
    state, classes, span, table, weight, shifts, rate, mix_v, relax_v, push_v,
    params, u_v, sum_v, v_v, coef_v, u_s, sum_s, v_s, coef_s, own_s,
    moved, swept, carry, scale, link, middle_scale,
    lap, hy_out, hy_in, x_out, x_in, weights, p_loc, q_loc, p_out, p_in, q_out, q_in,
    tend, hot, slots, got_one, part, got_two, full,
    state_sem, in_sem, table_sem,
    ys, yr, xs, xr, ps, pr, qs, qr, os, o_r, ts, t_r, fs, f_r,
):
    n_ex, n_ey, n_lb, fields, slab = dims
    rows = slab * 8
    tiles = n_ex * n_ey
    ex, ey, lb = lax.axis_index("ex"), lax.axis_index("ey"), lax.axis_index("lb")
    tile = ex * n_ey + ey
    sides = 1 if n_ey == 2 else 2
    size = 5 if fields % 5 == 0 else 1
    chunks = fields // size

    def tile_peer(o):
        t = lax.rem(tile + o, tiles)
        return (t // n_ey, lax.rem(t, n_ey), lb)

    def slab_peer(o):
        return (ex, ey, lax.rem(lb + o, n_lb))

    barrier = pltpu.get_barrier_semaphore()

    def greet_tiles(o, c):
        pl.semaphore_signal(barrier, inc=1, device_id=tile_peer(o), device_id_type=MESH)
        return c

    def greet_slabs(o, c):
        pl.semaphore_signal(barrier, inc=1, device_id=slab_peer(o), device_id_type=MESH)
        return c

    loads = [
        pltpu.make_async_copy(a, b, in_sem.at[i])
        for i, (a, b) in enumerate(
            (
                (shifts_h, shifts), (w_h, table), (classes_h, classes), (span_h, span),
                (rate_h, rate), (mix_h, mix_v), (relax_h, relax_v), (push_h, push_v),
            )
        )
    ]

    def chunk(f):
        return pl.ds(f * size, size)

    def load_state(f):
        return pltpu.make_async_copy(state_h.at[chunk(f)], state.at[chunk(f)], state_sem.at[f])

    def fetch(f, c):
        load_state(f).start()
        return c

    for copy in loads:
        copy.start()
    lax.fori_loop(0, chunks, fetch, 0)
    lax.fori_loop(1, tiles, greet_tiles, 0)
    lax.fori_loop(1, n_lb, greet_slabs, 0)

    row_x = lax.broadcasted_iota(jnp.int32, (8, 128), 0)
    lane = lax.broadcasted_iota(jnp.int32, (8, 128), 1)
    def derive(f, source, step):
        s = source[chunk(f)].reshape(size * slab, 8, 128)
        along = shifts[3][None] * s
        for d in (-3, -2, -1, 1, 2, 3):
            along = along + shifts[d + 3][None] * pltpu.roll(s, (8 - d) % 8, 1)
        both = jnp.concatenate(
            [s.reshape(size * rows, 128), along.reshape(size * rows, 128)], axis=1
        )
        high = both.astype(jnp.bfloat16)
        low = (both - high.astype(jnp.float32)).astype(jnp.bfloat16)
        result = (
            jnp.dot(high, weight[0], preferred_element_type=jnp.float32)
            + jnp.dot(low, weight[0], preferred_element_type=jnp.float32)
            + jnp.dot(high, weight[1], preferred_element_type=jnp.float32)
        )
        lap[chunk(f)] = result[:, :128].reshape(size, rows, 128)
        hy_out[step, chunk(f)] = result[:, 128:].reshape(size, rows, 128)

    def y_copy(step, f, side):
        peer = lax.rem(ey + (1 if side == 0 else n_ey - 1), n_ey)
        return pltpu.make_async_remote_copy(
            src_ref=hy_out.at[step, chunk(f)],
            dst_ref=hy_in.at[step, side, chunk(f)],
            send_sem=ys.at[step, side, f],
            recv_sem=yr.at[step, side, f],
            device_id=(ex, peer, lb),
            device_id_type=MESH,
        )

    def x_copy(step, f, side):
        peer = lax.rem(ex + (1 if side == 0 else n_ex - 1), n_ex)
        return pltpu.make_async_remote_copy(
            src_ref=x_out.at[step, side, chunk(f)],
            dst_ref=x_in.at[step, side, chunk(f)],
            send_sem=xs.at[step, side, f],
            recv_sem=xr.at[step, side, f],
            device_id=(peer, ey, lb),
            device_id_type=MESH,
        )

    def start_y(f, step):
        for side in range(sides):
            y_copy(step, f, side).start()

    def spread(f, step):
        for side in range(sides):
            y_copy(step, f, side).wait_recv()
        shape = (size * slab, 8, 128)
        value = lap[chunk(f)].reshape(shape)
        if sides == 1:
            value = value + hy_in[step, 0, chunk(f)].reshape(shape)
        else:
            value = value + jnp.where(lane == 0, hy_in[step, 0, chunk(f)].reshape(shape), 0.0)
            value = value + jnp.where(lane == 127, hy_in[step, 1, chunk(f)].reshape(shape), 0.0)
        lap[chunk(f)] = value.reshape(size, rows, 128)
        for i in range(size):
            x_out[step, 0, f * size + i] = lap[f * size + i, pl.ds(7, slab, stride=8), :]
            x_out[step, 1, f * size + i] = lap[f * size + i, pl.ds(0, slab, stride=8), :]
        x_copy(step, f, 0).start()
        x_copy(step, f, 1).start()

    def advance(f, source, step):
        x_copy(step, f, 0).wait_recv()
        x_copy(step, f, 1).wait_recv()
        joins = (row_x == 0) | (row_x == 3) | (row_x == 4) | (row_x == 7)
        for i in range(size):
            g = f * size + i
            value = lap[g].reshape(slab, 8, 128)
            before = pltpu.roll(value, 1, 1)
            after = pltpu.roll(value, 7, 1)
            first = jnp.broadcast_to(x_in[step, 0, g][:, None, :], (slab, 8, 128))
            last = jnp.broadcast_to(x_in[step, 1, g][:, None, :], (slab, 8, 128))
            partner = jnp.where(
                row_x == 0,
                first,
                jnp.where(row_x == 7, last, jnp.where(row_x == 3, after, before)),
            )
            edged = jnp.where(joins, 0.5 * (value + partner), value)
            moved[g] = source[g] + rate[g] * edged

    for copy in loads[:2]:
        copy.wait()
    split = table[...].astype(jnp.bfloat16)
    weight[0] = split
    weight[1] = (table[...] - split.astype(jnp.float32)).astype(jnp.bfloat16)
    load_state(0).wait()
    derive(0, state, 0)
    pl.semaphore_wait(barrier, tiles - 1 + n_lb - 1)
    start_y(0, 0)

    def open_rest(f, c):
        load_state(f).wait()
        derive(f, state, 0)
        start_y(f, 0)
        spread(f - 1, 0)
        return c

    lax.fori_loop(1, chunks, open_rest, 0)
    spread(chunks - 1, 0)
    for copy in loads[2:]:
        copy.wait()
    prepare(slab, n_lb, params, mix_v, relax_v, push_v, u_v, sum_v, v_v, coef_v)
    own_v = ((u_v, u_s), (sum_v, sum_s), (v_v, v_s), (coef_v, coef_s), (params, own_s))
    tables = [pltpu.make_async_copy(a, b, table_sem.at[i]) for i, (a, b) in enumerate(own_v)]
    for copy in tables:
        copy.start()
    cls = classes[...]
    for x in range(8):
        mine = lax.broadcasted_iota(jnp.int32, (128, 1024), 0) + x * 128
        hot[x * 128 : (x + 1) * 128, :] = (
            (mine == span[...]).astype(jnp.float32).astype(jnp.bfloat16)
        )
    for copy in tables:
        copy.wait()

    half = slab // 2

    def factor(i, previous):
        found = []
        for side, before in enumerate(previous):
            l = i if side == 0 else slab - 1 - i
            at = lb * slab + l
            low, high = own_s[2, at], own_s[0, at]
            outer, inner = (low, high) if side == 0 else (high, low)
            ratio = jnp.where(i == 0, 0.0, outer) * before
            inverse = 1.0 / (1.0 + own_s[1, at] + low + high - jnp.where(i == 0, 0.0, outer) * ratio)
            carry[l] = ratio
            scale[l] = inverse
            link[l] = inner * inverse
            found.append(inverse)
        return tuple(found)

    lax.fori_loop(0, half, factor, (jnp.zeros((8, 128), jnp.float32),) * 2)
    middle_scale[...] = 1.0 / (1.0 - link[half - 1] * link[half])

    def set_weight(l, c):
        at = lb * slab + l
        w = [u_s[k * 16 + 15, at] - 1.0 for k in range(1, 5)]
        weights[l] = jnp.where(
            cls == 0, w[0], jnp.where(cls == 1, w[1], jnp.where(cls == 2, w[2], w[3]))
        )
        return c

    lax.fori_loop(0, slab, set_weight, 0)
    def middle(f, c):
        advance(f, state, 0)
        derive(f, moved, 1)
        start_y(f, 1)

        @pl.when(f > 0)
        def _():
            spread(f - 1, 1)

        return c

    lax.fori_loop(0, chunks, middle, 0)
    spread(chunks - 1, 1)

    def pick(group, k, base):
        return coef_s[base + lb, group * SUBSTEPS + k]

    def convolve(group, base, k, value):
        out = pick(group, 0, base) * value[k]
        for i in range(1, k + 1):
            out = out + pick(group, i, base) * value[k - i]
        return out

    def scan_copy(f, down):
        if down:
            return pltpu.make_async_remote_copy(
                src_ref=p_out.at[chunk(f)], dst_ref=p_in.at[chunk(f)],
                send_sem=ps.at[f], recv_sem=pr.at[f],
                device_id=(ex, ey, lax.rem(lb + 1, n_lb)), device_id_type=MESH,
            )
        return pltpu.make_async_remote_copy(
            src_ref=q_out.at[chunk(f)], dst_ref=q_in.at[chunk(f)],
            send_sem=qs.at[f], recv_sem=qr.at[f],
            device_id=(ex, ey, lax.rem(lb + n_lb - 1, n_lb)), device_id_type=MESH,
        )

    def scan_step(f, down):
        arrives = lb > 0 if down else lb < n_lb - 1
        leaves = lb < n_lb - 1 if down else lb > 0
        inward, outward = (p_in, p_out) if down else (q_in, q_out)
        same, opposite = (p_loc, q_loc) if down else (q_loc, p_loc)
        base = 0 if down else 4

        @pl.when((f >= 0) & (f < chunks))
        def _():
            @pl.when(arrives)
            def _():
                scan_copy(f, down).wait_recv()
                own = [same[chunk(f), k] for k in range(SUBSTEPS)]
                facing = [opposite[chunk(f), k] for k in range(SUBSTEPS)]
                coming = [inward[chunk(f), k] for k in range(SUBSTEPS)]
                for k in range(SUBSTEPS):
                    outward[chunk(f), k] = (
                        own[k] + convolve(0, base, k, coming) + convolve(1, base, k, facing)
                    )

            @pl.when(jnp.logical_not(arrives))
            def _():
                for k in range(SUBSTEPS):
                    outward[chunk(f), k] = same[chunk(f), k]

            @pl.when(leaves)
            def _():
                scan_copy(f, down).start()

    def scan_steps(i):
        scan_step(i - lb * SKEW, True)
        scan_step(i - (n_lb - 1 - lb) * SKEW, False)

    def summarise(f):
        zero = jnp.zeros((size, 8, 128), jnp.float32)

        def level(l, c):
            x = moved[chunk(f), l]
            at = lb * slab + l
            out = [c[k] + v_s[k * 8 + lb, at] * x for k in range(4)]
            out += [c[4 + k] + v_s[k * 8 + 4 + lb, at] * x for k in range(4)]
            out.append(c[8] + weights[l][None] * x)
            return tuple(out)

        sums = lax.fori_loop(0, slab, level, (zero,) * 9, unroll=4)
        for k in range(SUBSTEPS):
            p_loc[chunk(f), k] = sums[k]
            q_loc[chunk(f), k] = sums[4 + k]
        for i in range(size):
            g = f * size + i
            h = [sum_s[g, k] * (1.0 / n_lb) for k in range(4)]
            extra = jnp.where(
                cls == 0, h[0], jnp.where(cls == 1, h[1], jnp.where(cls == 2, h[2], h[3]))
            )
            tend[pl.ds(pl.multiple_of(g * 8, 8), 8), :] = sums[8][i] + extra

    tend[fields * 8 : 128, :] = jnp.zeros((128 - fields * 8, 128), jnp.float32)

    @pl.when(lb == 0)
    def _():
        p_in[...] = jnp.zeros_like(p_in)

    @pl.when(lb == n_lb - 1)
    def _():
        q_in[...] = jnp.zeros_like(q_in)

    def store(f):
        return pltpu.make_async_copy(
            moved.at[chunk(f)], out.at[chunk(f)], state_sem.at[f]
        )

    def sweep(g):
        group = size
        start = g * size
        at = chunk(g)
        above = [p_in[at, k] for k in range(SUBSTEPS)]
        below = [q_in[at, k] for k in range(SUBSTEPS)]
        own_p = [p_out[at, k] for k in range(SUBSTEPS)]
        own_q = [q_out[at, k] for k in range(SUBSTEPS)]
        for k in range(SUBSTEPS):
            p_loc[at, k] = convolve(2, 0, k, above) + convolve(3, 0, k, own_q)
            q_loc[at, k] = convolve(2, 4, k, below) + convolve(3, 4, k, own_p)

        def push(f, l):
            h = [u_s[k * 16 + f, lb * slab + l] for k in range(4)]
            return jnp.where(
                cls == 0, h[0], jnp.where(cls == 1, h[1], jnp.where(cls == 2, h[2], h[3]))
            )

        def keep(k, l, y):
            if k > 0:
                y = jnp.where(cls >= k, y, moved[at, l])
            if k < SUBSTEPS - 1:
                moved[at, l] = y
            else:
                for f in range(group):
                    moved[start + f, l] = y[f] + push(start + f, l)

        for k in range(SUBSTEPS):

            def inward(i, z):
                top, low = i, slab - 1 - i
                above = moved[at, top] + carry[top][None] * z[0]
                below = moved[at, low] + carry[low][None] * z[1]
                swept[at, top] = above
                swept[at, low] = below
                return above, below

            first = moved[at, 0] + p_loc[at, k]
            last = moved[at, slab - 1] + q_loc[at, k]
            swept[at, 0] = first
            swept[at, slab - 1] = last
            first, last = lax.fori_loop(1, half, inward, (first, last), unroll=5)
            first = first * scale[half - 1][None]
            last = last * scale[half][None]
            above = (first + link[half - 1][None] * last) * middle_scale[...][None]
            below = last + link[half][None] * above
            keep(k, half - 1, above)
            keep(k, half, below)

            def outward(i, y, k=k):
                top, low = half - 1 - i, half + i
                above = swept[at, top] * scale[top][None] + link[top][None] * y[0]
                below = swept[at, low] * scale[low][None] + link[low][None] * y[1]
                keep(k, top, above)
                keep(k, low, below)
                return above, below

            lax.fori_loop(1, half, outward, (above, below), unroll=5 if k < SUBSTEPS - 1 else 3)
        store(g).start()

    def closing(i, c):
        advance(i, moved, 1)
        summarise(i)
        scan_steps(i)
        return c

    hops = (n_lb - 1) * SKEW

    lax.fori_loop(0, chunks, closing, 0)

    def three(value):
        a = value.astype(jnp.bfloat16)
        rest = value - a.astype(jnp.float32)
        b = rest.astype(jnp.bfloat16)
        last = (rest - b.astype(jnp.float32)).astype(jnp.bfloat16)
        return jnp.concatenate([a, b, last], axis=0)

    def together(value):
        return value[:16] + value[16:32] + value[32:]

    span_slots = 1024 // n_lb
    gathered = jnp.zeros((48, 1024), jnp.float32)
    for x in range(0, 8, 2):
        pair = [three(tend[pl.ds(x + i, 16, stride=8), :]) for i in range(2)]
        gathered = gathered + jnp.dot(
            jnp.concatenate(pair, axis=1),
            hot[x * 128 : (x + 2) * 128, :],
            preferred_element_type=jnp.float32,
        )
    gathered = together(gathered)
    for g in range(n_lb):
        slots[g] = gathered[:, g * span_slots : (g + 1) * span_slots]

    def one_copy(o):
        return pltpu.make_async_remote_copy(
            src_ref=slots.at[lax.rem(lb + o, n_lb)], dst_ref=got_one.at[o - 1],
            send_sem=os.at[o - 1], recv_sem=o_r.at[o - 1],
            device_id=slab_peer(o), device_id_type=MESH,
        )

    def two_copy(o):
        return pltpu.make_async_remote_copy(
            src_ref=part, dst_ref=got_two.at[o - 1],
            send_sem=ts.at[o - 1], recv_sem=t_r.at[o - 1],
            device_id=tile_peer(o), device_id_type=MESH,
        )

    def three_copy(o):
        return pltpu.make_async_remote_copy(
            src_ref=full.at[lb], dst_ref=full.at[lb],
            send_sem=fs.at[o - 1], recv_sem=f_r.at[o - 1],
            device_id=slab_peer(o), device_id_type=MESH,
        )

    def three_arrival(o):
        other = lax.rem(lb + n_lb - o, n_lb)
        return pltpu.make_async_remote_copy(
            src_ref=full.at[other], dst_ref=full.at[other],
            send_sem=fs.at[o - 1], recv_sem=f_r.at[o - 1],
            device_id=slab_peer(o), device_id_type=MESH,
        )

    for o in range(1, n_lb):
        one_copy(o).start()

    def trailing(i, c):
        scan_steps(i)

        @pl.when(i >= hops)
        def _():
            sweep(i - hops)

        return c

    lax.fori_loop(chunks, chunks + 1, trailing, 0)
    total = slots[lb]
    for o in range(1, n_lb):
        one_copy(o).wait_recv()
        total = total + got_one[o - 1]
    part[...] = total

    def start_two(o, c):
        two_copy(o).start()
        return c

    lax.fori_loop(1, tiles, start_two, 0)
    lax.fori_loop(chunks + 1, chunks + 2, trailing, 0)

    def add_two(o, c):
        two_copy(o).wait_recv()
        return c + got_two[o - 1]

    total = lax.fori_loop(1, tiles, add_two, part[...])
    full[lb] = total * (1.0 / (tiles * slab * n_lb))
    for o in range(1, n_lb):
        three_copy(o).start()

    lax.fori_loop(chunks + 2, chunks + hops, trailing, 0)
    for o in range(1, n_lb):
        three_arrival(o).wait_recv()
    spread_share = jnp.zeros((48, 1024), jnp.float32)
    for g in range(n_lb):
        spread_share = spread_share + lax.dot_general(
            three(full[g]),
            hot[:, g * span_slots : (g + 1) * span_slots],
            (((1,), (1,)), ((), ())),
            preferred_element_type=jnp.float32,
        )
    spread_share = together(spread_share)
    for x in range(8):
        share[pl.ds(x, fields, stride=8), :] = spread_share[:fields, x * 128 : (x + 1) * 128]

    def drain_store(f, c):
        store(f).wait()
        return c

    lax.fori_loop(0, chunks, drain_store, 0)

    def drain(f, c):
        for step in range(STEPS):
            for side in range(sides):
                y_copy(step, f, side).wait_send()
            for side in range(2):
                x_copy(step, f, side).wait_send()

        @pl.when(lb < n_lb - 1)
        def _():
            scan_copy(f, True).wait_send()

        @pl.when(lb > 0)
        def _():
            scan_copy(f, False).wait_send()

        return c

    lax.fori_loop(0, chunks, drain, 0)
    for o in range(1, n_lb):
        one_copy(o).wait_send()
        three_copy(o).wait_send()

    def drain_two(o, c):
        two_copy(o).wait_send()
        return c

    lax.fori_loop(1, tiles, drain_two, 0)


def local(atmosphere_state, diffusivity, mixing, relaxation, forcing, span_map, cost_class):
    fields, slab, width_x, width_y = atmosphere_state.shape
    n_ex, n_ey, n_lb = (lax.axis_size(a) for a in ("ex", "ey", "lb"))
    levels = slab * n_lb
    dims = (n_ex, n_ey, n_lb, fields, slab)
    rows = slab * 8
    tiles = n_ex * n_ey
    sides = 1 if n_ey == 2 else 2
    weight, shifts = operator_tables(width_x, width_y)
    hbm = pl.BlockSpec(memory_space=pltpu.HBM)
    f32 = jnp.float32
    dma = pltpu.SemaphoreType.DMA
    wide = 1024 // n_lb
    volume = (fields, slab, 8, 128)
    physics, share = pl.pallas_call(
        functools.partial(main_kernel, dims),
        out_shape=[
            jax.ShapeDtypeStruct(volume, f32),
            jax.ShapeDtypeStruct((fields * 8, 128), f32),
        ],
        in_specs=[hbm] * 9,
        out_specs=[hbm, pl.BlockSpec(memory_space=pltpu.VMEM)],
        scratch_shapes=[
            pltpu.VMEM(volume, f32),
            pltpu.VMEM((8, 128), jnp.int32),
            pltpu.VMEM((1, 1024), jnp.int32),
            pltpu.VMEM((256, 256), f32),
            pltpu.VMEM((2, 256, 256), jnp.bfloat16),
            pltpu.VMEM((7, 8, 128), f32),
            pltpu.SMEM((fields,), f32),
            pltpu.VMEM((1, levels - 1), f32),
            pltpu.VMEM((1, levels), f32),
            pltpu.VMEM((fields, levels), f32),
            pltpu.VMEM((24, levels), f32),
            pltpu.VMEM((80, levels), f32),
            pltpu.VMEM((16, levels), f32),
            pltpu.VMEM((SUBSTEPS * 8, levels), f32),
            pltpu.VMEM((8, levels), f32),
            pltpu.SMEM((80, levels), f32),
            pltpu.SMEM((16, levels), f32),
            pltpu.SMEM((SUBSTEPS * 8, levels), f32),
            pltpu.SMEM((8, levels), f32),
            pltpu.SMEM((24, levels), f32),
            pltpu.VMEM(volume, f32),
            pltpu.VMEM(volume, f32),
            pltpu.VMEM((slab, 8, 128), f32),
            pltpu.VMEM((slab, 8, 128), f32),
            pltpu.VMEM((slab, 8, 128), f32),
            pltpu.VMEM((8, 128), f32),
            pltpu.VMEM((fields, rows, 128), f32),
            pltpu.VMEM((STEPS, fields, rows, 128), f32),
            pltpu.VMEM((STEPS, sides, fields, rows, 128), f32),
            pltpu.VMEM((STEPS, 2, fields, slab, 128), f32),
            pltpu.VMEM((STEPS, 2, fields, slab, 128), f32),
            pltpu.VMEM((slab, 8, 128), f32),
        ]
        + [pltpu.VMEM((fields, SUBSTEPS, 8, 128), f32)] * 6
        + [
            pltpu.VMEM((128, 128), f32),
            pltpu.VMEM((1024, 1024), jnp.bfloat16),
            pltpu.VMEM((n_lb, 16, wide), f32),
            pltpu.VMEM((n_lb - 1, 16, wide), f32),
            pltpu.VMEM((16, wide), f32),
            pltpu.VMEM((tiles - 1, 16, wide), f32),
            pltpu.VMEM((n_lb, 16, wide), f32),
            dma((fields,)),
            dma((8,)),
            dma((5,)),
            dma((STEPS, sides, fields)),
            dma((STEPS, sides, fields)),
            dma((STEPS, 2, fields)),
            dma((STEPS, 2, fields)),
            dma((fields,)),
            dma((fields,)),
            dma((fields,)),
            dma((fields,)),
            dma((n_lb - 1,)),
            dma((n_lb - 1,)),
            dma((tiles - 1,)),
            dma((tiles - 1,)),
            dma((n_lb - 1,)),
            dma((n_lb - 1,)),
        ],
        compiler_params=pltpu.CompilerParams(
            collective_id=0, has_side_effects=True, vmem_limit_bytes=VMEM_MIB * 1024 * 1024
        ),
    )(
        atmosphere_state, cost_class, span_map.reshape(1, width_x * width_y),
        jnp.asarray(weight), jnp.asarray(shifts), diffusivity,
        mixing.reshape(1, levels - 1), relaxation.reshape(1, levels), forcing,
    )
    return physics - share.reshape(fields, 1, 8, 128)


def solution(mesh):
    return jax.shard_map(
        local,
        mesh=mesh,
        in_specs=(
            P(None, "lb", "ex", "ey"),
            P(),
            P(),
            P(),
            P(),
            P("ex", "ey", None),
            P("ex", "ey"),
        ),
        out_specs=P(None, "lb", "ex", "ey"),
        check_vma=False,
    )
```
